128 devices in a mesh: grp: 8 (over y, core), seq: 16 (over z, x).
Axes of the slice: x: 4, y: 4, z: 4, core: 2. Of those that a mesh axis runs over, the one named last changes fastest.
Arguments:
- queries: bfloat16 [32, 2, 8192], P('grp', None, 'seq'), may hold values from -12 to 12
- new_kv: bfloat16 [32, 2, 2, 1024], P('grp'), may hold values from -64 to 64
- prefix_keys: bfloat16 [131072, 1024], P(('grp', 'seq')), may hold values from -64 to 64
- prefix_values: bfloat16 [131072, 1024], P(('grp', 'seq')), may hold values from -6 to 6
- suffix_keys: bfloat16 [32, 4096, 1024], P('grp', 'seq'), may hold values from -64 to 64
- suffix_values: bfloat16 [32, 4096, 1024], P('grp', 'seq'), may hold values from -6 to 6
- suffix_lengths: int32 [32], P('grp'), may hold values from 16 to 4096, as said below
- row_slot: int32 [32], replicated, may hold values from 0 to 31, as said below
Outputs:
- attended: bfloat16 [32, 2, 8192], P('grp', None, 'seq')
The draws below stay inside these ranges and needn't reach their ends.
Inputs may be any that keep to these rules, and one draw needn't show every extreme that they name: Row r's continuation is held in cache slot row_slot[r]; every slot belongs to exactly one row. Slot s holds its first suffix_lengths[s] positions live; at least one slot holds exactly 4096.
All inputs are finite; a program needn't handle non-finite values.
Results may differ from the reference program's by a relative error of at most 0.0095.
Values may be sent and summed in bfloat16 or wider, within the bound.
No kernel may reach another device: no remote copies, remote signals or barrier semaphores. Data moves between devices by JAX's collectives and lax.ppermute only.
A program may use at most 512 MiB of HBM per device.

```python
import jax
import jax.numpy as jnp
from jax import lax

H = 64
KVH = 8
HEAD = 128
STEPS = 2
S_CAP = 4096
ROWS = 32
PREFIX = 131072


query_scale = 3.0


own_gain = 12.0


suffix_scale = 1.3


shortest = 16


key_bound = 64.0


def slot_order(key):
    return jax.random.permutation(jax.random.fold_in(key, 103), ROWS).astype(jnp.int32)


def shared_queries(key):
    shape = (ROWS, STEPS, H * HEAD)
    normal_part = jax.random.normal(jax.random.fold_in(key, 101), shape, jnp.float32)
    return jnp.clip(query_scale * normal_part, -12.0, 12.0)


def base_field(key, shape, spread):
    normal_part = jnp.clip(jax.random.normal(jax.random.fold_in(key, 1), shape, jnp.float32), -6.0, 6.0)
    return spread * normal_part


def new_fields(key, own_key):
    sharing = H // KVH
    queries = shared_queries(key)
    summed = queries.reshape(ROWS, STEPS, KVH, sharing, HEAD).sum(axis=3).reshape(ROWS, STEPS, KVH * HEAD)
    shape = (ROWS, STEPS, KVH * HEAD)
    keys_field = base_field(jax.random.fold_in(own_key, 1), shape, 1.0)
    keys_field = keys_field + own_gain / (sharing * query_scale * query_scale) * summed
    values_field = base_field(jax.random.fold_in(own_key, 2), shape, 1.0)
    return (keys_field, values_field)


def draw_queries(key, part):
    return shared_queries(key).astype(jnp.bfloat16)


def draw_row_slot(key, part):
    return slot_order(key)


def draw_prefix_keys(key, part):
    own_key = jax.random.fold_in(key, 3)
    shape = (PREFIX, KVH * HEAD)
    field = base_field(own_key, shape, 1.0)
    return jnp.clip(field, -key_bound, key_bound).astype(jnp.bfloat16)


def draw_suffix_keys(key, part):
    own_key = jax.random.fold_in(key, 4)
    shape = (ROWS, S_CAP, KVH * HEAD)
    field = base_field(own_key, shape, suffix_scale)
    return jnp.clip(field, -key_bound, key_bound).astype(jnp.bfloat16)


def draw_new_kv(key, part):
    own_key = jax.random.fold_in(key, 5)
    keys_field, values_field = new_fields(key, own_key)
    stacked = jnp.stack([keys_field, values_field], axis=2)
    return jnp.clip(stacked, -key_bound, key_bound).astype(jnp.bfloat16)


def draw_suffix_lengths(key, part):
    own_key = jax.random.fold_in(key, 6)
    first_draw = jax.random.randint(jax.random.fold_in(own_key, 1), (ROWS,), 1, S_CAP + 1, jnp.int32)
    second_draw = jax.random.randint(jax.random.fold_in(own_key, 2), (ROWS,), 1, S_CAP + 1, jnp.int32)
    lengths = jnp.maximum(first_draw * second_draw // S_CAP, shortest)
    longest = jax.random.randint(jax.random.fold_in(own_key, 3), (), 0, ROWS, jnp.int32)
    return lengths.at[longest].set(S_CAP).astype(jnp.int32)


def shard_levels(key, shape, cuts, low, top_value):
    factor_of = 1.0
    for axis_at, blocks in cuts:
        heights = jax.random.uniform(jax.random.fold_in(jax.random.fold_in(key, 6), axis_at), (blocks,), jnp.float32, low / len(cuts), top_value / len(cuts))
        factor_of = factor_of * jnp.repeat(jnp.exp(heights), shape[axis_at] // blocks).reshape((-1,) + (1,) * (len(shape) - 1 - axis_at))
    return factor_of


def bell_draw(key, shape, width, limit, cuts=(), held_as=jnp.bfloat16):
    drawn = jax.random.normal(key, shape, jnp.float32) * width
    if len(cuts) > 0:
        drawn = shard_levels(key, shape, cuts, -0.22, 0.18) * drawn
    return jnp.clip(drawn, min=-limit, max=limit).astype(held_as)


def setup_inputs(seed: int = 0) -> dict:
    key_of = jax.random.split(jax.random.key(seed), 9)
    return {
        "queries": draw_queries(jax.random.fold_in(key_of[8], 71), 0),
        "new_kv": draw_new_kv(jax.random.fold_in(key_of[8], 71), 0),
        "prefix_keys": draw_prefix_keys(jax.random.fold_in(key_of[8], 71), 0),
        "prefix_values": bell_draw(key_of[3], (PREFIX, KVH * HEAD), 1.0, 6.0, ((0, 128),)),
        "suffix_keys": draw_suffix_keys(jax.random.fold_in(key_of[8], 71), 0),
        "suffix_values": bell_draw(key_of[5], (ROWS, S_CAP, KVH * HEAD), 1.0, 6.0, ((0, 8), (1, 16))),
        "suffix_lengths": draw_suffix_lengths(jax.random.fold_in(key_of[8], 71), 0),
        "row_slot": draw_row_slot(jax.random.fold_in(key_of[8], 71), 0),
    }


def reference(queries, new_kv, prefix_keys, prefix_values, suffix_keys, suffix_values, suffix_lengths, row_slot):
    sharing = H // KVH
    scale_factor = HEAD ** -0.5
    highest = lax.Precision.HIGHEST
    row_lengths = jnp.take(suffix_lengths, row_slot, axis=0)
    live_mask = jnp.arange(S_CAP, dtype=jnp.int32)[None, :] < row_lengths[:, None]
    causal = jnp.arange(STEPS, dtype=jnp.int32)[None, :] <= jnp.arange(STEPS, dtype=jnp.int32)[:, None]

    def rounded(weights):
        return lax.optimization_barrier(weights.astype(jnp.bfloat16)).astype(jnp.float32)

    def one_head(head_index):
        kv_group = (head_index // sharing).astype(jnp.int32)
        start = (kv_group * HEAD).astype(jnp.int32)
        query_rows = lax.dynamic_slice_in_dim(queries, (head_index * HEAD).astype(jnp.int32), HEAD, 2).astype(jnp.float32)
        prefix_k = lax.dynamic_slice_in_dim(prefix_keys, start, HEAD, 1).astype(jnp.float32)
        prefix_v = lax.dynamic_slice_in_dim(prefix_values, start, HEAD, 1).astype(jnp.float32)
        suffix_k = jnp.take(lax.dynamic_slice_in_dim(suffix_keys, start, HEAD, 2), row_slot, axis=0).astype(jnp.float32)
        suffix_v = jnp.take(lax.dynamic_slice_in_dim(suffix_values, start, HEAD, 2), row_slot, axis=0).astype(jnp.float32)
        new_k = lax.dynamic_slice_in_dim(new_kv[:, :, 0], start, HEAD, 2).astype(jnp.float32)
        new_v = lax.dynamic_slice_in_dim(new_kv[:, :, 1], start, HEAD, 2).astype(jnp.float32)
        prefix_s = jnp.einsum("rtd,pd->rtp", query_rows, prefix_k, precision=highest) * scale_factor
        suffix_s = jnp.einsum("rtd,rsd->rts", query_rows, suffix_k, precision=highest) * scale_factor
        suffix_s = jnp.where(live_mask[:, None, :], suffix_s, -jnp.inf)
        new_s = jnp.einsum("rtd,rud->rtu", query_rows, new_k, precision=highest) * scale_factor
        new_s = jnp.where(causal[None], new_s, -jnp.inf)
        row_top = jnp.maximum(jnp.maximum(jnp.max(prefix_s, axis=-1), jnp.max(suffix_s, axis=-1)), jnp.max(new_s, axis=-1))
        prefix_w = jnp.exp(prefix_s - row_top[..., None])
        suffix_w = jnp.exp(suffix_s - row_top[..., None])
        new_w = jnp.exp(new_s - row_top[..., None])
        denominator = jnp.sum(prefix_w, axis=-1) + jnp.sum(suffix_w, axis=-1) + jnp.sum(new_w, axis=-1)
        numerator = jnp.einsum("rtp,pd->rtd", rounded(prefix_w), prefix_v, precision=highest)
        numerator = numerator + jnp.einsum("rts,rsd->rtd", rounded(suffix_w), suffix_v, precision=highest)
        numerator = numerator + jnp.einsum("rtu,rud->rtd", rounded(new_w), new_v, precision=highest)
        return numerator / denominator[..., None]

    per_head = lax.map(one_head, jnp.arange(H, dtype=jnp.int32))
    return jnp.transpose(per_head, (1, 2, 0, 3)).reshape(ROWS, STEPS, H * HEAD).astype(jnp.bfloat16)
```

```python
import functools
import math

import jax
import jax.numpy as jnp
from jax import lax
from jax.experimental import pallas as pl
from jax.experimental.pallas import tpu as pltpu
from jax.sharding import PartitionSpec as P

H = 64
KVH = 8
HEAD = 128
LOWEST = -(2.0**100)
SCALE = HEAD ** (-0.5) * math.log2(math.e)
NUM_ROWS = 32
ALL_ROWS = 40
HEADS = NUM_ROWS // 8
PARAMS = pltpu.CompilerParams(vmem_limit_bytes=32 << 20)

NT = (((1,), (1,)), ((), ()))
NN = (((1,), (0,)), ((), ()))


def dot(a, b, dims):
    return lax.dot_general(a, b, dims, preferred_element_type=jnp.float32)


def iota(shape, axis):
    return lax.broadcasted_iota(jnp.int32, shape, axis)


def as_bf16(x):
    return x.astype(jnp.bfloat16).astype(jnp.float32)


def columns(x):
    return [x[:, a * HEAD : (a + 1) * HEAD] for a in range(x.shape[1] // HEAD)]


def pack(tops, totals):
    lane = iota((8, HEAD), 1)
    piece = lax.rem(lane, 32) // 8
    packed = None
    for a in range(HEADS):
        high = as_bf16(totals[a])
        mixed = jnp.where(piece == 1, high, totals[a] - high)
        mixed = jnp.where(piece == 0, tops[a], mixed)
        packed = mixed if a == 0 else jnp.where(lane // 32 == a, mixed, packed)
    return packed.astype(jnp.bfloat16)


def unpack(tails):
    shape = (HEAD, HEADS * HEAD)
    start = iota(shape, 0) - 32 * (iota(shape, 1) // HEAD)
    first = (start == 0).astype(jnp.float32).astype(jnp.bfloat16)
    second = ((start == 8) | (start == 16)).astype(jnp.float32).astype(jnp.bfloat16)
    return dot(tails, first, NN), dot(tails, second, NN)


def combine(tops, totals, numerators):
    upper = functools.reduce(jnp.maximum, tops)
    factors = [jnp.exp2(top - upper) for top in tops]
    total = sum(x * f for x, f in zip(totals, factors))
    return upper, total, sum(x * f for x, f in zip(numerators, factors))


def spread_kernel(q_ref, out_ref):
    held = [q_ref[r].astype(jnp.float32) for r in range(q_ref.shape[0])]
    heads = range(q_ref.shape[2] // HEAD)
    block = [x[:, h * HEAD : (h + 1) * HEAD] for h in heads for x in held]
    block = jnp.concatenate(block, axis=0).astype(jnp.bfloat16)
    for d in range(out_ref.shape[0]):
        out_ref[d] = block


def spread(queries, copies):
    return pl.pallas_call(
        spread_kernel,
        out_shape=jax.ShapeDtypeStruct((copies, NUM_ROWS, HEAD), jnp.bfloat16),
        compiler_params=PARAMS,
        name="spread",
    )(queries)


def stage_kernel(*refs):
    sources, outs, sems = refs[:4], refs[4:8], refs[8]
    copies = []
    for n, (source, out) in enumerate(zip(sources, outs)):
        for k in range(KVH):
            at = pl.ds(k * HEAD, HEAD)
            part = source.at[:, at] if n < 2 else source.at[:, :, at]
            copies.append(pltpu.make_async_copy(part, out.at[k], sems.at[n, k]))
    for copy in copies:
        copy.start()
    for copy in copies:
        copy.wait()


def stage(*arrays):
    outs = [pltpu.VMEM((KVH,) + x.shape[:-1] + (HEAD,), x.dtype) for x in arrays]
    size = sum(2 * x.size * x.dtype.itemsize for x in arrays)
    return pl.pallas_call(
        stage_kernel,
        in_specs=[pl.BlockSpec(memory_space=pl.ANY)] * len(arrays),
        out_specs=[pl.BlockSpec(memory_space=pl.ANY)] * len(arrays),
        out_shape=outs,
        scratch_shapes=[pltpu.SemaphoreType.DMA((len(arrays), KVH))],
        compiler_params=PARAMS,
        cost_estimate=pl.CostEstimate(flops=0, bytes_accessed=size, transcendentals=0),
        name="stage",
    )(*[pltpu.with_memory_space_constraint(x, pltpu.HBM) for x in arrays])


def attend_kernel(info, *refs, heads, chunk):
    near_ref, far_ref, k_ref, v_ref, sk_ref, sv_ref, near_out, far_out = refs[:8]
    q_ref, own_top, own_acc = refs[8:]
    pieces, _, rows, _ = q_ref.shape
    near = near_out.shape[0]
    halves = rows // NUM_ROWS
    per_chunk = chunk // rows
    length = k_ref.shape[1]
    _, slots, span, _ = sk_ref.shape
    ones = jnp.ones((length, HEAD), jnp.bfloat16)

    @pl.when(pl.program_id(0) == 0)
    def _():
        own_top[...] = jnp.full(own_top.shape, LOWEST, jnp.float32)
        own_acc[...] = jnp.zeros(own_acc.shape, jnp.float32)

    q_ref[:near] = near_ref[...]
    q_ref[near:] = far_ref[...]

    def scored(i, c):
        q = q_ref[c * per_chunk : (c + 1) * per_chunk, i].reshape(chunk, HEAD)
        return dot(q, k_ref[i], NT)

    items = [(i, c) for i in range(heads) for c in range(pieces // per_chunk)]
    scores = scored(*items[0])

    row_id = lax.rem(iota((rows, HEAD), 0), 8) // 2
    row_ids = lax.rem(iota((rows, span), 0), 8) // 2
    position = iota((rows, span), 1)
    found = []
    for j in range(slots):
        group, row, live = info[j], info[slots + j], info[2 * slots + j]
        kept = (row_ids == row) & (position < live)
        for i in range(heads):
            own = dot(q_ref[group, i], sk_ref[i, j], NT) * SCALE
            own = jnp.where(kept, own, LOWEST)
            peak = jnp.max(own, axis=1, keepdims=True)
            peak = jnp.broadcast_to(as_bf16(peak), (rows, HEAD))
            shift = jnp.concatenate([peak] * (span // HEAD), axis=1)
            weights = jnp.exp2(own - shift).astype(jnp.bfloat16)
            values = jnp.concatenate([sv_ref[i, j], ones[:span]], axis=1)
            found.append((group, i, row_id == row, peak, dot(weights, values, NN)))
    for group, i, here, peak, summed in found:
        own_top[group, i] = jnp.where(here, peak, own_top[group, i])
        both = jnp.concatenate([here, here], axis=1)
        own_acc[group, i] = jnp.where(both, summed, own_acc[group, i])

    for number, (i, c) in enumerate(items):
        later = scored(*items[number + 1]) if number + 1 < len(items) else None
        at = slice(c * per_chunk, (c + 1) * per_chunk)
        before = own_top[at, i].reshape(chunk, HEAD)
        carried = own_acc[at, i].reshape(chunk, 2 * HEAD)
        peak = jnp.max(scores, axis=1, keepdims=True) * SCALE
        top = jnp.maximum(jnp.broadcast_to(as_bf16(peak), (chunk, HEAD)), before)
        shift = jnp.concatenate([top] * (length // HEAD), axis=1)
        weights = jnp.exp2(scores * SCALE - shift).astype(jnp.bfloat16)
        values = jnp.concatenate([v_ref[i], ones], axis=1)
        keep = jnp.exp2(before - top)
        summed = dot(weights, values, NN) + carried * jnp.concatenate([keep, keep], axis=1)
        results = []
        for b in range(chunk // NUM_ROWS):
            low = b * NUM_ROWS
            parts = [slice(low + 8 * a, low + 8 * a + 8) for a in range(HEADS)]
            tail = pack([top[p] for p in parts], [summed[p, HEAD:] for p in parts])
            results.append((summed[low : low + NUM_ROWS, :HEAD].astype(jnp.bfloat16), tail))
        for b, (block, tail) in enumerate(results):
            g = c * per_chunk + b // halves
            out_ref = (near_out if g < near else far_out).at[g % near, i * halves + b % halves]
            out_ref[:NUM_ROWS] = block
            out_ref[NUM_ROWS:] = tail
        scores = later


def attend(info, near, far, keys, values, suffix_keys, suffix_values, heads, chunk):
    layers, members = near.shape[:2]
    rows = members // KVH * NUM_ROWS
    near, far = (x.reshape(layers, KVH, rows, HEAD) for x in (near, far))
    length = keys.shape[1]
    _, slots, span, _ = suffix_keys.shape
    by_head = pl.BlockSpec((layers, heads, rows, HEAD), lambda k: (0, k, 0, 0))
    prompt = pl.BlockSpec((heads, length, HEAD), lambda k: (k, 0, 0))
    own = pl.BlockSpec((heads, slots, span, HEAD), lambda k: (k, 0, 0, 0))
    out_block = (layers, heads * rows // NUM_ROWS, ALL_ROWS, HEAD)
    out_spec = pl.BlockSpec(out_block, lambda k: (0, k, 0, 0))
    out = jax.ShapeDtypeStruct((layers, members, ALL_ROWS, HEAD), jnp.bfloat16)
    return pl.pallas_call(
        functools.partial(attend_kernel, heads=heads, chunk=chunk),
        grid=(KVH // heads,),
        in_specs=[pl.BlockSpec(memory_space=pltpu.SMEM)]
        + [by_head, by_head, prompt, prompt, own, own],
        out_specs=[out_spec, out_spec],
        out_shape=[out, out],
        scratch_shapes=[
            pltpu.VMEM((2 * layers, heads, rows, HEAD), jnp.bfloat16),
            pltpu.VMEM((2 * layers, heads, rows, HEAD), jnp.float32),
            pltpu.VMEM((2 * layers, heads, rows, 2 * HEAD), jnp.float32),
        ],
        compiler_params=PARAMS,
        name="attend",
    )(info, near, far, keys, values, suffix_keys, suffix_values)


def join_parts(parts):
    count = len(parts[0])
    opened = []
    for blocks in parts:
        tails = [x[NUM_ROWS:].astype(jnp.float32) for x in blocks]
        opened.append(unpack(jnp.concatenate(tails, axis=0).astype(jnp.bfloat16)))
    joined = []
    for b in range(count):
        tops, totals, numerators = [], [], []
        for blocks, (top, total) in zip(parts, opened):
            tops.append(columns(top[b * 8 : b * 8 + 8]))
            totals.append(columns(total[b * 8 : b * 8 + 8]))
            numerator = blocks[b][:NUM_ROWS].astype(jnp.float32)
            numerators.append([numerator[a * 8 : a * 8 + 8] for a in range(HEADS)])
        rows = [
            combine([x[a] for x in tops], [x[a] for x in totals], [x[a] for x in numerators])
            for a in range(HEADS)
        ]
        block = jnp.concatenate([x[2] for x in rows], axis=0).astype(jnp.bfloat16)
        joined.append((block, pack([x[0] for x in rows], [x[1] for x in rows])))
    return joined


def join_cores_kernel(a_ref, b_ref, out_ref):
    layers, members = a_ref.shape[:2]
    for y in range(layers):
        parts = [[ref[y, m] for m in range(members)] for ref in (a_ref, b_ref)]
        for m, (block, tail) in enumerate(join_parts(parts)):
            out_ref[y, m, :NUM_ROWS] = block
            out_ref[y, m, NUM_ROWS:] = tail


def join_cores(a, b):
    return pl.pallas_call(
        join_cores_kernel,
        out_shape=jax.ShapeDtypeStruct(a.shape, a.dtype),
        compiler_params=PARAMS,
        name="join_cores",
    )(a, b)


def new_kernel(q_ref, new_ref, score_ref, value_ref):
    rows, steps, _ = q_ref.shape
    member = lax.axis_index("z") * lax.axis_size("x") + lax.axis_index("x")
    kv_head = member * HEADS // (H // KVH)
    at_head = pl.ds(pl.multiple_of(kv_head * HEAD, HEAD), HEAD)

    def new_rows(u, which):
        found = [new_ref[r, u, which : which + 1, at_head].astype(jnp.float32) for r in range(rows)]
        return jnp.concatenate([jnp.broadcast_to(x, (steps, HEAD)) for x in found], axis=0)

    held = [q_ref[r].astype(jnp.float32) for r in range(rows)]
    step = lax.rem(iota((8, HEAD), 0), steps)
    for u in range(steps):
        keys = new_rows(u, 0)
        value_ref[u] = new_rows(u, 1)
        for a in range(HEADS):
            q = jnp.concatenate([x[:, a * HEAD : (a + 1) * HEAD] for x in held], axis=0)
            score = jnp.sum(q * keys, axis=1, keepdims=True) * SCALE
            score = jnp.broadcast_to(score, (8, HEAD))
            score_ref[u, a] = jnp.where(step >= u, score, LOWEST)


def new_tokens(queries, new_kv):
    steps = queries.shape[1]
    return pl.pallas_call(
        new_kernel,
        out_shape=[
            jax.ShapeDtypeStruct((steps, HEADS, 8, HEAD), jnp.float32),
            jax.ShapeDtypeStruct((steps, 8, HEAD), jnp.float32),
        ],
        compiler_params=PARAMS,
        name="new_tokens",
    )(queries, new_kv)


def merge_kernel(parts_ref, score_ref, value_ref, out_ref):
    rows, steps, _ = out_ref.shape
    blocks = [parts_ref[s] for s in range(parts_ref.shape[0])]
    tails = [x[NUM_ROWS:].astype(jnp.float32) for x in blocks]
    opened = unpack(jnp.concatenate(tails, axis=0).astype(jnp.bfloat16))
    opened = [columns(x) for x in opened]
    one = jnp.ones((8, HEAD), jnp.float32)
    results = []
    for a in range(HEADS):
        pieces = [slice(s * 8, s * 8 + 8) for s in range(len(blocks))]
        tops = [opened[0][a][p] for p in pieces]
        totals = [opened[1][a][p] for p in pieces]
        sums = [x[a * 8 : a * 8 + 8].astype(jnp.float32) for x in blocks]
        for u in range(steps):
            tops.append(score_ref[u, a])
            totals.append(one)
            sums.append(value_ref[u])
        _, total, summed = combine(tops, totals, sums)
        results.append(summed / total)
    for a, result in enumerate(results):
        for r in range(rows):
            out_ref[r, :, a * HEAD : (a + 1) * HEAD] = result[r * steps : (r + 1) * steps].astype(
                jnp.bfloat16
            )


def merge(parts, scores, values, shape):
    return pl.pallas_call(
        merge_kernel,
        out_shape=jax.ShapeDtypeStruct(shape, jnp.bfloat16),
        compiler_params=PARAMS,
        name="merge",
    )(parts, scores, values)


CHIPS = ("y", "z", "x")


def exchange(x, axes):
    return lax.all_to_all(x, axes, split_axis=0, concat_axis=0, tiled=True)


def per_device(
    queries,
    new_kv,
    prefix_keys,
    prefix_values,
    suffix_keys,
    suffix_values,
    suffix_lengths,
    row_slot,
):
    layers = lax.axis_size("y")
    cores = lax.axis_size("core")
    members = lax.axis_size("z") * lax.axis_size("x")
    layer = lax.axis_index("y")
    core = lax.axis_index("core")
    member_index = lax.axis_index("z") * lax.axis_size("x") + lax.axis_index("x")
    per_group = queries.shape[0]
    swap = [(i, (i + 1) % cores) for i in range(cores)]

    chips = layers * members
    block = (layers, members)

    copies = spread(queries, chips)
    copies, *cached = lax.optimization_barrier(
        (copies, prefix_keys, prefix_values, suffix_keys, suffix_values)
    )
    near = exchange(copies, CHIPS).reshape(block + (NUM_ROWS, HEAD))
    near, *cached = lax.optimization_barrier((near, *stage(*cached)))
    far = lax.ppermute(near, "core", swap)

    slot_ids = (layer * cores + core) * per_group + jnp.arange(per_group, dtype=jnp.int32)
    belongs = row_slot[None, :] == slot_ids[:, None]
    row_ids = jnp.arange(row_slot.shape[0], dtype=jnp.int32)
    row_of = jnp.sum(jnp.where(belongs, row_ids[None, :], 0), axis=1)
    row_group = row_of // per_group
    place = row_group // cores + jnp.where(row_group % cores == core, 0, layers)
    span = suffix_keys.shape[1]
    live = jnp.clip(suffix_lengths - member_index * span, 0, span)
    info = jnp.concatenate([place, row_of % per_group, live])

    near_part, far_part = attend(info, near, far, *cached, 2, 128)
    joined = join_cores(near_part, lax.ppermute(far_part, "core", swap))
    joined, queries, new_kv = lax.optimization_barrier((joined, queries, new_kv))
    received = exchange(joined.reshape(chips, ALL_ROWS, HEAD), CHIPS)
    scores, values = new_tokens(queries, new_kv)
    return merge(received, scores, values, queries.shape)


def solution(mesh):
    fine = jax.sharding.Mesh(mesh.devices.reshape(4, 2, 4, 4), ("y", "core", "z", "x"))
    grp, seq = ("y", "core"), ("z", "x")
    placed = (
        P(grp, None, seq),
        P(grp, None, None, None),
        P(grp + seq, None),
        P(grp + seq, None),
        P(grp, seq, None),
        P(grp, seq, None),
        P(grp),
        P(),
    )
    return jax.shard_map(
        per_device, mesh=fine, in_specs=placed, out_specs=P(grp, None, seq), check_vma=False
    )
```

```python
import functools
import math

import jax
import jax.numpy as jnp
from jax import lax
from jax.experimental import pallas as pl
from jax.experimental.pallas import tpu as pltpu
from jax.sharding import PartitionSpec as P

H = 64
KVH = 8
HEAD = 128
LOWEST = -(2.0**100)
SCALE = HEAD ** (-0.5) * math.log2(math.e)
TAIL = 8
SHARES = 1
PARAMS = pltpu.CompilerParams(vmem_limit_bytes=32 << 20)

NT = (((1,), (1,)), ((), ()))
NN = (((1,), (0,)), ((), ()))


def dot(a, b, dims):
    return lax.dot_general(a, b, dims, preferred_element_type=jnp.float32)


def iota(shape, axis):
    return lax.broadcasted_iota(jnp.int32, shape, axis)


def as_bf16(x):
    return x.astype(jnp.bfloat16).astype(jnp.float32)


def columns(x):
    return [x[:, a * HEAD : (a + 1) * HEAD] for a in range(x.shape[1] // HEAD)]


def pack(tops, totals):
    lane = iota((TAIL, HEAD), 1)
    piece = lax.rem(lane, 32) // 8
    packed = None
    for a, (top, total) in enumerate(zip(tops, totals)):
        high = as_bf16(total)
        mixed = jnp.where(piece == 1, high, total - high)
        mixed = jnp.where(piece == 0, top, mixed)
        packed = mixed if a == 0 else jnp.where(lane // 32 == a, mixed, packed)
    return packed.astype(jnp.bfloat16)


def unpack(tails, tiles):
    shape = (HEAD, tiles * HEAD)
    start = iota(shape, 0) - 32 * (iota(shape, 1) // HEAD)
    first = (start == 0).astype(jnp.float32).astype(jnp.bfloat16)
    second = ((start == 8) | (start == 16)).astype(jnp.float32).astype(jnp.bfloat16)
    return dot(tails, first, NN), dot(tails, second, NN)


def combine(tops, totals, numerators):
    upper = functools.reduce(jnp.maximum, tops)
    factors = [jnp.exp2(top - upper) for top in tops]
    total = sum(x * f for x, f in zip(totals, factors))
    return upper, total, sum(x * f for x, f in zip(numerators, factors))


def query_rows(q_ref, share):
    count = q_ref.shape[0] // SHARES
    held = [q_ref[share * count + r].astype(jnp.float32) for r in range(count)]
    heads = range(q_ref.shape[2] // HEAD)
    return jnp.concatenate([x[:, h * HEAD : (h + 1) * HEAD] for h in heads for x in held], axis=0)


def spread_kernel(q_ref, *out_refs):
    for share, out_ref in enumerate(out_refs):
        block = query_rows(q_ref, share).astype(jnp.bfloat16)
        for d in range(out_ref.shape[0]):
            out_ref[d] = block


def spread(queries, copies):
    rows = queries.size // HEAD // SHARES
    out = jax.ShapeDtypeStruct((copies, rows, HEAD), jnp.bfloat16)
    return pl.pallas_call(
        spread_kernel,
        out_shape=[out] * SHARES,
        compiler_params=PARAMS,
        name="spread",
    )(queries)


def locate_kernel(slot_ref, length_ref, info, *, span):
    slots = length_ref.shape[0]
    cores, layers = lax.axis_size("core"), lax.axis_size("y")
    core = lax.axis_index("core")
    first = (lax.axis_index("y") * cores + core) * slots
    start = (lax.axis_index("z") * lax.axis_size("x") + lax.axis_index("x")) * span
    for j in range(slots):
        row = jnp.int32(0)
        for r in range(slot_ref.shape[0]):
            row = jnp.where(slot_ref[r] == first + j, jnp.int32(r), row)
        group = lax.div(row, slots)
        far = jnp.where(lax.rem(group, cores) == core, 0, layers)
        info[j] = lax.div(group, cores) + far
        info[slots + j] = lax.rem(row, slots)
        info[2 * slots + j] = jnp.clip(length_ref[j] - start, 0, span)


def locate(row_slot, lengths, span):
    smem = pl.BlockSpec(memory_space=pltpu.SMEM)
    return pl.pallas_call(
        functools.partial(locate_kernel, span=span),
        in_specs=[smem, smem],
        out_specs=smem,
        out_shape=jax.ShapeDtypeStruct((3 * lengths.shape[0],), jnp.int32),
        compiler_params=PARAMS,
        name="locate",
    )(row_slot, lengths)


def attend_kernel(info, *refs, heads, chunk, share, steps):
    near_ref, far_ref, k_ref, v_ref, sk_ref, sv_ref, near_out, far_out = refs[:8]
    q_ref, own_top, own_acc = refs[8:]
    pieces, _, rows, _ = q_ref.shape
    near = near_out.shape[0]
    numerators = near_out.shape[2] - TAIL
    halves = rows // numerators
    per_chunk = chunk // rows
    length = k_ref.shape[0]
    slots, span, _ = sk_ref.shape
    count = slots // SHARES
    stride = count * steps
    ones = jnp.ones((length, HEAD), jnp.bfloat16)

    @pl.when(pl.program_id(0) == 0)
    def _():
        own_top[...] = jnp.full(own_top.shape, LOWEST, jnp.float32)
        own_acc[...] = jnp.zeros(own_acc.shape, jnp.float32)

    q_ref[:near] = near_ref[...]
    q_ref[near:] = far_ref[...]

    def cut(i):
        return slice(i * HEAD, (i + 1) * HEAD)

    def scored(i, c):
        q = q_ref[c * per_chunk : (c + 1) * per_chunk, i].reshape(chunk, HEAD)
        return dot(q, k_ref[:, cut(i)], NT)

    items = [(i, c) for i in range(heads) for c in range(pieces // per_chunk)]
    scores = scored(*items[0])

    row_id = lax.rem(iota((rows, HEAD), 0), stride) // steps + share * count
    row_ids = lax.rem(iota((rows, span), 0), stride) // steps + share * count
    position = iota((rows, span), 1)
    found = []
    for j in range(slots):
        group, row, live = info[j], info[slots + j], info[2 * slots + j]
        kept = (row_ids == row) & (position < live)
        for i in range(heads):
            own = dot(q_ref[group, i], sk_ref[j, :, cut(i)], NT) * SCALE
            own = jnp.where(kept, own, LOWEST)
            peak = jnp.max(own, axis=1, keepdims=True)
            peak = jnp.broadcast_to(as_bf16(peak), (rows, HEAD))
            shift = jnp.concatenate([peak] * (span // HEAD), axis=1)
            weights = jnp.exp2(own - shift).astype(jnp.bfloat16)
            values = jnp.concatenate([sv_ref[j, :, cut(i)], ones[:span]], axis=1)
            found.append((group, i, row_id == row, peak, dot(weights, values, NN)))
    for group, i, here, peak, summed in found:
        own_top[group, i] = jnp.where(here, peak, own_top[group, i])
        both = jnp.concatenate([here, here], axis=1)
        own_acc[group, i] = jnp.where(both, summed, own_acc[group, i])

    for number, (i, c) in enumerate(items):
        later = scored(*items[number + 1]) if number + 1 < len(items) else None
        at = slice(c * per_chunk, (c + 1) * per_chunk)
        before = own_top[at, i].reshape(chunk, HEAD)
        carried = own_acc[at, i].reshape(chunk, 2 * HEAD)
        peak = jnp.max(scores, axis=1, keepdims=True) * SCALE
        top = jnp.maximum(jnp.broadcast_to(as_bf16(peak), (chunk, HEAD)), before)
        shift = jnp.concatenate([top] * (length // HEAD), axis=1)
        weights = jnp.exp2(scores * SCALE - shift).astype(jnp.bfloat16)
        values = jnp.concatenate([v_ref[:, cut(i)], ones], axis=1)
        keep = jnp.exp2(before - top)
        summed = dot(weights, values, NN) + carried * jnp.concatenate([keep, keep], axis=1)
        results = []
        for b in range(chunk // numerators):
            low = b * numerators
            parts = [slice(low + 8 * a, low + 8 * a + 8) for a in range(numerators // 8)]
            tail = pack([top[p] for p in parts], [summed[p, HEAD:] for p in parts])
            results.append((summed[low : low + numerators, :HEAD].astype(jnp.bfloat16), tail))
        for b, (block, tail) in enumerate(results):
            g = c * per_chunk + b // halves
            out_ref = (near_out if g < near else far_out).at[g % near, i * halves + b % halves]
            out_ref[:numerators] = block
            out_ref[numerators:] = tail
        scores = later


def attend(info, near, far, keys, values, suffix_keys, suffix_values, share, heads, chunk):
    layers, members, numerators, _ = near.shape
    rows = members // KVH * numerators
    near, far = (x.reshape(layers, KVH, rows, HEAD) for x in (near, far))
    length = keys.shape[0]
    slots, span, _ = suffix_keys.shape
    steps = numerators * members * SHARES // (H * slots)
    in_hbm = [
        pltpu.with_memory_space_constraint(x, pltpu.HBM)
        for x in (keys, values, suffix_keys, suffix_values)
    ]
    wide = heads * HEAD
    by_head = pl.BlockSpec((layers, heads, rows, HEAD), lambda k: (0, k, 0, 0))
    prompt = pl.BlockSpec((length, wide), lambda k: (0, k))
    own = pl.BlockSpec((slots, span, wide), lambda k: (0, 0, k))
    out_block = (layers, heads * members // KVH, numerators + TAIL, HEAD)
    out_spec = pl.BlockSpec(out_block, lambda k: (0, k, 0, 0))
    out = jax.ShapeDtypeStruct((layers, members, numerators + TAIL, HEAD), jnp.bfloat16)
    return pl.pallas_call(
        functools.partial(attend_kernel, heads=heads, chunk=chunk, share=share, steps=steps),
        grid=(KVH // heads,),
        in_specs=[pl.BlockSpec(memory_space=pltpu.SMEM), by_head, by_head, prompt, prompt, own, own],
        out_specs=[out_spec, out_spec],
        out_shape=[out, out],
        scratch_shapes=[
            pltpu.VMEM((2 * layers, heads, rows, HEAD), jnp.bfloat16),
            pltpu.VMEM((2 * layers, heads, rows, HEAD), jnp.float32),
            pltpu.VMEM((2 * layers, heads, rows, 2 * HEAD), jnp.float32),
        ],
        compiler_params=PARAMS,
        name="attend",
    )(info, near, far, *in_hbm)


def join_parts(parts):
    numerators = parts[0][0].shape[0] - TAIL
    tiles = numerators // 8
    opened = []
    for blocks in parts:
        tails = [x[numerators:].astype(jnp.float32) for x in blocks]
        opened.append(unpack(jnp.concatenate(tails, axis=0).astype(jnp.bfloat16), tiles))
    joined = []
    for b in range(len(parts[0])):
        tops, totals, sums = [], [], []
        for blocks, (top, total) in zip(parts, opened):
            tops.append(columns(top[b * 8 : b * 8 + 8]))
            totals.append(columns(total[b * 8 : b * 8 + 8]))
            found = blocks[b][:numerators].astype(jnp.float32)
            sums.append([found[a * 8 : a * 8 + 8] for a in range(tiles)])
        rows = [
            combine([x[a] for x in tops], [x[a] for x in totals], [x[a] for x in sums])
            for a in range(tiles)
        ]
        block = jnp.concatenate([x[2] for x in rows], axis=0).astype(jnp.bfloat16)
        joined.append((block, pack([x[0] for x in rows], [x[1] for x in rows])))
    return joined


def join_cores_kernel(a_ref, b_ref, out_ref):
    layers, members, rows, _ = a_ref.shape
    for y in range(layers):
        parts = [[ref[y, m] for m in range(members)] for ref in (a_ref, b_ref)]
        for m, (block, tail) in enumerate(join_parts(parts)):
            out_ref[y, m, : rows - TAIL] = block
            out_ref[y, m, rows - TAIL :] = tail


def join_cores(a, b):
    return pl.pallas_call(
        join_cores_kernel,
        out_shape=jax.ShapeDtypeStruct(a.shape, a.dtype),
        compiler_params=PARAMS,
        name="join_cores",
    )(a, b)


def new_kernel(q_ref, new_ref, score_ref, value_ref):
    rows, steps, _ = q_ref.shape
    shares, _, tiles = score_ref.shape[:3]
    count = rows // shares
    heads = q_ref.shape[2] // HEAD
    member = lax.axis_index("z") * lax.axis_size("x") + lax.axis_index("x")
    kv_head = member * heads // (H // KVH)
    at_head = pl.ds(pl.multiple_of(kv_head * HEAD, HEAD), HEAD)
    step = lax.rem(iota((8, HEAD), 0), steps)

    def new_rows(share, u, which):
        found = [
            new_ref[share * count + r, u, which : which + 1, at_head].astype(jnp.float32)
            for r in range(count)
        ]
        found = [jnp.broadcast_to(x, (steps, HEAD)) for x in found]
        return jnp.concatenate(found * (8 // (count * steps)), axis=0)

    for share in range(shares):
        queries = query_rows(q_ref, share)
        for u in range(steps):
            keys = new_rows(share, u, 0)
            value_ref[share, u] = new_rows(share, u, 1)
            for a in range(tiles):
                score = jnp.sum(queries[a * 8 : a * 8 + 8] * keys, axis=1, keepdims=True) * SCALE
                score = jnp.broadcast_to(score, (8, HEAD))
                score_ref[share, u, a] = jnp.where(step >= u, score, LOWEST)


def new_tokens(queries, new_kv):
    steps = queries.shape[1]
    tiles = queries.size // HEAD // SHARES // 8
    return pl.pallas_call(
        new_kernel,
        out_shape=[
            jax.ShapeDtypeStruct((SHARES, steps, tiles, 8, HEAD), jnp.float32),
            jax.ShapeDtypeStruct((SHARES, steps, 8, HEAD), jnp.float32),
        ],
        compiler_params=PARAMS,
        name="new_tokens",
    )(queries, new_kv)


def merge_kernel(*refs):
    parts, (score_ref, value_ref, out_ref) = refs[:-3], refs[-3:]
    rows, steps, _ = out_ref.shape
    count = rows // len(parts)
    one = jnp.ones((8, HEAD), jnp.float32)
    results = []
    for share, ref in enumerate(parts):
        sources, size, _ = ref.shape
        numerators = size - TAIL
        tiles = numerators // 8
        blocks = [ref[s] for s in range(sources)]
        tails = [x[numerators:].astype(jnp.float32) for x in blocks]
        opened = unpack(jnp.concatenate(tails, axis=0).astype(jnp.bfloat16), tiles)
        opened = [columns(x) for x in opened]
        for a in range(tiles):
            pieces = [slice(s * 8, s * 8 + 8) for s in range(sources)]
            tops = [opened[0][a][p] for p in pieces]
            totals = [opened[1][a][p] for p in pieces]
            sums = [x[a * 8 : a * 8 + 8].astype(jnp.float32) for x in blocks]
            for u in range(steps):
                tops.append(score_ref[share, u, a])
                totals.append(one)
                sums.append(value_ref[share, u])
            _, total, summed = combine(tops, totals, sums)
            results.append((share, a * 8, summed / total))
    for share, low, result in results:
        for at in range(0, 8, steps):
            head, row = divmod((low + at) // steps, count)
            out_ref[share * count + row, :, head * HEAD : (head + 1) * HEAD] = result[
                at : at + steps
            ].astype(jnp.bfloat16)


def merge(parts, scores, values, shape):
    return pl.pallas_call(
        merge_kernel,
        out_shape=jax.ShapeDtypeStruct(shape, jnp.bfloat16),
        compiler_params=PARAMS,
        name="merge",
    )(*parts, scores, values)


CHIPS = ("y", "z", "x")


def exchange(x, axes):
    return lax.all_to_all(x, axes, split_axis=0, concat_axis=0, tiled=True)


def per_device(
    queries,
    new_kv,
    prefix_keys,
    prefix_values,
    suffix_keys,
    suffix_values,
    suffix_lengths,
    row_slot,
):
    layers = lax.axis_size("y")
    cores = lax.axis_size("core")
    members = lax.axis_size("z") * lax.axis_size("x")
    chips = layers * members
    swap = [(i, (i + 1) % cores) for i in range(cores)]

    blocks, row_slot, suffix_lengths = lax.optimization_barrier(
        (spread(queries, chips), row_slot, suffix_lengths)
    )
    near = [exchange(x, CHIPS).reshape((layers, members) + x.shape[1:]) for x in blocks]
    info = locate(row_slot, suffix_lengths, suffix_keys.shape[1])
    received = []
    for share, mine in enumerate(near):
        mine, info = lax.optimization_barrier((mine, info))
        other = lax.ppermute(mine, "core", swap)
        near_part, far_part = attend(
            info, mine, other, prefix_keys, prefix_values, suffix_keys, suffix_values, share, 2, 128
        )
        joined = join_cores(near_part, lax.ppermute(far_part, "core", swap))
        if share == SHARES - 1:
            joined, queries, new_kv = lax.optimization_barrier((joined, queries, new_kv))
        received.append(exchange(joined.reshape((chips,) + joined.shape[2:]), CHIPS))
    scores, values = new_tokens(queries, new_kv)
    return merge(received, scores, values, queries.shape)


def solution(mesh):
    fine = jax.sharding.Mesh(mesh.devices.reshape(4, 2, 4, 4), ("y", "core", "z", "x"))
    grp, seq = ("y", "core"), ("z", "x")
    placed = (
        P(grp, None, seq),
        P(grp, None, None, None),
        P(grp + seq, None),
        P(grp + seq, None),
        P(grp, seq, None),
        P(grp, seq, None),
        P(grp),
        P(),
    )
    return jax.shard_map(
        per_device, mesh=fine, in_specs=placed, out_specs=P(grp, None, seq), check_vma=False
    )
```

```python
import functools
import math

import jax
import jax.numpy as jnp
from jax import lax
from jax.experimental import pallas as pl
from jax.experimental.pallas import tpu as pltpu
from jax.sharding import PartitionSpec as P

H = 64
KVH = 8
HEAD = 128
LOWEST = -(2.0**100)
SCALE = HEAD ** (-0.5) * math.log2(math.e)
TAIL = 8
PARAMS = pltpu.CompilerParams(vmem_limit_bytes=32 << 20)

NT = (((1,), (1,)), ((), ()))
NN = (((1,), (0,)), ((), ()))


def dot(a, b, dims):
    return lax.dot_general(a, b, dims, preferred_element_type=jnp.float32)


def iota(shape, axis):
    return lax.broadcasted_iota(jnp.int32, shape, axis)


def as_bf16(x):
    return x.astype(jnp.bfloat16).astype(jnp.float32)


def columns(x):
    return [x[:, a * HEAD : (a + 1) * HEAD] for a in range(x.shape[1] // HEAD)]


def pack(tops, totals):
    lane = iota((TAIL, HEAD), 1)
    piece = lax.rem(lane, 32) // 8
    packed = None
    for a, (top, total) in enumerate(zip(tops, totals)):
        high = as_bf16(total)
        mixed = jnp.where(piece == 1, high, total - high)
        mixed = jnp.where(piece == 0, top, mixed)
        packed = mixed if a == 0 else jnp.where(lane // 32 == a, mixed, packed)
    return packed.astype(jnp.bfloat16)


def unpack(tails, tiles):
    shape = (HEAD, tiles * HEAD)
    start = iota(shape, 0) - 32 * (iota(shape, 1) // HEAD)
    first = (start == 0).astype(jnp.float32).astype(jnp.bfloat16)
    second = ((start == 8) | (start == 16)).astype(jnp.float32).astype(jnp.bfloat16)
    return dot(tails, first, NN), dot(tails, second, NN)


def combine(tops, totals, numerators):
    upper = functools.reduce(jnp.maximum, tops)
    factors = [jnp.exp2(top - upper) for top in tops]
    total = sum(x * f for x, f in zip(totals, factors))
    return upper, total, sum(x * f for x, f in zip(numerators, factors))


def query_rows(q_ref):
    heads = range(q_ref.shape[2] // HEAD)
    held = [q_ref[r].astype(jnp.float32) for r in range(q_ref.shape[0])]
    return jnp.concatenate([x[:, h * HEAD : (h + 1) * HEAD] for x in held for h in heads], axis=0)


def spread_kernel(q_ref, out_ref):
    block = query_rows(q_ref).astype(jnp.bfloat16)
    for d in range(out_ref.shape[0]):
        out_ref[d] = block


def spread(queries, copies):
    return pl.pallas_call(
        spread_kernel,
        out_shape=jax.ShapeDtypeStruct((copies, queries.size // HEAD, HEAD), jnp.bfloat16),
        compiler_params=PARAMS,
        name="spread",
    )(queries)


def locate_kernel(slot_ref, length_ref, info, *, span):
    slots = length_ref.shape[0]
    cores, layers = lax.axis_size("core"), lax.axis_size("y")
    core = lax.axis_index("core")
    first = (lax.axis_index("y") * cores + core) * slots
    start = (lax.axis_index("z") * lax.axis_size("x") + lax.axis_index("x")) * span
    for j in range(slots):
        row = jnp.int32(0)
        for r in range(slot_ref.shape[0]):
            row = jnp.where(slot_ref[r] == first + j, jnp.int32(r), row)
        group = lax.div(row, slots)
        far = jnp.where(lax.rem(group, cores) == core, 0, layers)
        info[j] = lax.div(group, cores) + far
        info[slots + j] = lax.rem(row, slots)
        info[2 * slots + j] = jnp.clip(length_ref[j] - start, 0, span)


def locate(row_slot, lengths, span):
    smem = pl.BlockSpec(memory_space=pltpu.SMEM)
    return pl.pallas_call(
        functools.partial(locate_kernel, span=span),
        in_specs=[smem, smem],
        out_specs=smem,
        out_shape=jax.ShapeDtypeStruct((3 * lengths.shape[0],), jnp.int32),
        compiler_params=PARAMS,
        name="locate",
    )(row_slot, lengths)


def attend_kernel(info, *refs, heads, chunk):
    near_ref, far_ref, k_ref, v_ref, sk_ref, sv_ref, near_out, far_out = refs[:8]
    q_ref, own_top, own_acc = refs[8:]
    near, _, rows, _ = near_ref.shape
    pieces, _, halves, tiles = q_ref.shape[:4]
    numerators = tiles * 8
    per_chunk = chunk // rows
    length = k_ref.shape[0]
    slots, span, _ = sk_ref.shape
    ones = jnp.ones((length, HEAD), jnp.bfloat16)

    @pl.when(pl.program_id(0) == 0)
    def _():
        own_top[...] = jnp.full(own_top.shape, LOWEST, jnp.float32)
        own_acc[...] = jnp.zeros(own_acc.shape, jnp.float32)

    def cut(i):
        return slice(i * HEAD, (i + 1) * HEAD)

    def scored(i, c):
        g = c * per_chunk
        ref = near_ref if g < near else far_ref
        q = ref[g % near : g % near + per_chunk, i].reshape(chunk, HEAD)
        return dot(q, k_ref[:, cut(i)], NT)

    items = [(i, c) for i in range(heads) for c in range(pieces // per_chunk)]
    scores = scored(*items[0])

    held = [near_ref[...].astype(jnp.float32), far_ref[...].astype(jnp.float32)]
    for n, x in enumerate(held):
        q_ref[n * near : (n + 1) * near] = x.reshape((near,) + q_ref.shape[1:])
    position = iota((halves * 8, span), 1)
    found = []
    for j in range(slots):
        group, row, live = info[j], info[slots + j], info[2 * slots + j]
        for i in range(heads):
            q = q_ref[group, i, :, row].reshape(halves * 8, HEAD).astype(jnp.bfloat16)
            own = dot(q, sk_ref[j, :, cut(i)], NT) * SCALE
            own = jnp.where(position < live, own, LOWEST)
            peak = jnp.max(own, axis=1, keepdims=True)
            peak = jnp.broadcast_to(as_bf16(peak), (halves * 8, HEAD))
            shift = jnp.concatenate([peak] * (span // HEAD), axis=1)
            weights = jnp.exp2(own - shift).astype(jnp.bfloat16)
            values = jnp.concatenate([sv_ref[j, :, cut(i)], ones[:span]], axis=1)
            found.append((group, i, row, peak, dot(weights, values, NN)))
    for group, i, row, peak, summed in found:
        own_top[group, i, :, row] = peak.reshape(halves, 8, HEAD)
        own_acc[group, i, :, row] = summed.reshape(halves, 8, 2 * HEAD)

    for number, (i, c) in enumerate(items):
        later = scored(*items[number + 1]) if number + 1 < len(items) else None
        peak = jnp.max(scores, axis=1, keepdims=True) * SCALE
        peak = jnp.broadcast_to(as_bf16(peak), (chunk, HEAD))
        shift = jnp.concatenate([peak] * (length // HEAD), axis=1)
        weights = jnp.exp2(scores * SCALE - shift).astype(jnp.bfloat16)
        values = jnp.concatenate([v_ref[:, cut(i)], ones], axis=1)
        summed = dot(weights, values, NN)
        at = slice(c * per_chunk, (c + 1) * per_chunk)
        own = own_top[at, i].reshape(chunk, HEAD)
        carried = own_acc[at, i].reshape(chunk, 2 * HEAD)
        top = jnp.maximum(peak, own)
        keep, add = jnp.exp2(peak - top), jnp.exp2(own - top)
        total = summed[:, HEAD:] * keep + carried[:, HEAD:] * add
        numerator = (summed[:, :HEAD] * keep + carried[:, :HEAD] * add).astype(jnp.bfloat16)
        results = []
        for b in range(chunk // numerators):
            low = b * numerators
            parts = [slice(low + 8 * a, low + 8 * a + 8) for a in range(tiles)]
            tail = pack([top[p] for p in parts], [total[p] for p in parts])
            results.append((numerator[low : low + numerators], tail))
        for b, (block, tail) in enumerate(results):
            g = c * per_chunk + b // halves
            out_ref = (near_out if g < near else far_out).at[g % near, i * halves + b % halves]
            out_ref[:numerators] = block
            out_ref[numerators:] = tail
        scores = later


def attend(info, near, far, keys, values, suffix_keys, suffix_values, heads, chunk):
    layers, members, numerators, _ = near.shape
    halves = members // KVH
    rows = halves * numerators
    near, far = (x.reshape(layers, KVH, rows, HEAD) for x in (near, far))
    length = keys.shape[0]
    slots, span, _ = suffix_keys.shape
    in_hbm = [
        pltpu.with_memory_space_constraint(x, pltpu.HBM)
        for x in (keys, values, suffix_keys, suffix_values)
    ]
    wide = heads * HEAD
    by_head = pl.BlockSpec((layers, heads, rows, HEAD), lambda k: (0, k, 0, 0))
    prompt = pl.BlockSpec((length, wide), lambda k: (0, k))
    own = pl.BlockSpec((slots, span, wide), lambda k: (0, 0, k))
    out_block = (layers, heads * halves, numerators + TAIL, HEAD)
    out_spec = pl.BlockSpec(out_block, lambda k: (0, k, 0, 0))
    out = jax.ShapeDtypeStruct((layers, members, numerators + TAIL, HEAD), jnp.bfloat16)
    tiled = (2 * layers, heads, halves, numerators // 8, 8)
    return pl.pallas_call(
        functools.partial(attend_kernel, heads=heads, chunk=chunk),
        grid=(KVH // heads,),
        in_specs=[pl.BlockSpec(memory_space=pltpu.SMEM), by_head, by_head, prompt, prompt, own, own],
        out_specs=[out_spec, out_spec],
        out_shape=[out, out],
        scratch_shapes=[
            pltpu.VMEM(tiled + (HEAD,), jnp.float32),
            pltpu.VMEM(tiled + (HEAD,), jnp.float32),
            pltpu.VMEM(tiled + (2 * HEAD,), jnp.float32),
        ],
        compiler_params=PARAMS,
        name="attend",
    )(info, near, far, *in_hbm)


def join_parts(parts):
    numerators = parts[0][0].shape[0] - TAIL
    tiles = numerators // 8
    opened = []
    for blocks in parts:
        tails = [x[numerators:].astype(jnp.float32) for x in blocks]
        opened.append(unpack(jnp.concatenate(tails, axis=0).astype(jnp.bfloat16), tiles))
    joined = []
    for b in range(len(parts[0])):
        tops, totals, sums = [], [], []
        for blocks, (top, total) in zip(parts, opened):
            tops.append(columns(top[b * 8 : b * 8 + 8]))
            totals.append(columns(total[b * 8 : b * 8 + 8]))
            found = blocks[b][:numerators].astype(jnp.float32)
            sums.append([found[a * 8 : a * 8 + 8] for a in range(tiles)])
        rows = [
            combine([x[a] for x in tops], [x[a] for x in totals], [x[a] for x in sums])
            for a in range(tiles)
        ]
        block = jnp.concatenate([x[2] for x in rows], axis=0).astype(jnp.bfloat16)
        joined.append((block, pack([x[0] for x in rows], [x[1] for x in rows])))
    return joined


def join_cores_kernel(a_ref, b_ref, out_ref):
    layers, members, rows, _ = a_ref.shape
    for y in range(layers):
        parts = [[ref[y, m] for m in range(members)] for ref in (a_ref, b_ref)]
        for m, (block, tail) in enumerate(join_parts(parts)):
            out_ref[y, m, : rows - TAIL] = block
            out_ref[y, m, rows - TAIL :] = tail


def join_cores(a, b):
    return pl.pallas_call(
        join_cores_kernel,
        out_shape=jax.ShapeDtypeStruct(a.shape, a.dtype),
        compiler_params=PARAMS,
        name="join_cores",
    )(a, b)


def new_kernel(q_ref, new_ref, score_ref, value_ref):
    rows, steps, width = q_ref.shape
    member = lax.axis_index("z") * lax.axis_size("x") + lax.axis_index("x")
    kv_head = member * (width // HEAD) // (H // KVH)
    at_head = pl.ds(pl.multiple_of(kv_head * HEAD, HEAD), HEAD)
    step = lax.rem(iota((8, HEAD), 0), steps)
    queries = query_rows(q_ref)
    for r in range(rows):
        for u in range(steps):
            key, value = (
                jnp.broadcast_to(new_ref[r, u, n : n + 1, at_head].astype(jnp.float32), (8, HEAD))
                for n in range(2)
            )
            score = jnp.sum(queries[r * 8 : r * 8 + 8] * key, axis=1, keepdims=True) * SCALE
            score_ref[u, r] = jnp.where(step >= u, jnp.broadcast_to(score, (8, HEAD)), LOWEST)
            value_ref[u, r] = value


def new_tokens(queries, new_kv):
    rows, steps, _ = queries.shape
    out = jax.ShapeDtypeStruct((steps, rows, 8, HEAD), jnp.float32)
    return pl.pallas_call(
        new_kernel,
        out_shape=[out, out],
        compiler_params=PARAMS,
        name="new_tokens",
    )(queries, new_kv)


def merge_kernel(parts_ref, score_ref, value_ref, out_ref):
    rows, steps, width = out_ref.shape
    sources, size, _ = parts_ref.shape
    numerators = size - TAIL
    one = jnp.ones((8, HEAD), jnp.float32)
    blocks = [parts_ref[s] for s in range(sources)]
    tails = [x[numerators:].astype(jnp.float32) for x in blocks]
    opened = unpack(jnp.concatenate(tails, axis=0).astype(jnp.bfloat16), rows)
    opened = [columns(x) for x in opened]
    results = []
    for r in range(rows):
        pieces = [slice(s * 8, s * 8 + 8) for s in range(sources)]
        tops = [opened[0][r][p] for p in pieces]
        totals = [opened[1][r][p] for p in pieces]
        sums = [x[r * 8 : r * 8 + 8].astype(jnp.float32) for x in blocks]
        for u in range(steps):
            tops.append(score_ref[u, r])
            totals.append(one)
            sums.append(value_ref[u, r])
        _, total, summed = combine(tops, totals, sums)
        results.append(summed / total)
    for r, result in enumerate(results):
        for h in range(width // HEAD):
            out_ref[r, :, h * HEAD : (h + 1) * HEAD] = result[h * steps : (h + 1) * steps].astype(
                jnp.bfloat16
            )


def merge(parts, scores, values, shape):
    return pl.pallas_call(
        merge_kernel,
        out_shape=jax.ShapeDtypeStruct(shape, jnp.bfloat16),
        compiler_params=PARAMS,
        name="merge",
    )(parts, scores, values)


CHIPS = ("y", "z", "x")


def exchange(x, axes):
    return lax.all_to_all(x, axes, split_axis=0, concat_axis=0, tiled=True)


def per_device(
    queries,
    new_kv,
    prefix_keys,
    prefix_values,
    suffix_keys,
    suffix_values,
    suffix_lengths,
    row_slot,
):
    layers = lax.axis_size("y")
    cores = lax.axis_size("core")
    members = lax.axis_size("z") * lax.axis_size("x")
    chips = layers * members
    swap = [(i, (i + 1) % cores) for i in range(cores)]

    blocks, row_slot, suffix_lengths = lax.optimization_barrier(
        (spread(queries, chips), row_slot, suffix_lengths)
    )
    near = exchange(blocks, CHIPS)
    near, info = lax.optimization_barrier(
        (near, locate(row_slot, suffix_lengths, suffix_keys.shape[1]))
    )
    near = near.reshape((layers, members) + near.shape[1:])
    far = lax.ppermute(near, "core", swap)
    near_part, far_part = attend(
        info, near, far, prefix_keys, prefix_values, suffix_keys, suffix_values, 2, 128
    )
    joined = join_cores(near_part, lax.ppermute(far_part, "core", swap))
    joined, queries, new_kv = lax.optimization_barrier((joined, queries, new_kv))
    received = exchange(joined.reshape((chips,) + joined.shape[2:]), CHIPS)
    scores, values = new_tokens(queries, new_kv)
    return merge(received, scores, values, queries.shape)


def solution(mesh):
    fine = jax.sharding.Mesh(mesh.devices.reshape(4, 2, 4, 4), ("y", "core", "z", "x"))
    grp, seq = ("y", "core"), ("z", "x")
    placed = (
        P(grp, None, seq),
        P(grp, None, None, None),
        P(grp + seq, None),
        P(grp + seq, None),
        P(grp, seq, None),
        P(grp, seq, None),
        P(grp),
        P(),
    )
    return jax.shard_map(
        per_device, mesh=fine, in_specs=placed, out_specs=P(grp, None, seq), check_vma=False
    )
```

```python
import functools
import math

import jax
import jax.numpy as jnp
from jax import lax
from jax.experimental import pallas as pl
from jax.experimental.pallas import tpu as pltpu
from jax.sharding import PartitionSpec as P

H = 64
KVH = 8
HEAD = 128
LOWEST = -(2.0**100)
SCALE = HEAD ** (-0.5) * math.log2(math.e)
TAIL = 8
PARAMS = pltpu.CompilerParams(vmem_limit_bytes=32 << 20)

NT = (((1,), (1,)), ((), ()))
NN = (((1,), (0,)), ((), ()))


def dot(a, b, dims):
    return lax.dot_general(a, b, dims, preferred_element_type=jnp.float32)


def iota(shape, axis):
    return lax.broadcasted_iota(jnp.int32, shape, axis)


def as_bf16(x):
    return x.astype(jnp.bfloat16).astype(jnp.float32)


def columns(x):
    return [x[:, a * HEAD : (a + 1) * HEAD] for a in range(x.shape[1] // HEAD)]


def pack(tops, totals):
    lane = iota((TAIL, HEAD), 1)
    piece = lax.rem(lane, 32) // 8
    packed = None
    for a, (top, total) in enumerate(zip(tops, totals)):
        high = as_bf16(total)
        mixed = jnp.where(piece == 1, high, total - high)
        mixed = jnp.where(piece == 0, top, mixed)
        packed = mixed if a == 0 else jnp.where(lane // 32 == a, mixed, packed)
    return packed.astype(jnp.bfloat16)


def unpack(tails, tiles):
    shape = (HEAD, tiles * HEAD)
    start = iota(shape, 0) - 32 * (iota(shape, 1) // HEAD)
    first = (start == 0).astype(jnp.float32).astype(jnp.bfloat16)
    second = ((start == 8) | (start == 16)).astype(jnp.float32).astype(jnp.bfloat16)
    return dot(tails, first, NN), dot(tails, second, NN)


def combine(tops, totals, numerators):
    upper = functools.reduce(jnp.maximum, tops)
    factors = [jnp.exp2(top - upper) for top in tops]
    total = sum(x * f for x, f in zip(totals, factors))
    return upper, total, sum(x * f for x, f in zip(numerators, factors))


def query_rows(q_ref):
    heads = range(q_ref.shape[2] // HEAD)
    held = [q_ref[r].astype(jnp.float32) for r in range(q_ref.shape[0])]
    return jnp.concatenate([x[:, h * HEAD : (h + 1) * HEAD] for x in held for h in heads], axis=0)


def gather_rows_kernel(q_ref, out_ref):
    out_ref[...] = query_rows(q_ref).astype(jnp.bfloat16)


def gather_rows(queries):
    return pl.pallas_call(
        gather_rows_kernel,
        out_shape=jax.ShapeDtypeStruct((queries.size // HEAD, HEAD), jnp.bfloat16),
        compiler_params=PARAMS,
        name="gather_rows",
    )(pltpu.with_memory_space_constraint(queries, pltpu.HBM))


def layer_at(offset):
    size = lax.axis_size("y")
    return lax.rem(lax.axis_index("y") + offset + size, size)


def place_kernel(*refs):
    out_ref = refs[-1]
    blocks = [ref[...] for ref in refs[:-1]]
    for offset, block in enumerate(blocks):
        layer = layer_at(-offset)
        for d in range(out_ref.shape[0]):
            out_ref[d, layer] = block


def place(blocks, copies):
    return pl.pallas_call(
        place_kernel,
        out_shape=jax.ShapeDtypeStruct((copies, len(blocks)) + blocks[0].shape, jnp.bfloat16),
        compiler_params=PARAMS,
        name="place",
    )(*blocks)


def locate_kernel(slot_ref, length_ref, info, *, span):
    slots = length_ref.shape[0]
    cores, core = lax.axis_size("core"), lax.axis_index("core")
    first = (lax.axis_index("y") * cores + core) * slots
    start = (lax.axis_index("z") * lax.axis_size("x") + lax.axis_index("x")) * span
    for j in range(slots):
        row = jnp.int32(0)
        for r in range(slot_ref.shape[0]):
            row = jnp.where(slot_ref[r] == first + j, jnp.int32(r), row)
        group = lax.div(row, slots)
        info[j] = jnp.where(lax.rem(group, cores) == core, 0, 1)
        info[slots + j] = lax.div(group, cores)
        info[2 * slots + j] = lax.rem(row, slots)
        info[3 * slots + j] = jnp.clip(length_ref[j] - start, 0, span)


def locate(row_slot, lengths, span):
    smem = pl.BlockSpec(memory_space=pltpu.SMEM)
    return pl.pallas_call(
        functools.partial(locate_kernel, span=span),
        in_specs=[smem, smem],
        out_specs=smem,
        out_shape=jax.ShapeDtypeStruct((4 * lengths.shape[0],), jnp.int32),
        compiler_params=PARAMS,
        name="locate",
    )(row_slot, lengths)


def attend_kernel(info, *refs, heads):
    near_ref, far_ref, k_ref, v_ref, sk_ref, sv_ref, near_out, far_out = refs[:8]
    q_ref, own_top, own_acc = refs[8:]
    _, layers, numerators, _ = near_ref.shape
    halves = near_ref.shape[0] // heads
    tiles = numerators // 8
    chunk = layers * numerators
    length = k_ref.shape[0]
    slots, span, _ = sk_ref.shape
    ones = jnp.ones((length, HEAD), jnp.bfloat16)

    @pl.when(pl.program_id(0) == 0)
    def _():
        own_top[...] = jnp.full(own_top.shape, LOWEST, jnp.float32)
        own_acc[...] = jnp.zeros(own_acc.shape, jnp.float32)

    def cut(i):
        return slice(i * HEAD, (i + 1) * HEAD)

    def scored(i, side, half):
        q = (near_ref, far_ref)[side][i * halves + half].reshape(chunk, HEAD)
        return dot(q, k_ref[:, cut(i)], NT)

    items = [(i, side, half) for i in range(heads) for side in range(2) for half in range(halves)]
    scores = scored(*items[0])

    for side, ref in enumerate((near_ref, far_ref)):
        q_ref[side] = ref[...].astype(jnp.float32).reshape(q_ref.shape[1:])
    position = iota((halves * 8, span), 1)
    found = []
    for j in range(slots):
        side, layer, row, live = (info[n * slots + j] for n in range(4))
        for i in range(heads):
            at = slice(i * halves, (i + 1) * halves)
            q = q_ref[side, at, layer, row].reshape(halves * 8, HEAD).astype(jnp.bfloat16)
            own = dot(q, sk_ref[j, :, cut(i)], NT) * SCALE
            own = jnp.where(position < live, own, LOWEST)
            peak = jnp.max(own, axis=1, keepdims=True)
            peak = jnp.broadcast_to(as_bf16(peak), (halves * 8, HEAD))
            shift = jnp.concatenate([peak] * (span // HEAD), axis=1)
            weights = jnp.exp2(own - shift).astype(jnp.bfloat16)
            values = jnp.concatenate([sv_ref[j, :, cut(i)], ones[:span]], axis=1)
            found.append(((side, at, layer, row), peak, dot(weights, values, NN)))
    for at, peak, summed in found:
        own_top[at] = peak.reshape(halves, 8, HEAD)
        own_acc[at] = summed.reshape(halves, 8, 2 * HEAD)

    for number, (i, side, half) in enumerate(items):
        later = scored(*items[number + 1]) if number + 1 < len(items) else None
        peak = jnp.max(scores, axis=1, keepdims=True) * SCALE
        peak = jnp.broadcast_to(as_bf16(peak), (chunk, HEAD))
        shift = jnp.concatenate([peak] * (length // HEAD), axis=1)
        weights = jnp.exp2(scores * SCALE - shift).astype(jnp.bfloat16)
        values = jnp.concatenate([v_ref[:, cut(i)], ones], axis=1)
        summed = dot(weights, values, NN)
        own = own_top[side, i * halves + half].reshape(chunk, HEAD)
        carried = own_acc[side, i * halves + half].reshape(chunk, 2 * HEAD)
        top = jnp.maximum(peak, own)
        keep, add = jnp.exp2(peak - top), jnp.exp2(own - top)
        total = summed[:, HEAD:] * keep + carried[:, HEAD:] * add
        numerator = (summed[:, :HEAD] * keep + carried[:, :HEAD] * add).astype(jnp.bfloat16)
        results = []
        for b in range(chunk // numerators):
            low = b * numerators
            parts = [slice(low + 8 * a, low + 8 * a + 8) for a in range(tiles)]
            tail = pack([top[p] for p in parts], [total[p] for p in parts])
            results.append((numerator[low : low + numerators], tail))
        out_ref = (near_out, far_out)[side].at[i * halves + half]
        for layer, (block, tail) in enumerate(results):
            out_ref[layer, :numerators] = block
            out_ref[layer, numerators:] = tail
        scores = later


def attend(info, near, far, keys, values, suffix_keys, suffix_values, heads):
    members, layers, numerators, _ = near.shape
    halves = members // KVH
    length = keys.shape[0]
    slots, span, _ = suffix_keys.shape
    in_hbm = [
        pltpu.with_memory_space_constraint(x, pltpu.HBM)
        for x in (keys, values, suffix_keys, suffix_values)
    ]
    wide = heads * HEAD
    by_head = pl.BlockSpec((heads * halves, layers, numerators, HEAD), lambda k: (k, 0, 0, 0))
    prompt = pl.BlockSpec((length, wide), lambda k: (0, k))
    own = pl.BlockSpec((slots, span, wide), lambda k: (0, 0, k))
    rows = numerators + TAIL
    out_spec = pl.BlockSpec((heads * halves, layers, rows, HEAD), lambda k: (k, 0, 0, 0))
    out = jax.ShapeDtypeStruct((members, layers, rows, HEAD), jnp.bfloat16)
    tiled = (2, heads * halves, layers, numerators // 8, 8)
    return pl.pallas_call(
        functools.partial(attend_kernel, heads=heads),
        grid=(KVH // heads,),
        in_specs=[pl.BlockSpec(memory_space=pltpu.SMEM), by_head, by_head, prompt, prompt, own, own],
        out_specs=[out_spec, out_spec],
        out_shape=[out, out],
        scratch_shapes=[
            pltpu.VMEM(tiled + (HEAD,), jnp.float32),
            pltpu.VMEM(tiled + (HEAD,), jnp.float32),
            pltpu.VMEM(tiled + (2 * HEAD,), jnp.float32),
        ],
        compiler_params=PARAMS,
        name="attend",
    )(info, near, far, *in_hbm)


def join_parts(parts):
    numerators = parts[0][0].shape[0] - TAIL
    tiles = numerators // 8
    opened = []
    for blocks in parts:
        tails = [x[numerators:].astype(jnp.float32) for x in blocks]
        opened.append(unpack(jnp.concatenate(tails, axis=0).astype(jnp.bfloat16), tiles))
    joined = []
    for b in range(len(parts[0])):
        tops, totals, sums = [], [], []
        for blocks, (top, total) in zip(parts, opened):
            tops.append(columns(top[b * 8 : b * 8 + 8]))
            totals.append(columns(total[b * 8 : b * 8 + 8]))
            found = blocks[b][:numerators].astype(jnp.float32)
            sums.append([found[a * 8 : a * 8 + 8] for a in range(tiles)])
        rows = [
            combine([x[a] for x in tops], [x[a] for x in totals], [x[a] for x in sums])
            for a in range(tiles)
        ]
        block = jnp.concatenate([x[2] for x in rows], axis=0).astype(jnp.bfloat16)
        joined.append((block, pack([x[0] for x in rows], [x[1] for x in rows])))
    return joined


def join_cores_kernel(a_ref, b_ref, out_ref):
    members, layers, rows, _ = a_ref.shape
    for first in range(0, members, 4):
        at = [(m, y) for m in range(first, first + 4) for y in range(layers)]
        parts = [[ref[m, y] for m, y in at] for ref in (a_ref, b_ref)]
        for (m, y), (block, tail) in zip(at, join_parts(parts)):
            out_ref[m, y, : rows - TAIL] = block
            out_ref[m, y, rows - TAIL :] = tail


def join_cores(a, b):
    return pl.pallas_call(
        join_cores_kernel,
        out_shape=jax.ShapeDtypeStruct(a.shape, a.dtype),
        compiler_params=PARAMS,
        name="join_cores",
    )(a, b)


def join_plane_kernel(parts_ref, *out_refs):
    members, _, rows, _ = parts_ref.shape
    order = [layer_at(offset) for offset in range(len(out_refs))]
    parts = [[parts_ref[m, y] for y in order] for m in range(members)]
    for (block, tail), out_ref in zip(join_parts(parts), out_refs):
        out_ref[: rows - TAIL] = block
        out_ref[rows - TAIL :] = tail


def join_plane(parts):
    out = jax.ShapeDtypeStruct(parts.shape[2:], parts.dtype)
    return pl.pallas_call(
        join_plane_kernel,
        out_shape=[out] * parts.shape[1],
        compiler_params=PARAMS,
        name="join_plane",
    )(parts)


def new_kernel(q_ref, new_ref, score_ref, value_ref):
    rows, steps, width = q_ref.shape
    member = lax.axis_index("z") * lax.axis_size("x") + lax.axis_index("x")
    kv_head = member * (width // HEAD) // (H // KVH)
    at_head = pl.ds(pl.multiple_of(kv_head * HEAD, HEAD), HEAD)
    step = lax.rem(iota((8, HEAD), 0), steps)
    queries = query_rows(q_ref)
    for r in range(rows):
        for u in range(steps):
            key, value = (
                jnp.broadcast_to(new_ref[r, u, n : n + 1, at_head].astype(jnp.float32), (8, HEAD))
                for n in range(2)
            )
            score = jnp.sum(queries[r * 8 : r * 8 + 8] * key, axis=1, keepdims=True) * SCALE
            score_ref[u, r] = jnp.where(step >= u, jnp.broadcast_to(score, (8, HEAD)), LOWEST)
            value_ref[u, r] = value


def new_tokens(queries, new_kv):
    rows, steps, _ = queries.shape
    out = jax.ShapeDtypeStruct((steps, rows, 8, HEAD), jnp.float32)
    return pl.pallas_call(
        new_kernel,
        out_shape=[out, out],
        compiler_params=PARAMS,
        name="new_tokens",
    )(queries, new_kv)


def merge_kernel(*refs):
    score_ref, value_ref, out_ref = refs[-3:]
    rows, steps, width = out_ref.shape
    sources = len(refs) - 3
    numerators = refs[0].shape[0] - TAIL
    one = jnp.ones((8, HEAD), jnp.float32)
    blocks = [ref[...] for ref in refs[:sources]]
    tails = [x[numerators:].astype(jnp.float32) for x in blocks]
    opened = unpack(jnp.concatenate(tails, axis=0).astype(jnp.bfloat16), rows)
    opened = [columns(x) for x in opened]
    results = []
    for r in range(rows):
        pieces = [slice(s * 8, s * 8 + 8) for s in range(sources)]
        tops = [opened[0][r][p] for p in pieces]
        totals = [opened[1][r][p] for p in pieces]
        sums = [x[r * 8 : r * 8 + 8].astype(jnp.float32) for x in blocks]
        for u in range(steps):
            tops.append(score_ref[u, r])
            totals.append(one)
            sums.append(value_ref[u, r])
        _, total, summed = combine(tops, totals, sums)
        results.append(summed / total)
    for r, result in enumerate(results):
        for h in range(width // HEAD):
            out_ref[r, :, h * HEAD : (h + 1) * HEAD] = result[h * steps : (h + 1) * steps].astype(
                jnp.bfloat16
            )


def merge(parts, scores, values, shape):
    return pl.pallas_call(
        merge_kernel,
        out_shape=jax.ShapeDtypeStruct(shape, jnp.bfloat16),
        compiler_params=PARAMS,
        name="merge",
    )(*parts, scores, values)


PLANE = ("z", "x")


def exchange(x, axes):
    return lax.all_to_all(x, axes, split_axis=0, concat_axis=0, tiled=True)


def per_device(
    queries,
    new_kv,
    prefix_keys,
    prefix_values,
    suffix_keys,
    suffix_values,
    suffix_lengths,
    row_slot,
):
    layers = lax.axis_size("y")
    cores = lax.axis_size("core")
    members = lax.axis_size("z") * lax.axis_size("x")
    swap = [(i, (i + 1) % cores) for i in range(cores)]

    def to_layer(x, by):
        return lax.ppermute(x, "y", [(i, (i + by) % layers) for i in range(layers)])

    own = gather_rows(queries)
    blocks = place([own] + [to_layer(own, by) for by in range(1, layers)], members)
    blocks, row_slot, suffix_lengths = lax.optimization_barrier((blocks, row_slot, suffix_lengths))
    near = exchange(blocks, PLANE)
    near, info = lax.optimization_barrier(
        (near, locate(row_slot, suffix_lengths, suffix_keys.shape[1]))
    )
    far = lax.ppermute(near, "core", swap)
    near_part, far_part = attend(
        info, near, far, prefix_keys, prefix_values, suffix_keys, suffix_values, 2
    )
    joined = join_cores(near_part, lax.ppermute(far_part, "core", swap))
    joined, queries, new_kv = lax.optimization_barrier((joined, queries, new_kv))
    parts, scores, values = lax.optimization_barrier(
        (exchange(joined, PLANE), *new_tokens(queries, new_kv))
    )
    parts = join_plane(parts)
    received = [parts[0]] + [to_layer(parts[by], by) for by in range(1, layers)]
    return merge(received, scores, values, queries.shape)


def solution(mesh):
    fine = jax.sharding.Mesh(mesh.devices.reshape(4, 2, 4, 4), ("y", "core", "z", "x"))
    grp, seq = ("y", "core"), ("z", "x")
    placed = (
        P(grp, None, seq),
        P(grp, None, None, None),
        P(grp + seq, None),
        P(grp + seq, None),
        P(grp, seq, None),
        P(grp, seq, None),
        P(grp),
        P(),
    )
    return jax.shard_map(
        per_device, mesh=fine, in_specs=placed, out_specs=P(grp, None, seq), check_vma=False
    )
```

```python
import functools
import math

import jax
import jax.numpy as jnp
from jax import lax
from jax.experimental import pallas as pl
from jax.experimental.pallas import tpu as pltpu
from jax.sharding import PartitionSpec as P

H = 64
KVH = 8
HEAD = 128
LOWEST = -(2.0**100)
SCALE = HEAD ** (-0.5) * math.log2(math.e)
TAIL = 8
PARAMS = pltpu.CompilerParams(vmem_limit_bytes=32 << 20)

NT = (((1,), (1,)), ((), ()))
NN = (((1,), (0,)), ((), ()))


def dot(a, b, dims):
    return lax.dot_general(a, b, dims, preferred_element_type=jnp.float32)


def iota(shape, axis):
    return lax.broadcasted_iota(jnp.int32, shape, axis)


def as_bf16(x):
    return x.astype(jnp.bfloat16).astype(jnp.float32)


def columns(x):
    return [x[:, a * HEAD : (a + 1) * HEAD] for a in range(x.shape[1] // HEAD)]


def pack(tops, totals):
    lane = iota((TAIL, HEAD), 1)
    piece = lax.rem(lane, 32) // 8
    packed = None
    for a, (top, total) in enumerate(zip(tops, totals)):
        high = as_bf16(total)
        mixed = jnp.where(piece == 1, high, total - high)
        mixed = jnp.where(piece == 0, top, mixed)
        packed = mixed if a == 0 else jnp.where(lane // 32 == a, mixed, packed)
    return packed.astype(jnp.bfloat16)


def unpack(tails, tiles):
    shape = (HEAD, tiles * HEAD)
    start = iota(shape, 0) - 32 * (iota(shape, 1) // HEAD)
    first = (start == 0).astype(jnp.float32).astype(jnp.bfloat16)
    second = ((start == 8) | (start == 16)).astype(jnp.float32).astype(jnp.bfloat16)
    return dot(tails, first, NN), dot(tails, second, NN)


def combine(tops, totals, numerators):
    upper = functools.reduce(jnp.maximum, tops)
    factors = [jnp.exp2(top - upper) for top in tops]
    total = sum(x * f for x, f in zip(totals, factors))
    return upper, total, sum(x * f for x, f in zip(numerators, factors))


def query_rows(q_ref):
    heads = range(q_ref.shape[2] // HEAD)
    held = [q_ref[r].astype(jnp.float32) for r in range(q_ref.shape[0])]
    return jnp.concatenate([x[:, h * HEAD : (h + 1) * HEAD] for x in held for h in heads], axis=0)


def spread_kernel(q_ref, out_ref):
    block = query_rows(q_ref).astype(jnp.bfloat16)
    for d in range(out_ref.shape[0]):
        out_ref[d] = block


def spread(queries, copies):
    return pl.pallas_call(
        spread_kernel,
        out_shape=jax.ShapeDtypeStruct((copies, queries.size // HEAD, HEAD), jnp.bfloat16),
        compiler_params=PARAMS,
        name="spread",
    )(pltpu.with_memory_space_constraint(queries, pltpu.HBM))


def locate_kernel(slot_ref, length_ref, info, *, span):
    slots = length_ref.shape[0]
    cores, layers = lax.axis_size("core"), lax.axis_size("y")
    core = lax.axis_index("core")
    first = (lax.axis_index("y") * cores + core) * slots
    start = (lax.axis_index("z") * lax.axis_size("x") + lax.axis_index("x")) * span
    for j in range(slots):
        row = jnp.int32(0)
        for r in range(slot_ref.shape[0]):
            row = jnp.where(slot_ref[r] == first + j, jnp.int32(r), row)
        group = lax.div(row, slots)
        far = jnp.where(lax.rem(group, cores) == core, 0, layers)
        info[j] = lax.div(group, cores) + far
        info[slots + j] = lax.rem(row, slots)
        info[2 * slots + j] = jnp.clip(length_ref[j] - start, 0, span)


def locate(row_slot, lengths, span):
    smem = pl.BlockSpec(memory_space=pltpu.SMEM)
    return pl.pallas_call(
        functools.partial(locate_kernel, span=span),
        in_specs=[smem, smem],
        out_specs=smem,
        out_shape=jax.ShapeDtypeStruct((3 * lengths.shape[0],), jnp.int32),
        compiler_params=PARAMS,
        name="locate",
    )(row_slot, lengths)


def attend_kernel(info, near_ref, far_ref, *refs, heads):
    sources, (near_out, far_out), held = refs[:4], refs[4:6], refs[6:10]
    q_ref, own_top, own_acc, sems = refs[10:]
    k_ref, v_ref, sk_ref, sv_ref = held
    near, _, rows, _ = near_ref.shape
    _, _, halves, tiles = q_ref.shape[:4]
    numerators = tiles * 8
    chunk = near * rows
    length = k_ref.shape[1]
    _, slots, span, _ = sk_ref.shape
    ones = jnp.ones((length, HEAD), jnp.bfloat16)

    def copy(n, k):
        start = k * HEAD if isinstance(k, int) else pl.multiple_of(k * HEAD, HEAD)
        at = pl.ds(start, HEAD)
        part = sources[n].at[:, at] if n < 2 else sources[n].at[:, :, at]
        return pltpu.make_async_copy(part, held[n].at[k], sems.at[n, k])

    for k in range(KVH):
        for n in range(4):
            copy(n, k).start()

    own_top[...] = jnp.full(own_top.shape, LOWEST, jnp.float32)
    own_acc[...] = jnp.zeros(own_acc.shape, jnp.float32)
    position = iota((halves * 8, span), 1)

    def work(first):
        for i in range(heads):
            for n in range(4):
                copy(n, first + i).wait()

        def scored(i, side):
            q = (near_ref, far_ref)[side][:, first + i].reshape(chunk, HEAD)
            return dot(q, k_ref[first + i], NT)

        items = [(i, side) for i in range(heads) for side in range(2)]
        scores = scored(*items[0])

        for i in range(heads):
            for side, ref in enumerate((near_ref, far_ref)):
                x = ref[:, first + i].astype(jnp.float32)
                q_ref[side * near : (side + 1) * near, i] = x.reshape((near,) + q_ref.shape[2:])
        found = []
        for j in range(slots):
            group, row, live = info[j], info[slots + j], info[2 * slots + j]
            for i in range(heads):
                q = q_ref[group, i, :, row].reshape(halves * 8, HEAD).astype(jnp.bfloat16)
                own = dot(q, sk_ref[first + i, j], NT) * SCALE
                own = jnp.where(position < live, own, LOWEST)
                peak = jnp.max(own, axis=1, keepdims=True)
                peak = jnp.broadcast_to(as_bf16(peak), (halves * 8, HEAD))
                shift = jnp.concatenate([peak] * (span // HEAD), axis=1)
                weights = jnp.exp2(own - shift).astype(jnp.bfloat16)
                values = jnp.concatenate([sv_ref[first + i, j], ones[:span]], axis=1)
                found.append((group, i, row, peak, dot(weights, values, NN)))
        for group, i, row, peak, summed in found:
            own_top[group, i, :, row] = peak.reshape(halves, 8, HEAD)
            own_acc[group, i, :, row] = summed.reshape(halves, 8, 2 * HEAD)

        for number, (i, side) in enumerate(items):
            later = scored(*items[number + 1]) if number + 1 < len(items) else None
            peak = jnp.max(scores, axis=1, keepdims=True) * SCALE
            peak = jnp.broadcast_to(as_bf16(peak), (chunk, HEAD))
            shift = jnp.concatenate([peak] * (length // HEAD), axis=1)
            weights = jnp.exp2(scores * SCALE - shift).astype(jnp.bfloat16)
            values = jnp.concatenate([v_ref[first + i], ones], axis=1)
            summed = dot(weights, values, NN)
            at = slice(side * near, (side + 1) * near)
            own = own_top[at, i].reshape(chunk, HEAD)
            carried = own_acc[at, i].reshape(chunk, 2 * HEAD)
            top = jnp.maximum(peak, own)
            keep, add = jnp.exp2(peak - top), jnp.exp2(own - top)
            total = summed[:, HEAD:] * keep + carried[:, HEAD:] * add
            numerator = (summed[:, :HEAD] * keep + carried[:, :HEAD] * add).astype(jnp.bfloat16)
            results = []
            for b in range(chunk // numerators):
                low = b * numerators
                parts = [slice(low + 8 * a, low + 8 * a + 8) for a in range(tiles)]
                tail = pack([top[p] for p in parts], [total[p] for p in parts])
                results.append((numerator[low : low + numerators], tail))
            for b, (block, tail) in enumerate(results):
                member = (first + i) * halves + b % halves
                out_ref = (near_out, far_out)[side].at[b // halves, member]
                out_ref[:numerators] = block
                out_ref[numerators:] = tail
            scores = later

    @pl.loop(0, KVH // heads)
    def _(pair):
        work(pair * heads)


def attend(info, near, far, keys, values, suffix_keys, suffix_values, heads):
    layers, members, numerators, _ = near.shape
    halves = members // KVH
    near, far = (x.reshape(layers, KVH, halves * numerators, HEAD) for x in (near, far))
    arrays = (keys, values, suffix_keys, suffix_values)
    vmem = pl.BlockSpec(memory_space=pltpu.VMEM)
    out = jax.ShapeDtypeStruct((layers, members, numerators + TAIL, HEAD), jnp.bfloat16)
    tiled = (2 * layers, heads, halves, numerators // 8, 8)
    return pl.pallas_call(
        functools.partial(attend_kernel, heads=heads),
        in_specs=[pl.BlockSpec(memory_space=pltpu.SMEM), vmem, vmem]
        + [pl.BlockSpec(memory_space=pl.ANY)] * len(arrays),
        out_specs=[vmem, vmem],
        out_shape=[out, out],
        scratch_shapes=[pltpu.VMEM((KVH,) + x.shape[:-1] + (HEAD,), x.dtype) for x in arrays]
        + [
            pltpu.VMEM(tiled + (HEAD,), jnp.float32),
            pltpu.VMEM(tiled + (HEAD,), jnp.float32),
            pltpu.VMEM(tiled + (2 * HEAD,), jnp.float32),
            pltpu.SemaphoreType.DMA((len(arrays), KVH)),
        ],
        compiler_params=PARAMS,
        name="attend",
    )(info, near, far, *[pltpu.with_memory_space_constraint(x, pltpu.HBM) for x in arrays])


def join_parts(parts):
    numerators = parts[0][0].shape[0] - TAIL
    tiles = numerators // 8
    opened = []
    for blocks in parts:
        tails = [x[numerators:].astype(jnp.float32) for x in blocks]
        opened.append(unpack(jnp.concatenate(tails, axis=0).astype(jnp.bfloat16), tiles))
    joined = []
    for b in range(len(parts[0])):
        tops, totals, sums = [], [], []
        for blocks, (top, total) in zip(parts, opened):
            tops.append(columns(top[b * 8 : b * 8 + 8]))
            totals.append(columns(total[b * 8 : b * 8 + 8]))
            found = blocks[b][:numerators].astype(jnp.float32)
            sums.append([found[a * 8 : a * 8 + 8] for a in range(tiles)])
        rows = [
            combine([x[a] for x in tops], [x[a] for x in totals], [x[a] for x in sums])
            for a in range(tiles)
        ]
        block = jnp.concatenate([x[2] for x in rows], axis=0).astype(jnp.bfloat16)
        joined.append((block, pack([x[0] for x in rows], [x[1] for x in rows])))
    return joined


def join_cores_kernel(a_ref, b_ref, out_ref, held, sems):
    layers, members, rows, _ = a_ref.shape
    copies = [
        pltpu.make_async_copy(held.at[y], out_ref.at[y], sems.at[y]) for y in range(layers)
    ]
    for y in range(layers):
        parts = [[ref[y, m] for m in range(members)] for ref in (a_ref, b_ref)]
        for m, (block, tail) in enumerate(join_parts(parts)):
            held[y, m, : rows - TAIL] = block
            held[y, m, rows - TAIL :] = tail
        copies[y].start()
    for copy in copies:
        copy.wait()


def join_cores(a, b):
    vmem = pl.BlockSpec(memory_space=pltpu.VMEM)
    return pl.pallas_call(
        join_cores_kernel,
        in_specs=[vmem, vmem],
        out_specs=pl.BlockSpec(memory_space=pl.ANY),
        out_shape=jax.ShapeDtypeStruct(a.shape, a.dtype),
        scratch_shapes=[
            pltpu.VMEM(a.shape, a.dtype),
            pltpu.SemaphoreType.DMA((a.shape[0],)),
        ],
        compiler_params=PARAMS,
        name="join_cores",
    )(a, b)


def new_kernel(q_ref, new_ref, score_ref, value_ref):
    rows, steps, width = q_ref.shape
    member = lax.axis_index("z") * lax.axis_size("x") + lax.axis_index("x")
    kv_head = member * (width // HEAD) // (H // KVH)
    at_head = pl.ds(pl.multiple_of(kv_head * HEAD, HEAD), HEAD)
    step = lax.rem(iota((8, HEAD), 0), steps)
    queries = query_rows(q_ref)
    for r in range(rows):
        for u in range(steps):
            key, value = (
                jnp.broadcast_to(new_ref[r, u, n : n + 1, at_head].astype(jnp.float32), (8, HEAD))
                for n in range(2)
            )
            score = jnp.sum(queries[r * 8 : r * 8 + 8] * key, axis=1, keepdims=True) * SCALE
            score_ref[u, r] = jnp.where(step >= u, jnp.broadcast_to(score, (8, HEAD)), LOWEST)
            value_ref[u, r] = value


def new_tokens(queries, new_kv):
    rows, steps, _ = queries.shape
    out = jax.ShapeDtypeStruct((steps, rows, 8, HEAD), jnp.float32)
    return pl.pallas_call(
        new_kernel,
        out_shape=[out, out],
        compiler_params=PARAMS,
        name="new_tokens",
    )(queries, new_kv)


def merge_kernel(parts_ref, score_ref, value_ref, out_ref):
    rows, steps, width = out_ref.shape
    sources, size, _ = parts_ref.shape
    numerators = size - TAIL
    one = jnp.ones((8, HEAD), jnp.float32)
    blocks = [parts_ref[s] for s in range(sources)]
    tails = [x[numerators:].astype(jnp.float32) for x in blocks]
    opened = unpack(jnp.concatenate(tails, axis=0).astype(jnp.bfloat16), rows)
    opened = [columns(x) for x in opened]
    results = []
    for r in range(rows):
        pieces = [slice(s * 8, s * 8 + 8) for s in range(sources)]
        tops = [opened[0][r][p] for p in pieces]
        totals = [opened[1][r][p] for p in pieces]
        sums = [x[r * 8 : r * 8 + 8].astype(jnp.float32) for x in blocks]
        for u in range(steps):
            tops.append(score_ref[u, r])
            totals.append(one)
            sums.append(value_ref[u, r])
        _, total, summed = combine(tops, totals, sums)
        results.append(summed / total)
    for r, result in enumerate(results):
        for h in range(width // HEAD):
            out_ref[r, :, h * HEAD : (h + 1) * HEAD] = result[h * steps : (h + 1) * steps].astype(
                jnp.bfloat16
            )


def merge(parts, scores, values, shape):
    return pl.pallas_call(
        merge_kernel,
        out_shape=jax.ShapeDtypeStruct(shape, jnp.bfloat16),
        compiler_params=PARAMS,
        name="merge",
    )(parts, scores, values)


CHIPS = ("y", "z", "x")


def exchange(x, axes):
    return lax.all_to_all(x, axes, split_axis=0, concat_axis=0, tiled=True)


def per_device(
    queries,
    new_kv,
    prefix_keys,
    prefix_values,
    suffix_keys,
    suffix_values,
    suffix_lengths,
    row_slot,
):
    layers = lax.axis_size("y")
    cores = lax.axis_size("core")
    members = lax.axis_size("z") * lax.axis_size("x")
    chips = layers * members
    swap = [(i, (i + 1) % cores) for i in range(cores)]

    blocks, row_slot, suffix_lengths = lax.optimization_barrier(
        (spread(queries, chips), row_slot, suffix_lengths)
    )
    near = exchange(blocks, CHIPS)
    near, info = lax.optimization_barrier(
        (near, locate(row_slot, suffix_lengths, suffix_keys.shape[1]))
    )
    near = near.reshape((layers, members) + near.shape[1:])
    far = lax.ppermute(near, "core", swap)
    near_part, far_part = attend(
        info, near, far, prefix_keys, prefix_values, suffix_keys, suffix_values, 2
    )
    joined = join_cores(near_part, lax.ppermute(far_part, "core", swap))
    joined, queries, new_kv = lax.optimization_barrier((joined, queries, new_kv))
    received = exchange(joined.reshape((chips,) + joined.shape[2:]), CHIPS)
    scores, values = new_tokens(queries, new_kv)
    return merge(received, scores, values, queries.shape)


def solution(mesh):
    fine = jax.sharding.Mesh(mesh.devices.reshape(4, 2, 4, 4), ("y", "core", "z", "x"))
    grp, seq = ("y", "core"), ("z", "x")
    placed = (
        P(grp, None, seq),
        P(grp, None, None, None),
        P(grp + seq, None),
        P(grp + seq, None),
        P(grp, seq, None),
        P(grp, seq, None),
        P(grp),
        P(),
    )
    return jax.shard_map(
        per_device, mesh=fine, in_specs=placed, out_specs=P(grp, None, seq), check_vma=False
    )
```

```python
import functools
import math

import jax
import jax.numpy as jnp
from jax import lax
from jax.experimental import pallas as pl
from jax.experimental.pallas import tpu as pltpu
from jax.sharding import PartitionSpec as P

H = 64
KVH = 8
HEAD = 128
LOWEST = -(2.0**100)
SCALE = HEAD ** (-0.5) * math.log2(math.e)
TAIL = 8
PARAMS = pltpu.CompilerParams(vmem_limit_bytes=32 << 20)

NT = (((1,), (1,)), ((), ()))
NN = (((1,), (0,)), ((), ()))


def dot(a, b, dims):
    return lax.dot_general(a, b, dims, preferred_element_type=jnp.float32)


def iota(shape, axis):
    return lax.broadcasted_iota(jnp.int32, shape, axis)


def as_bf16(x):
    return x.astype(jnp.bfloat16).astype(jnp.float32)


def columns(x):
    return [x[:, a * HEAD : (a + 1) * HEAD] for a in range(x.shape[1] // HEAD)]


def pack(tops, totals):
    lane = iota((TAIL, HEAD), 1)
    piece = lax.rem(lane, 32) // 8
    packed = None
    for a, (top, total) in enumerate(zip(tops, totals)):
        high = as_bf16(total)
        mixed = jnp.where(piece == 1, high, total - high)
        mixed = jnp.where(piece == 0, top, mixed)
        packed = mixed if a == 0 else jnp.where(lane // 32 == a, mixed, packed)
    return packed.astype(jnp.bfloat16)


def unpack(tails, tiles):
    shape = (HEAD, tiles * HEAD)
    start = iota(shape, 0) - 32 * (iota(shape, 1) // HEAD)
    first = (start == 0).astype(jnp.float32).astype(jnp.bfloat16)
    second = ((start == 8) | (start == 16)).astype(jnp.float32).astype(jnp.bfloat16)
    return dot(tails, first, NN), dot(tails, second, NN)


def combine(tops, totals, numerators):
    upper = functools.reduce(jnp.maximum, tops)
    factors = [jnp.exp2(top - upper) for top in tops]
    total = sum(x * f for x, f in zip(totals, factors))
    return upper, total, sum(x * f for x, f in zip(numerators, factors))


def query_rows(q_ref):
    heads = range(q_ref.shape[2] // HEAD)
    held = [q_ref[r].astype(jnp.float32) for r in range(q_ref.shape[0])]
    return jnp.concatenate([x[:, h * HEAD : (h + 1) * HEAD] for x in held for h in heads], axis=0)


def spread_kernel(q_ref, out_ref):
    block = query_rows(q_ref).astype(jnp.bfloat16)
    for d in range(out_ref.shape[0]):
        out_ref[d] = block


def spread(queries, copies):
    return pl.pallas_call(
        spread_kernel,
        out_shape=jax.ShapeDtypeStruct((copies, queries.size // HEAD, HEAD), jnp.bfloat16),
        compiler_params=PARAMS,
        name="spread",
    )(pltpu.with_memory_space_constraint(queries, pltpu.HBM))


def locate_kernel(slot_ref, *refs, span):
    lengths, info = refs[:-1], refs[-1]
    slots = lengths[0].shape[0]
    cores, layers = lax.axis_size("core"), lax.axis_size("y")
    core = lax.axis_index("core")
    start = (lax.axis_index("z") * lax.axis_size("x") + lax.axis_index("x")) * span
    total = slots * len(lengths)
    for side, length_ref in enumerate(lengths):
        owner = lax.rem(core + side, cores)
        first = (lax.axis_index("y") * cores + owner) * slots
        for j in range(slots):
            row = jnp.int32(0)
            for r in range(slot_ref.shape[0]):
                row = jnp.where(slot_ref[r] == first + j, jnp.int32(r), row)
            group = lax.div(row, slots)
            served = lax.rem(group, cores) == core
            at = side * slots + j
            info[at] = jnp.where(served, lax.div(group, cores), layers)
            info[total + at] = lax.rem(row, slots)
            info[2 * total + at] = jnp.clip(length_ref[j] - start, 0, span)


def locate(row_slot, lengths, span):
    smem = pl.BlockSpec(memory_space=pltpu.SMEM)
    total = sum(x.shape[0] for x in lengths)
    return pl.pallas_call(
        functools.partial(locate_kernel, span=span),
        in_specs=[smem] * (1 + len(lengths)),
        out_specs=smem,
        out_shape=jax.ShapeDtypeStruct((3 * total,), jnp.int32),
        compiler_params=PARAMS,
        name="locate",
    )(row_slot, *lengths)


def attend_kernel(info, near_ref, *refs, sides, heads, chunk):
    count = 4 * sides
    sources, out_ref, held = refs[:count], refs[count], refs[count + 1 : 2 * count + 1]
    block, q_ref, own_top, own_acc, sems, out_sems = refs[2 * count + 1 :]
    layers, _, rows, _ = near_ref.shape
    _, _, halves, tiles = q_ref.shape[:4]
    numerators = tiles * 8
    per_chunk = chunk // rows
    wide = heads * HEAD
    length = sources[0].shape[0]
    slots, span, _ = sources[2].shape
    ones = jnp.ones((length, HEAD), jnp.bfloat16)
    pairs = KVH // heads

    def copy(n, pair):
        start = pair * wide if isinstance(pair, int) else pl.multiple_of(pair * wide, wide)
        at = pl.ds(start, wide)
        part = sources[n].at[:, at] if n % 4 < 2 else sources[n].at[:, :, at]
        return pltpu.make_async_copy(part, held[n].at[pair], sems.at[n, pair])

    def send(pair):
        at = pl.ds(pair * heads * halves, heads * halves)
        return pltpu.make_async_copy(block.at[:, at], out_ref.at[:, at], out_sems.at[pair])

    for pair in range(pairs):
        for n in range(count):
            copy(n, pair).start()

    own_top[...] = jnp.full(own_top.shape, LOWEST, jnp.float32)
    own_acc[...] = jnp.zeros(own_acc.shape, jnp.float32)
    position = iota((halves * 8, span), 1)

    def cut(i):
        return slice(i * HEAD, (i + 1) * HEAD)

    @pl.loop(0, pairs)
    def _(pair):
        for n in range(count):
            copy(n, pair).wait()
        first = pair * heads

        def scored(i, c):
            at = slice(c * per_chunk, (c + 1) * per_chunk)
            q = near_ref[at, first + i].reshape(chunk, HEAD)
            return [dot(q, held[4 * side][pair, :, cut(i)], NT) for side in range(sides)]

        items = [(i, c) for i in range(heads) for c in range(layers // per_chunk)]
        scores = scored(*items[0])

        for i in range(heads):
            x = near_ref[:, first + i].astype(jnp.float32)
            q_ref[:, i] = x.reshape((layers,) + q_ref.shape[2:])
        found = []
        total = sides * slots
        for j in range(total):
            layer, row, live = info[j], info[total + j], info[2 * total + j]
            sk_ref, sv_ref = held[4 * (j // slots) + 2 : 4 * (j // slots) + 4]
            for i in range(heads):
                q = q_ref[jnp.minimum(layer, layers - 1), i, :, row]
                q = q.reshape(halves * 8, HEAD).astype(jnp.bfloat16)
                own = dot(q, sk_ref[pair, j % slots, :, cut(i)], NT) * SCALE
                own = jnp.where(position < live, own, LOWEST)
                peak = jnp.max(own, axis=1, keepdims=True)
                peak = jnp.broadcast_to(as_bf16(peak), (halves * 8, HEAD))
                shift = jnp.concatenate([peak] * (span // HEAD), axis=1)
                weights = jnp.exp2(own - shift).astype(jnp.bfloat16)
                values = sv_ref[pair, j % slots, :, cut(i)]
                values = jnp.concatenate([values, ones[:span]], axis=1)
                found.append((layer, i, row, peak, dot(weights, values, NN)))
        for layer, i, row, peak, summed in found:
            own_top[layer, i, :, row] = peak.reshape(halves, 8, HEAD)
            own_acc[layer, i, :, row] = summed.reshape(halves, 8, 2 * HEAD)

        for number, (i, c) in enumerate(items):
            later = scored(*items[number + 1]) if number + 1 < len(items) else None
            peak = functools.reduce(jnp.maximum, [jnp.max(x, axis=1, keepdims=True) for x in scores])
            peak = jnp.broadcast_to(as_bf16(peak * SCALE), (chunk, HEAD))
            shift = jnp.concatenate([peak] * (length // HEAD), axis=1)
            summed = None
            for side, x in enumerate(scores):
                weights = jnp.exp2(x * SCALE - shift).astype(jnp.bfloat16)
                values = held[4 * side + 1][pair, :, cut(i)]
                part = dot(weights, jnp.concatenate([values, ones], axis=1), NN)
                summed = part if summed is None else summed + part
            at = slice(c * per_chunk, (c + 1) * per_chunk)
            own = own_top[at, i].reshape(chunk, HEAD)
            carried = own_acc[at, i].reshape(chunk, 2 * HEAD)
            top = jnp.maximum(peak, own)
            keep, add = jnp.exp2(peak - top), jnp.exp2(own - top)
            sums = summed[:, HEAD:] * keep + carried[:, HEAD:] * add
            numerator = (summed[:, :HEAD] * keep + carried[:, :HEAD] * add).astype(jnp.bfloat16)
            results = []
            for b in range(chunk // numerators):
                low = b * numerators
                parts = [slice(low + 8 * a, low + 8 * a + 8) for a in range(tiles)]
                tail = pack([top[p] for p in parts], [sums[p] for p in parts])
                results.append((numerator[low : low + numerators], tail))
            for b, (found_block, tail) in enumerate(results):
                to = block.at[c * per_chunk + b // halves, (first + i) * halves + b % halves]
                to[:numerators] = found_block
                to[numerators:] = tail
            scores = later
        send(pair).start()

    for pair in range(pairs):
        send(pair).wait()


def attend(info, near, caches, heads, chunk):
    layers, members, numerators, _ = near.shape
    halves = members // KVH
    near = near.reshape(layers, KVH, halves * numerators, HEAD)
    arrays = [x for cache in caches for x in cache]
    out = jax.ShapeDtypeStruct((layers, members, numerators + TAIL, HEAD), jnp.bfloat16)
    tiled = (heads, halves, numerators // 8, 8)
    anywhere = pl.BlockSpec(memory_space=pl.ANY)
    pairs = KVH // heads
    return pl.pallas_call(
        functools.partial(attend_kernel, sides=len(caches), heads=heads, chunk=chunk),
        in_specs=[
            pl.BlockSpec(memory_space=pltpu.SMEM),
            pl.BlockSpec(memory_space=pltpu.VMEM),
        ]
        + [anywhere] * len(arrays),
        out_specs=anywhere,
        out_shape=out,
        scratch_shapes=[
            pltpu.VMEM((pairs,) + x.shape[:-1] + (heads * HEAD,), x.dtype) for x in arrays
        ]
        + [
            pltpu.VMEM(out.shape, out.dtype),
            pltpu.VMEM((layers,) + tiled + (HEAD,), jnp.float32),
            pltpu.VMEM((layers + 1,) + tiled + (HEAD,), jnp.float32),
            pltpu.VMEM((layers + 1,) + tiled + (2 * HEAD,), jnp.float32),
            pltpu.SemaphoreType.DMA((len(arrays), pairs)),
            pltpu.SemaphoreType.DMA((pairs,)),
        ],
        compiler_params=pltpu.CompilerParams(vmem_limit_bytes=48 << 20),
        name="attend",
    )(info, near, *arrays)


def new_kernel(q_ref, new_ref, score_ref, value_ref):
    rows, steps, width = q_ref.shape
    member = lax.axis_index("z") * lax.axis_size("x") + lax.axis_index("x")
    kv_head = member * (width // HEAD) // (H // KVH)
    at_head = pl.ds(pl.multiple_of(kv_head * HEAD, HEAD), HEAD)
    step = lax.rem(iota((8, HEAD), 0), steps)
    queries = query_rows(q_ref)
    for r in range(rows):
        for u in range(steps):
            key, value = (
                jnp.broadcast_to(new_ref[r, u, n : n + 1, at_head].astype(jnp.float32), (8, HEAD))
                for n in range(2)
            )
            score = jnp.sum(queries[r * 8 : r * 8 + 8] * key, axis=1, keepdims=True) * SCALE
            score_ref[u, r] = jnp.where(step >= u, jnp.broadcast_to(score, (8, HEAD)), LOWEST)
            value_ref[u, r] = value


def new_tokens(queries, new_kv):
    rows, steps, _ = queries.shape
    out = jax.ShapeDtypeStruct((steps, rows, 8, HEAD), jnp.float32)
    return pl.pallas_call(
        new_kernel,
        out_shape=[out, out],
        compiler_params=PARAMS,
        name="new_tokens",
    )(queries, new_kv)


def merge_kernel(parts_ref, score_ref, value_ref, out_ref):
    rows, steps, width = out_ref.shape
    sources, size, _ = parts_ref.shape
    numerators = size - TAIL
    one = jnp.ones((8, HEAD), jnp.float32)
    blocks = [parts_ref[s] for s in range(sources)]
    tails = [x[numerators:].astype(jnp.float32) for x in blocks]
    opened = unpack(jnp.concatenate(tails, axis=0).astype(jnp.bfloat16), rows)
    opened = [columns(x) for x in opened]
    results = []
    for r in range(rows):
        pieces = [slice(s * 8, s * 8 + 8) for s in range(sources)]
        tops = [opened[0][r][p] for p in pieces]
        totals = [opened[1][r][p] for p in pieces]
        sums = [x[r * 8 : r * 8 + 8].astype(jnp.float32) for x in blocks]
        for u in range(steps):
            tops.append(score_ref[u, r])
            totals.append(one)
            sums.append(value_ref[u, r])
        _, total, summed = combine(tops, totals, sums)
        results.append(summed / total)
    for r, result in enumerate(results):
        for h in range(width // HEAD):
            out_ref[r, :, h * HEAD : (h + 1) * HEAD] = result[h * steps : (h + 1) * steps].astype(
                jnp.bfloat16
            )


def merge(parts, scores, values, shape):
    return pl.pallas_call(
        merge_kernel,
        out_shape=jax.ShapeDtypeStruct(shape, jnp.bfloat16),
        compiler_params=PARAMS,
        name="merge",
    )(parts, scores, values)


CHIPS = ("y", "z", "x")


def exchange(x, axes):
    return lax.all_to_all(x, axes, split_axis=0, concat_axis=0, tiled=True)


def per_device(
    queries,
    new_kv,
    prefix_keys,
    prefix_values,
    suffix_keys,
    suffix_values,
    suffix_lengths,
    row_slot,
):
    layers = lax.axis_size("y")
    cores = lax.axis_size("core")
    members = lax.axis_size("z") * lax.axis_size("x")
    chips = layers * members
    swap = [(i, (i + 1) % cores) for i in range(cores)]

    own = (prefix_keys, prefix_values, suffix_keys, suffix_values)
    far = tuple(lax.ppermute(x, "core", swap) for x in own)
    own = tuple(pltpu.with_memory_space_constraint(x, pltpu.HBM) for x in own)
    far_lengths = lax.ppermute(suffix_lengths, "core", swap)

    blocks, row_slot = lax.optimization_barrier((spread(queries, chips), row_slot))
    near = exchange(blocks, CHIPS)
    info = locate(row_slot, (suffix_lengths, far_lengths), suffix_keys.shape[1])
    near, info = lax.optimization_barrier((near, info))
    near = near.reshape((layers, members) + near.shape[1:])
    parts = attend(info, near, (own, far), 2, 128)
    parts, queries, new_kv = lax.optimization_barrier((parts, queries, new_kv))
    received = exchange(parts.reshape((chips,) + parts.shape[2:]), CHIPS)
    scores, values = new_tokens(queries, new_kv)
    return merge(received, scores, values, queries.shape)


def solution(mesh):
    fine = jax.sharding.Mesh(mesh.devices.reshape(4, 2, 4, 4), ("y", "core", "z", "x"))
    grp, seq = ("y", "core"), ("z", "x")
    placed = (
        P(grp, None, seq),
        P(grp, None, None, None),
        P(grp + seq, None),
        P(grp + seq, None),
        P(grp, seq, None),
        P(grp, seq, None),
        P(grp),
        P(),
    )
    return jax.shard_map(
        per_device, mesh=fine, in_specs=placed, out_specs=P(grp, None, seq), check_vma=False
    )
```

```python
import functools
import math

import jax
import jax.numpy as jnp
from jax import lax
from jax.experimental import pallas as pl
from jax.experimental.pallas import tpu as pltpu
from jax.sharding import PartitionSpec as P

H = 64
KVH = 8
HEAD = 128
LOWEST = -(2.0**100)
SCALE = HEAD ** (-0.5) * math.log2(math.e)
TAIL = 8
PARAMS = pltpu.CompilerParams(vmem_limit_bytes=32 << 20)

NT = (((1,), (1,)), ((), ()))
NN = (((1,), (0,)), ((), ()))


def dot(a, b, dims):
    return lax.dot_general(a, b, dims, preferred_element_type=jnp.float32)


def iota(shape, axis):
    return lax.broadcasted_iota(jnp.int32, shape, axis)


def as_bf16(x):
    return x.astype(jnp.bfloat16).astype(jnp.float32)


def columns(x):
    return [x[:, a * HEAD : (a + 1) * HEAD] for a in range(x.shape[1] // HEAD)]


def pack(tops, totals):
    lane = iota((TAIL, HEAD), 1)
    piece = lax.rem(lane, 32) // 8
    packed = None
    for a, (top, total) in enumerate(zip(tops, totals)):
        high = as_bf16(total)
        mixed = jnp.where(piece == 1, high, total - high)
        mixed = jnp.where(piece == 0, top, mixed)
        packed = mixed if a == 0 else jnp.where(lane // 32 == a, mixed, packed)
    return packed.astype(jnp.bfloat16)


def unpack(tails, tiles):
    shape = (HEAD, tiles * HEAD)
    start = iota(shape, 0) - 32 * (iota(shape, 1) // HEAD)
    first = (start == 0).astype(jnp.float32).astype(jnp.bfloat16)
    second = ((start == 8) | (start == 16)).astype(jnp.float32).astype(jnp.bfloat16)
    return dot(tails, first, NN), dot(tails, second, NN)


def combine(tops, totals, numerators):
    upper = functools.reduce(jnp.maximum, tops)
    factors = [jnp.exp2(top - upper) for top in tops]
    total = sum(x * f for x, f in zip(totals, factors))
    return upper, total, sum(x * f for x, f in zip(numerators, factors))


def query_rows(q_ref):
    heads = range(q_ref.shape[2] // HEAD)
    held = [q_ref[r].astype(jnp.float32) for r in range(q_ref.shape[0])]
    return jnp.concatenate([x[:, h * HEAD : (h + 1) * HEAD] for x in held for h in heads], axis=0)


def spread_kernel(q_ref, out_ref):
    block = query_rows(q_ref).astype(jnp.bfloat16)
    for d in range(out_ref.shape[0]):
        out_ref[d] = block


def spread(queries, copies):
    return pl.pallas_call(
        spread_kernel,
        out_shape=jax.ShapeDtypeStruct((copies, queries.size // HEAD, HEAD), jnp.bfloat16),
        compiler_params=PARAMS,
        name="spread",
    )(pltpu.with_memory_space_constraint(queries, pltpu.HBM))


def locate_kernel(slot_ref, *refs, span):
    lengths, info = refs[:-1], refs[-1]
    slots = lengths[0].shape[0]
    cores, layers = lax.axis_size("core"), lax.axis_size("y")
    core = lax.axis_index("core")
    start = (lax.axis_index("z") * lax.axis_size("x") + lax.axis_index("x")) * span
    total = slots * len(lengths)
    for side, length_ref in enumerate(lengths):
        owner = lax.rem(core + side, cores)
        first = (lax.axis_index("y") * cores + owner) * slots
        for j in range(slots):
            row = jnp.int32(0)
            for r in range(slot_ref.shape[0]):
                row = jnp.where(slot_ref[r] == first + j, jnp.int32(r), row)
            group = lax.div(row, slots)
            served = lax.rem(group, cores) == core
            at = side * slots + j
            info[at] = jnp.where(served, lax.div(group, cores), layers)
            info[total + at] = lax.rem(row, slots)
            info[2 * total + at] = jnp.clip(length_ref[j] - start, 0, span)


def locate(row_slot, lengths, span):
    smem = pl.BlockSpec(memory_space=pltpu.SMEM)
    total = sum(x.shape[0] for x in lengths)
    return pl.pallas_call(
        functools.partial(locate_kernel, span=span),
        in_specs=[smem] * (1 + len(lengths)),
        out_specs=smem,
        out_shape=jax.ShapeDtypeStruct((3 * total,), jnp.int32),
        compiler_params=PARAMS,
        name="locate",
    )(row_slot, *lengths)


def attend_kernel(info, near_ref, *refs, sides, heads):
    count = 4 * sides
    sources, out_ref, held = refs[:count], refs[count], refs[count + 1 : 2 * count + 1]
    block, q_ref, own_top, own_acc, sems, out_sems = refs[2 * count + 1 :]
    layers, _, rows, _ = near_ref.shape
    _, _, halves, tiles = q_ref.shape[:4]
    numerators = tiles * 8
    chunk = layers * rows
    wide = heads * HEAD
    length = sources[0].shape[0]
    slots, span, _ = sources[2].shape
    ones = jnp.ones((length, HEAD), jnp.bfloat16)
    pairs = KVH // heads

    def copy(n, pair):
        start = pair * wide if isinstance(pair, int) else pl.multiple_of(pair * wide, wide)
        at = pl.ds(start, wide)
        part = sources[n].at[:, at] if n % 4 < 2 else sources[n].at[:, :, at]
        return pltpu.make_async_copy(part, held[n].at[pair], sems.at[n, pair])

    def send(pair):
        at = pl.ds(pair * heads * halves, heads * halves)
        return pltpu.make_async_copy(block.at[:, at], out_ref.at[:, at], out_sems.at[pair])

    for pair in range(pairs):
        for n in range(count):
            copy(n, pair).start()

    own_top[...] = jnp.full(own_top.shape, LOWEST, jnp.float32)
    own_acc[...] = jnp.zeros(own_acc.shape, jnp.float32)
    position = iota((heads * halves * 8, span), 1)

    def cut(i):
        return slice(i * HEAD, (i + 1) * HEAD)

    @pl.loop(0, pairs)
    def _(pair):
        first = pair * heads

        def wait(kind):
            for side in range(sides):
                copy(4 * side + kind, pair).wait()

        def scored(i):
            q = near_ref[:, first + i].reshape(chunk, HEAD)
            return [dot(q, held[4 * side][pair, :, cut(i)], NT) for side in range(sides)]

        def weigh(i, scores):
            peak = functools.reduce(jnp.maximum, [jnp.max(x, axis=1, keepdims=True) for x in scores])
            peak = jnp.broadcast_to(as_bf16(peak * SCALE), (chunk, HEAD))
            shift = jnp.concatenate([peak] * (length // HEAD), axis=1)
            summed = None
            for side, x in enumerate(scores):
                weights = jnp.exp2(x * SCALE - shift).astype(jnp.bfloat16)
                values = held[4 * side + 1][pair, :, cut(i)]
                part = dot(weights, jnp.concatenate([values, ones], axis=1), NN)
                summed = part if summed is None else summed + part
            return peak, summed

        def finish(i, peak, summed):
            own = own_top[:layers, i].reshape(chunk, HEAD)
            carried = own_acc[:layers, i].reshape(chunk, 2 * HEAD)
            top = jnp.maximum(peak, own)
            keep, add = jnp.exp2(peak - top), jnp.exp2(own - top)
            sums = summed[:, HEAD:] * keep + carried[:, HEAD:] * add
            numerator = (summed[:, :HEAD] * keep + carried[:, :HEAD] * add).astype(jnp.bfloat16)
            results = []
            for b in range(chunk // numerators):
                low = b * numerators
                parts = [slice(low + 8 * a, low + 8 * a + 8) for a in range(tiles)]
                tail = pack([top[p] for p in parts], [sums[p] for p in parts])
                results.append((numerator[low : low + numerators], tail))
            for b, (found_block, tail) in enumerate(results):
                to = block.at[b // halves, (first + i) * halves + b % halves]
                to[:numerators] = found_block
                to[numerators:] = tail

        def continuations():
            for i in range(heads):
                x = near_ref[:, first + i].astype(jnp.float32)
                q_ref[:, i] = x.reshape((layers,) + q_ref.shape[2:])
            total = sides * slots
            size = halves * 8
            none = jnp.zeros((size, HEAD), jnp.float32)
            found = []
            for j in range(total):
                layer, row, live = info[j], info[total + j], info[2 * total + j]
                sk_ref, sv_ref = held[4 * (j // slots) + 2 : 4 * (j // slots) + 4]
                wide_rows = []
                for i in range(heads):
                    q = q_ref[jnp.minimum(layer, layers - 1), i, :, row].reshape(size, HEAD)
                    wide_rows.append(
                        jnp.concatenate([q if n == i else none for n in range(heads)], axis=1)
                    )
                q = jnp.concatenate(wide_rows, axis=0).astype(jnp.bfloat16)
                own = dot(q, sk_ref[pair, j % slots], NT) * SCALE
                own = jnp.where(position < live, own, LOWEST)
                peak = jnp.max(own, axis=1, keepdims=True)
                peak = jnp.broadcast_to(as_bf16(peak), (heads * size, HEAD))
                shift = jnp.concatenate([peak] * (span // HEAD), axis=1)
                weights = jnp.exp2(own - shift)
                sums = jnp.sum(weights, axis=1, keepdims=True)
                sums = jnp.broadcast_to(sums, (heads * size, HEAD))
                summed = dot(weights.astype(jnp.bfloat16), sv_ref[pair, j % slots], NN)
                found.append((layer, row, peak, sums, summed))
            for layer, row, peak, sums, summed in found:
                for i in range(heads):
                    at = slice(i * size, (i + 1) * size)
                    state = jnp.concatenate([summed[at, cut(i)], sums[at]], axis=1)
                    own_top[layer, i, :, row] = peak[at].reshape(halves, 8, HEAD)
                    own_acc[layer, i, :, row] = state.reshape(halves, 8, 2 * HEAD)

        wait(0)
        scores = scored(0)
        wait(1)
        wait(2)
        wait(3)
        for i in range(heads):
            later = scored(i + 1) if i + 1 < heads else None
            peak, summed = weigh(i, scores)
            if i == 0:
                continuations()
            finish(i, peak, summed)
            scores = later
        send(pair).start()

    for pair in range(pairs):
        send(pair).wait()


def attend(info, near, caches, heads):
    layers, members, numerators, _ = near.shape
    halves = members // KVH
    near = near.reshape(layers, KVH, halves * numerators, HEAD)
    arrays = [x for cache in caches for x in cache]
    out = jax.ShapeDtypeStruct((layers, members, numerators + TAIL, HEAD), jnp.bfloat16)
    tiled = (heads, halves, numerators // 8, 8)
    anywhere = pl.BlockSpec(memory_space=pl.ANY)
    pairs = KVH // heads
    return pl.pallas_call(
        functools.partial(attend_kernel, sides=len(caches), heads=heads),
        in_specs=[
            pl.BlockSpec(memory_space=pltpu.SMEM),
            pl.BlockSpec(memory_space=pltpu.VMEM),
        ]
        + [anywhere] * len(arrays),
        out_specs=anywhere,
        out_shape=out,
        scratch_shapes=[
            pltpu.VMEM((pairs,) + x.shape[:-1] + (heads * HEAD,), x.dtype) for x in arrays
        ]
        + [
            pltpu.VMEM(out.shape, out.dtype),
            pltpu.VMEM((layers,) + tiled + (HEAD,), jnp.float32),
            pltpu.VMEM((layers + 1,) + tiled + (HEAD,), jnp.float32),
            pltpu.VMEM((layers + 1,) + tiled + (2 * HEAD,), jnp.float32),
            pltpu.SemaphoreType.DMA((len(arrays), pairs)),
            pltpu.SemaphoreType.DMA((pairs,)),
        ],
        compiler_params=pltpu.CompilerParams(vmem_limit_bytes=48 << 20),
        name="attend",
    )(info, near, *arrays)


def new_kernel(q_ref, new_ref, score_ref, value_ref):
    rows, steps, width = q_ref.shape
    member = lax.axis_index("z") * lax.axis_size("x") + lax.axis_index("x")
    kv_head = member * (width // HEAD) // (H // KVH)
    at_head = pl.ds(pl.multiple_of(kv_head * HEAD, HEAD), HEAD)
    step = lax.rem(iota((8, HEAD), 0), steps)
    queries = query_rows(q_ref)
    for r in range(rows):
        for u in range(steps):
            key, value = (
                jnp.broadcast_to(new_ref[r, u, n : n + 1, at_head].astype(jnp.float32), (8, HEAD))
                for n in range(2)
            )
            score = jnp.sum(queries[r * 8 : r * 8 + 8] * key, axis=1, keepdims=True) * SCALE
            score_ref[u, r] = jnp.where(step >= u, jnp.broadcast_to(score, (8, HEAD)), LOWEST)
            value_ref[u, r] = value


def new_tokens(queries, new_kv):
    rows, steps, _ = queries.shape
    out = jax.ShapeDtypeStruct((steps, rows, 8, HEAD), jnp.float32)
    return pl.pallas_call(
        new_kernel,
        out_shape=[out, out],
        compiler_params=PARAMS,
        name="new_tokens",
    )(queries, new_kv)


def merge_kernel(parts_ref, score_ref, value_ref, out_ref):
    rows, steps, width = out_ref.shape
    sources, size, _ = parts_ref.shape
    numerators = size - TAIL
    one = jnp.ones((8, HEAD), jnp.float32)
    blocks = [parts_ref[s] for s in range(sources)]
    tails = [x[numerators:].astype(jnp.float32) for x in blocks]
    opened = unpack(jnp.concatenate(tails, axis=0).astype(jnp.bfloat16), rows)
    opened = [columns(x) for x in opened]
    results = []
    for r in range(rows):
        pieces = [slice(s * 8, s * 8 + 8) for s in range(sources)]
        tops = [opened[0][r][p] for p in pieces]
        totals = [opened[1][r][p] for p in pieces]
        sums = [x[r * 8 : r * 8 + 8].astype(jnp.float32) for x in blocks]
        for u in range(steps):
            tops.append(score_ref[u, r])
            totals.append(one)
            sums.append(value_ref[u, r])
        _, total, summed = combine(tops, totals, sums)
        results.append(summed / total)
    for r, result in enumerate(results):
        for h in range(width // HEAD):
            out_ref[r, :, h * HEAD : (h + 1) * HEAD] = result[h * steps : (h + 1) * steps].astype(
                jnp.bfloat16
            )


def merge(parts, scores, values, shape):
    return pl.pallas_call(
        merge_kernel,
        out_shape=jax.ShapeDtypeStruct(shape, jnp.bfloat16),
        compiler_params=PARAMS,
        name="merge",
    )(parts, scores, values)


CHIPS = ("y", "z", "x")


def exchange(x, axes):
    return lax.all_to_all(x, axes, split_axis=0, concat_axis=0, tiled=True)


def per_device(
    queries,
    new_kv,
    prefix_keys,
    prefix_values,
    suffix_keys,
    suffix_values,
    suffix_lengths,
    row_slot,
):
    layers = lax.axis_size("y")
    cores = lax.axis_size("core")
    members = lax.axis_size("z") * lax.axis_size("x")
    chips = layers * members
    swap = [(i, (i + 1) % cores) for i in range(cores)]

    own = (prefix_keys, prefix_values, suffix_keys, suffix_values)
    far = tuple(lax.ppermute(x, "core", swap) for x in own)
    own = tuple(pltpu.with_memory_space_constraint(x, pltpu.HBM) for x in own)
    far_lengths = lax.ppermute(suffix_lengths, "core", swap)

    blocks, row_slot = lax.optimization_barrier((spread(queries, chips), row_slot))
    near = exchange(blocks, CHIPS)
    info = locate(row_slot, (suffix_lengths, far_lengths), suffix_keys.shape[1])
    near, info = lax.optimization_barrier((near, info))
    near = near.reshape((layers, members) + near.shape[1:])
    parts = attend(info, near, (own, far), 2)
    parts, queries, new_kv = lax.optimization_barrier((parts, queries, new_kv))
    received = exchange(parts.reshape((chips,) + parts.shape[2:]), CHIPS)
    scores, values = new_tokens(queries, new_kv)
    return merge(received, scores, values, queries.shape)


def solution(mesh):
    fine = jax.sharding.Mesh(mesh.devices.reshape(4, 2, 4, 4), ("y", "core", "z", "x"))
    grp, seq = ("y", "core"), ("z", "x")
    placed = (
        P(grp, None, seq),
        P(grp, None, None, None),
        P(grp + seq, None),
        P(grp + seq, None),
        P(grp, seq, None),
        P(grp, seq, None),
        P(grp),
        P(),
    )
    return jax.shard_map(
        per_device, mesh=fine, in_specs=placed, out_specs=P(grp, None, seq), check_vma=False
    )
```

```python
import functools
import math

import jax
import jax.numpy as jnp
from jax import lax
from jax.experimental import pallas as pl
from jax.experimental.pallas import tpu as pltpu
from jax.sharding import PartitionSpec as P

H = 64
KVH = 8
HEAD = 128
LOWEST = -(2.0**100)
SCALE = HEAD ** (-0.5) * math.log2(math.e)
TAIL = 8
PARAMS = pltpu.CompilerParams(vmem_limit_bytes=32 << 20)

NT = (((1,), (1,)), ((), ()))
NN = (((1,), (0,)), ((), ()))


def dot(a, b, dims):
    return lax.dot_general(a, b, dims, preferred_element_type=jnp.float32)


def iota(shape, axis):
    return lax.broadcasted_iota(jnp.int32, shape, axis)


def as_bf16(x):
    return x.astype(jnp.bfloat16).astype(jnp.float32)


def columns(x):
    return [x[:, a * HEAD : (a + 1) * HEAD] for a in range(x.shape[1] // HEAD)]


def pack(tops, totals):
    lane = iota((TAIL, HEAD), 1)
    piece = lax.rem(lane, 32) // 8
    packed = None
    for a, (top, total) in enumerate(zip(tops, totals)):
        high = as_bf16(total)
        mixed = jnp.where(piece == 1, high, total - high)
        mixed = jnp.where(piece == 0, top, mixed)
        packed = mixed if a == 0 else jnp.where(lane // 32 == a, mixed, packed)
    return packed.astype(jnp.bfloat16)


def unpack(tails, tiles):
    shape = (HEAD, tiles * HEAD)
    start = iota(shape, 0) - 32 * (iota(shape, 1) // HEAD)
    first = (start == 0).astype(jnp.float32).astype(jnp.bfloat16)
    second = ((start == 8) | (start == 16)).astype(jnp.float32).astype(jnp.bfloat16)
    return dot(tails, first, NN), dot(tails, second, NN)


def combine(tops, totals, numerators):
    upper = functools.reduce(jnp.maximum, tops)
    factors = [jnp.exp2(top - upper) for top in tops]
    total = sum(x * f for x, f in zip(totals, factors))
    return upper, total, sum(x * f for x, f in zip(numerators, factors))


def query_rows(q_ref):
    heads = range(q_ref.shape[2] // HEAD)
    held = [q_ref[r].astype(jnp.float32) for r in range(q_ref.shape[0])]
    return jnp.concatenate([x[:, h * HEAD : (h + 1) * HEAD] for x in held for h in heads], axis=0)


def spread_kernel(q_ref, out_ref):
    block = query_rows(q_ref).astype(jnp.bfloat16)
    for d in range(out_ref.shape[0]):
        out_ref[d] = block


def spread(queries, copies):
    return pl.pallas_call(
        spread_kernel,
        out_shape=jax.ShapeDtypeStruct((copies, queries.size // HEAD, HEAD), jnp.bfloat16),
        compiler_params=PARAMS,
        name="spread",
    )(pltpu.with_memory_space_constraint(queries, pltpu.HBM))


def locate_kernel(slot_ref, *refs, span):
    lengths, info = refs[:-1], refs[-1]
    slots = lengths[0].shape[0]
    cores, layers = lax.axis_size("core"), lax.axis_size("y")
    core = lax.axis_index("core")
    start = (lax.axis_index("z") * lax.axis_size("x") + lax.axis_index("x")) * span
    total = slots * len(lengths)
    for side, length_ref in enumerate(lengths):
        owner = lax.rem(core + side, cores)
        first = (lax.axis_index("y") * cores + owner) * slots
        for j in range(slots):
            row = jnp.int32(0)
            for r in range(slot_ref.shape[0]):
                row = jnp.where(slot_ref[r] == first + j, jnp.int32(r), row)
            group = lax.div(row, slots)
            served = lax.rem(group, cores) == core
            at = side * slots + j
            info[at] = jnp.where(served, lax.div(group, cores), layers)
            info[total + at] = lax.rem(row, slots)
            info[2 * total + at] = jnp.clip(length_ref[j] - start, 0, span)


def locate(row_slot, lengths, span):
    smem = pl.BlockSpec(memory_space=pltpu.SMEM)
    total = sum(x.shape[0] for x in lengths)
    return pl.pallas_call(
        functools.partial(locate_kernel, span=span),
        in_specs=[smem] * (1 + len(lengths)),
        out_specs=smem,
        out_shape=jax.ShapeDtypeStruct((3 * total,), jnp.int32),
        compiler_params=PARAMS,
        name="locate",
    )(row_slot, *lengths)


def attend_kernel(info, near_ref, *refs, sides, heads, tile):
    sources, out_ref = refs[: 4 * sides], refs[4 * sides]
    k_ref, v_ref, sk_ref, sv_ref, block, q_ref, own_top, own_acc = refs[4 * sides + 1 :][:8]
    even_scores, odd_scores, even_peak, odd_peak, sems, own_sems, out_sems = refs[4 * sides + 9 :]
    layers, _, rows, _ = near_ref.shape
    _, _, halves, tiles = q_ref.shape[:4]
    numerators = tiles * 8
    chunk = layers * rows
    wide = heads * HEAD
    length = sources[0].shape[0]
    slots, span, _ = sources[2].shape
    pairs = KVH // heads
    ones = jnp.ones((tile, HEAD), jnp.bfloat16)

    def columns_at(index, width):
        start = index * width if isinstance(index, int) else pl.multiple_of(index * width, width)
        return pl.ds(start, width)

    def copy(side, kind, index):
        source = sources[4 * side + kind]
        if kind < 2:
            to = (k_ref, v_ref)[kind].at[index, pl.ds(side * length, length)]
            part = source.at[:, columns_at(index, HEAD)]
            return pltpu.make_async_copy(part, to, sems.at[2 * side + kind, index])
        to = (sk_ref, sv_ref)[kind - 2].at[index, pl.ds(side * slots, slots)]
        part = source.at[:, :, columns_at(index, wide)]
        return pltpu.make_async_copy(part, to, own_sems.at[2 * side + kind - 2, index])

    def wait(kind, index):
        for side in range(sides):
            copy(side, kind, index).wait()

    def send(pair):
        at = pl.ds(pair * heads * halves, heads * halves)
        return pltpu.make_async_copy(block.at[:, at], out_ref.at[:, at], out_sems.at[pair])

    for pair in range(pairs):
        for kind in (0, 1):
            for i in range(heads):
                for side in range(sides):
                    copy(side, kind, pair * heads + i).start()
        for kind in (2, 3):
            for side in range(sides):
                copy(side, kind, pair).start()

    own_top[...] = jnp.full(own_top.shape, LOWEST, jnp.float32)
    own_acc[...] = jnp.zeros(own_acc.shape, jnp.float32)
    position = iota((heads * halves * 8, span), 1)
    steps = sides * length // tile

    def score(head, n, scores, peak):
        q = near_ref[:, head].reshape(chunk, HEAD)
        found = dot(q, k_ref[head, n * tile : (n + 1) * tile], NT)
        scores[n] = found
        return functools.reduce(jnp.maximum, columns(found) + ([] if peak is None else [peak]))

    def keep_peak(peak, peak_ref):
        peak = jnp.max(peak, axis=1, keepdims=True) * SCALE
        peak_ref[...] = jnp.broadcast_to(as_bf16(peak), (chunk, HEAD))

    def weigh(head, n, scores, shift, summed):
        weights = jnp.exp2(scores[n] * SCALE - shift).astype(jnp.bfloat16)
        values = v_ref[head, n * tile : (n + 1) * tile]
        part = dot(weights, jnp.concatenate([values, ones], axis=1), NN)
        return part if summed is None else summed + part

    def both(head, scores, peak_ref, next_head, next_scores):
        shift = jnp.concatenate([peak_ref[...]] * (tile // HEAD), axis=1)
        summed = peak = None
        for n in range(steps):
            summed = weigh(head, n, scores, shift, summed)
            peak = score(next_head, n, next_scores, peak)
        return summed, peak

    def finish(head, i, peak, summed):
        own = own_top[:layers, i].reshape(chunk, HEAD)
        carried = own_acc[:layers, i].reshape(chunk, 2 * HEAD)
        top = jnp.maximum(peak, own)
        keep, add = jnp.exp2(peak - top), jnp.exp2(own - top)
        sums = summed[:, HEAD:] * keep + carried[:, HEAD:] * add
        numerator = (summed[:, :HEAD] * keep + carried[:, :HEAD] * add).astype(jnp.bfloat16)
        results = []
        for b in range(chunk // numerators):
            low = b * numerators
            parts = [slice(low + 8 * a, low + 8 * a + 8) for a in range(tiles)]
            tail = pack([top[p] for p in parts], [sums[p] for p in parts])
            results.append((numerator[low : low + numerators], tail))
        for b, (found, tail) in enumerate(results):
            to = block.at[b // halves, head * halves + b % halves]
            to[:numerators] = found
            to[numerators:] = tail

    def continuations(pair):
        for i in range(heads):
            x = near_ref[:, pair * heads + i].astype(jnp.float32)
            q_ref[:, i] = x.reshape((layers,) + q_ref.shape[2:])
        total = sides * slots
        size = halves * 8
        none = jnp.zeros((size, HEAD), jnp.float32)
        found = []
        for j in range(total):
            layer, row, live = info[j], info[total + j], info[2 * total + j]
            wide_rows = []
            for i in range(heads):
                q = q_ref[jnp.minimum(layer, layers - 1), i, :, row].reshape(size, HEAD)
                q = [q if n == i else none for n in range(heads)]
                wide_rows.append(jnp.concatenate(q, axis=1))
            q = jnp.concatenate(wide_rows, axis=0).astype(jnp.bfloat16)
            own = dot(q, sk_ref[pair, j], NT) * SCALE
            own = jnp.where(position < live, own, LOWEST)
            peak = jnp.max(own, axis=1, keepdims=True)
            peak = jnp.broadcast_to(as_bf16(peak), (heads * size, HEAD))
            shift = jnp.concatenate([peak] * (span // HEAD), axis=1)
            weights = jnp.exp2(own - shift)
            sums = jnp.sum(weights, axis=1, keepdims=True)
            sums = jnp.broadcast_to(sums, (heads * size, HEAD))
            summed = dot(weights.astype(jnp.bfloat16), sv_ref[pair, j], NN)
            found.append((layer, row, peak, sums, summed))
        for layer, row, peak, sums, summed in found:
            for i in range(heads):
                at = slice(i * size, (i + 1) * size)
                state = [summed[at, i * HEAD : (i + 1) * HEAD], sums[at]]
                state = jnp.concatenate(state, axis=1)
                own_top[layer, i, :, row] = peak[at].reshape(halves, 8, HEAD)
                own_acc[layer, i, :, row] = state.reshape(halves, 8, 2 * HEAD)

    wait(0, 0)
    peak = None
    for n in range(steps):
        peak = score(0, n, even_scores, peak)
    keep_peak(peak, even_peak)

    @pl.loop(0, pairs)
    def _(pair):
        even = pair * heads
        odd, after = even + 1, jnp.minimum(even + 2, KVH - 1)
        wait(0, odd)
        wait(1, even)
        wait(2, pair)
        wait(3, pair)
        summed, peak = both(even, even_scores, even_peak, odd, odd_scores)
        continuations(pair)
        finish(even, 0, even_peak[...], summed)
        keep_peak(peak, odd_peak)
        wait(1, odd)

        @pl.when(pair < pairs - 1)
        def _():
            wait(0, after)

        summed, peak = both(odd, odd_scores, odd_peak, after, even_scores)
        finish(odd, 1, odd_peak[...], summed)
        keep_peak(peak, even_peak)
        send(pair).start()

    for pair in range(pairs):
        send(pair).wait()


def attend(info, near, caches, tile):
    heads = 2
    layers, members, numerators, _ = near.shape
    halves = members // KVH
    near = near.reshape(layers, KVH, halves * numerators, HEAD)
    keys, values, suffix_keys, suffix_values = caches[0]
    sides = len(caches)
    length = sides * keys.shape[0]
    slots, span, _ = suffix_keys.shape
    out = jax.ShapeDtypeStruct((layers, members, numerators + TAIL, HEAD), jnp.bfloat16)
    tiled = (heads, halves, numerators // 8, 8)
    rows = layers * halves * numerators
    anywhere = pl.BlockSpec(memory_space=pl.ANY)
    pairs = KVH // heads
    prompt = pltpu.VMEM((KVH, length, HEAD), keys.dtype)
    own = pltpu.VMEM((pairs, sides * slots, span, heads * HEAD), keys.dtype)
    scores = pltpu.VMEM((length // tile, rows, tile), jnp.float32)
    peak = pltpu.VMEM((rows, HEAD), jnp.float32)
    return pl.pallas_call(
        functools.partial(attend_kernel, sides=sides, heads=heads, tile=tile),
        in_specs=[
            pl.BlockSpec(memory_space=pltpu.SMEM),
            pl.BlockSpec(memory_space=pltpu.VMEM),
        ]
        + [anywhere] * (4 * sides),
        out_specs=anywhere,
        out_shape=out,
        scratch_shapes=[
            prompt,
            prompt,
            own,
            own,
            pltpu.VMEM(out.shape, out.dtype),
            pltpu.VMEM((layers,) + tiled + (HEAD,), jnp.float32),
            pltpu.VMEM((layers + 1,) + tiled + (HEAD,), jnp.float32),
            pltpu.VMEM((layers + 1,) + tiled + (2 * HEAD,), jnp.float32),
            scores,
            scores,
            peak,
            peak,
            pltpu.SemaphoreType.DMA((2 * sides, KVH)),
            pltpu.SemaphoreType.DMA((2 * sides, pairs)),
            pltpu.SemaphoreType.DMA((pairs,)),
        ],
        compiler_params=pltpu.CompilerParams(vmem_limit_bytes=48 << 20),
        name="attend",
    )(info, near, *[x for cache in caches for x in cache])


def new_kernel(q_ref, new_ref, score_ref, value_ref):
    rows, steps, width = q_ref.shape
    member = lax.axis_index("z") * lax.axis_size("x") + lax.axis_index("x")
    kv_head = member * (width // HEAD) // (H // KVH)
    at_head = pl.ds(pl.multiple_of(kv_head * HEAD, HEAD), HEAD)
    step = lax.rem(iota((8, HEAD), 0), steps)
    queries = query_rows(q_ref)
    for r in range(rows):
        for u in range(steps):
            key, value = (
                jnp.broadcast_to(new_ref[r, u, n : n + 1, at_head].astype(jnp.float32), (8, HEAD))
                for n in range(2)
            )
            score = jnp.sum(queries[r * 8 : r * 8 + 8] * key, axis=1, keepdims=True) * SCALE
            score_ref[u, r] = jnp.where(step >= u, jnp.broadcast_to(score, (8, HEAD)), LOWEST)
            value_ref[u, r] = value


def new_tokens(queries, new_kv):
    rows, steps, _ = queries.shape
    out = jax.ShapeDtypeStruct((steps, rows, 8, HEAD), jnp.float32)
    return pl.pallas_call(
        new_kernel,
        out_shape=[out, out],
        compiler_params=PARAMS,
        name="new_tokens",
    )(queries, new_kv)


def merge_kernel(parts_ref, score_ref, value_ref, out_ref):
    rows, steps, width = out_ref.shape
    sources, size, _ = parts_ref.shape
    numerators = size - TAIL
    one = jnp.ones((8, HEAD), jnp.float32)
    blocks = [parts_ref[s] for s in range(sources)]
    tails = [x[numerators:].astype(jnp.float32) for x in blocks]
    opened = unpack(jnp.concatenate(tails, axis=0).astype(jnp.bfloat16), rows)
    opened = [columns(x) for x in opened]
    results = []
    for r in range(rows):
        pieces = [slice(s * 8, s * 8 + 8) for s in range(sources)]
        tops = [opened[0][r][p] for p in pieces]
        totals = [opened[1][r][p] for p in pieces]
        sums = [x[r * 8 : r * 8 + 8].astype(jnp.float32) for x in blocks]
        for u in range(steps):
            tops.append(score_ref[u, r])
            totals.append(one)
            sums.append(value_ref[u, r])
        _, total, summed = combine(tops, totals, sums)
        results.append(summed / total)
    for r, result in enumerate(results):
        for h in range(width // HEAD):
            out_ref[r, :, h * HEAD : (h + 1) * HEAD] = result[h * steps : (h + 1) * steps].astype(
                jnp.bfloat16
            )


def merge(parts, scores, values, shape):
    return pl.pallas_call(
        merge_kernel,
        out_shape=jax.ShapeDtypeStruct(shape, jnp.bfloat16),
        compiler_params=PARAMS,
        name="merge",
    )(parts, scores, values)


CHIPS = ("y", "z", "x")


def exchange(x, axes):
    return lax.all_to_all(x, axes, split_axis=0, concat_axis=0, tiled=True)


def per_device(
    queries,
    new_kv,
    prefix_keys,
    prefix_values,
    suffix_keys,
    suffix_values,
    suffix_lengths,
    row_slot,
):
    layers = lax.axis_size("y")
    cores = lax.axis_size("core")
    members = lax.axis_size("z") * lax.axis_size("x")
    chips = layers * members
    swap = [(i, (i + 1) % cores) for i in range(cores)]

    own = (prefix_keys, prefix_values, suffix_keys, suffix_values)
    far = tuple(lax.ppermute(x, "core", swap) for x in own)
    own = tuple(pltpu.with_memory_space_constraint(x, pltpu.HBM) for x in own)
    far_lengths = lax.ppermute(suffix_lengths, "core", swap)

    blocks, row_slot = lax.optimization_barrier((spread(queries, chips), row_slot))
    near = exchange(blocks, CHIPS)
    info = locate(row_slot, (suffix_lengths, far_lengths), suffix_keys.shape[1])
    near, info = lax.optimization_barrier((near, info))
    near = near.reshape((layers, members) + near.shape[1:])
    parts = attend(info, near, (own, far), 512)
    parts, queries, new_kv = lax.optimization_barrier((parts, queries, new_kv))
    received = exchange(parts.reshape((chips,) + parts.shape[2:]), CHIPS)
    scores, values = new_tokens(queries, new_kv)
    return merge(received, scores, values, queries.shape)


def solution(mesh):
    fine = jax.sharding.Mesh(mesh.devices.reshape(4, 2, 4, 4), ("y", "core", "z", "x"))
    grp, seq = ("y", "core"), ("z", "x")
    placed = (
        P(grp, None, seq),
        P(grp, None, None, None),
        P(grp + seq, None),
        P(grp + seq, None),
        P(grp, seq, None),
        P(grp, seq, None),
        P(grp),
        P(),
    )
    return jax.shard_map(
        per_device, mesh=fine, in_specs=placed, out_specs=P(grp, None, seq), check_vma=False
    )
```

```python
import functools
import math

import jax
import jax.numpy as jnp
from jax import lax
from jax.experimental import pallas as pl
from jax.experimental.pallas import tpu as pltpu
from jax.sharding import PartitionSpec as P

H = 64
KVH = 8
HEAD = 128
LOWEST = -(2.0**100)
SCALE = HEAD ** (-0.5) * math.log2(math.e)
TAIL = 8
PARAMS = pltpu.CompilerParams(vmem_limit_bytes=32 << 20)

NT = (((1,), (1,)), ((), ()))
NN = (((1,), (0,)), ((), ()))


def dot(a, b, dims):
    return lax.dot_general(a, b, dims, preferred_element_type=jnp.float32)


def iota(shape, axis):
    return lax.broadcasted_iota(jnp.int32, shape, axis)


def as_bf16(x):
    return x.astype(jnp.bfloat16).astype(jnp.float32)


def columns(x):
    return [x[:, a * HEAD : (a + 1) * HEAD] for a in range(x.shape[1] // HEAD)]


def pack(tops, totals):
    lane = iota((TAIL, HEAD), 1)
    piece = lax.rem(lane, 32) // 8
    packed = None
    for a, (top, total) in enumerate(zip(tops, totals)):
        high = as_bf16(total)
        mixed = jnp.where(piece == 1, high, total - high)
        mixed = jnp.where(piece == 0, top, mixed)
        packed = mixed if a == 0 else jnp.where(lane // 32 == a, mixed, packed)
    return packed.astype(jnp.bfloat16)


def unpack(tails, tiles):
    shape = (HEAD, tiles * HEAD)
    start = iota(shape, 0) - 32 * (iota(shape, 1) // HEAD)
    first = (start == 0).astype(jnp.float32).astype(jnp.bfloat16)
    second = ((start == 8) | (start == 16)).astype(jnp.float32).astype(jnp.bfloat16)
    return dot(tails, first, NN), dot(tails, second, NN)


def combine(tops, totals, numerators):
    upper = functools.reduce(jnp.maximum, tops)
    factors = [jnp.exp2(top - upper) for top in tops]
    total = sum(x * f for x, f in zip(totals, factors))
    return upper, total, sum(x * f for x, f in zip(numerators, factors))


def query_rows(q_ref):
    heads = range(q_ref.shape[2] // HEAD)
    held = [q_ref[r].astype(jnp.float32) for r in range(q_ref.shape[0])]
    return jnp.concatenate([x[:, h * HEAD : (h + 1) * HEAD] for x in held for h in heads], axis=0)


def spread_kernel(q_ref, out_ref):
    block = query_rows(q_ref).astype(jnp.bfloat16)
    for d in range(out_ref.shape[0]):
        out_ref[d] = block


def spread(queries, copies):
    return pl.pallas_call(
        spread_kernel,
        out_shape=jax.ShapeDtypeStruct((copies, queries.size // HEAD, HEAD), jnp.bfloat16),
        compiler_params=PARAMS,
        name="spread",
    )(pltpu.with_memory_space_constraint(queries, pltpu.HBM))


def locate_kernel(slot_ref, *refs, span):
    lengths, info = refs[:-1], refs[-1]
    slots = lengths[0].shape[0]
    cores, layers = lax.axis_size("core"), lax.axis_size("y")
    core = lax.axis_index("core")
    start = (lax.axis_index("z") * lax.axis_size("x") + lax.axis_index("x")) * span
    total = slots * len(lengths)
    for side, length_ref in enumerate(lengths):
        owner = lax.rem(core + side, cores)
        first = (lax.axis_index("y") * cores + owner) * slots
        for j in range(slots):
            row = jnp.int32(0)
            for r in range(slot_ref.shape[0]):
                row = jnp.where(slot_ref[r] == first + j, jnp.int32(r), row)
            group = lax.div(row, slots)
            served = lax.rem(group, cores) == core
            at = side * slots + j
            info[at] = jnp.where(served, lax.div(group, cores), layers)
            info[total + at] = lax.rem(row, slots)
            info[2 * total + at] = jnp.clip(length_ref[j] - start, 0, span)


def locate(row_slot, lengths, span):
    smem = pl.BlockSpec(memory_space=pltpu.SMEM)
    total = sum(x.shape[0] for x in lengths)
    return pl.pallas_call(
        functools.partial(locate_kernel, span=span),
        in_specs=[smem] * (1 + len(lengths)),
        out_specs=smem,
        out_shape=jax.ShapeDtypeStruct((3 * total,), jnp.int32),
        compiler_params=PARAMS,
        name="locate",
    )(row_slot, *lengths)


def attend_kernel(info, near_ref, *refs, sides, heads, chunk):
    count = 4 * sides
    sources, out_ref, held = refs[:count], refs[count], refs[count + 1 : 2 * count + 1]
    block, q_ref, own_top, own_acc, sems, out_sems = refs[2 * count + 1 :]
    layers, _, rows, _ = near_ref.shape
    _, _, halves, tiles = q_ref.shape[:4]
    numerators = tiles * 8
    per_chunk = chunk // rows
    wide = heads * HEAD
    length = sources[0].shape[0]
    slots, span, _ = sources[2].shape
    ones = jnp.ones((length, HEAD), jnp.bfloat16)
    pairs = KVH // heads

    def copy(n, pair):
        start = pair * wide if isinstance(pair, int) else pl.multiple_of(pair * wide, wide)
        at = pl.ds(start, wide)
        part = sources[n].at[:, at] if n % 4 < 2 else sources[n].at[:, :, at]
        return pltpu.make_async_copy(part, held[n].at[pair], sems.at[n, pair])

    def send(pair):
        at = pl.ds(pair * heads * halves, heads * halves)
        return pltpu.make_async_copy(block.at[:, at], out_ref.at[:, at], out_sems.at[pair])

    order = [4 * side + kind for kind in (0, 2, 3, 1) for side in range(sides)]
    for pair in range(pairs):
        for n in order:
            copy(n, pair).start()

    own_top[...] = jnp.full(own_top.shape, LOWEST, jnp.float32)
    own_acc[...] = jnp.zeros(own_acc.shape, jnp.float32)
    position = iota((halves * 8, span), 1)

    def cut(i):
        return slice(i * HEAD, (i + 1) * HEAD)

    @pl.loop(0, pairs)
    def _(pair):
        first = pair * heads

        def wait(kind):
            for side in range(sides):
                copy(4 * side + kind, pair).wait()

        def scored(i, c):
            at = slice(c * per_chunk, (c + 1) * per_chunk)
            q = near_ref[at, first + i].reshape(chunk, HEAD)
            return [dot(q, held[4 * side][pair, :, cut(i)], NT) for side in range(sides)]

        items = [(i, c) for i in range(heads) for c in range(layers // per_chunk)]
        wait(0)
        scores = scored(*items[0])
        wait(2)
        wait(3)

        for i in range(heads):
            x = near_ref[:, first + i].astype(jnp.float32)
            q_ref[:, i] = x.reshape((layers,) + q_ref.shape[2:])
        found = []
        total = sides * slots
        for j in range(total):
            layer, row, live = info[j], info[total + j], info[2 * total + j]
            sk_ref, sv_ref = held[4 * (j // slots) + 2 : 4 * (j // slots) + 4]
            for i in range(heads):
                q = q_ref[jnp.minimum(layer, layers - 1), i, :, row]
                q = q.reshape(halves * 8, HEAD).astype(jnp.bfloat16)
                own = dot(q, sk_ref[pair, j % slots, :, cut(i)], NT) * SCALE
                own = jnp.where(position < live, own, LOWEST)
                peak = jnp.max(own, axis=1, keepdims=True)
                peak = jnp.broadcast_to(as_bf16(peak), (halves * 8, HEAD))
                shift = jnp.concatenate([peak] * (span // HEAD), axis=1)
                weights = jnp.exp2(own - shift)
                sums = jnp.sum(weights, axis=1, keepdims=True)
                sums = jnp.broadcast_to(sums, (halves * 8, HEAD))
                values = sv_ref[pair, j % slots, :, cut(i)]
                summed = dot(weights.astype(jnp.bfloat16), values, NN)
                found.append((layer, i, row, peak, jnp.concatenate([summed, sums], axis=1)))
        for layer, i, row, peak, summed in found:
            own_top[layer, i, :, row] = peak.reshape(halves, 8, HEAD)
            own_acc[layer, i, :, row] = summed.reshape(halves, 8, 2 * HEAD)

        wait(1)
        for number, (i, c) in enumerate(items):
            later = scored(*items[number + 1]) if number + 1 < len(items) else None
            peak = functools.reduce(jnp.maximum, [jnp.max(x, axis=1, keepdims=True) for x in scores])
            peak = jnp.broadcast_to(as_bf16(peak * SCALE), (chunk, HEAD))
            shift = jnp.concatenate([peak] * (length // HEAD), axis=1)
            summed = None
            for side, x in enumerate(scores):
                weights = jnp.exp2(x * SCALE - shift).astype(jnp.bfloat16)
                values = held[4 * side + 1][pair, :, cut(i)]
                part = dot(weights, jnp.concatenate([values, ones], axis=1), NN)
                summed = part if summed is None else summed + part
            at = slice(c * per_chunk, (c + 1) * per_chunk)
            own = own_top[at, i].reshape(chunk, HEAD)
            carried = own_acc[at, i].reshape(chunk, 2 * HEAD)
            top = jnp.maximum(peak, own)
            keep, add = jnp.exp2(peak - top), jnp.exp2(own - top)
            sums = summed[:, HEAD:] * keep + carried[:, HEAD:] * add
            numerator = (summed[:, :HEAD] * keep + carried[:, :HEAD] * add).astype(jnp.bfloat16)
            results = []
            for b in range(chunk // numerators):
                low = b * numerators
                parts = [slice(low + 8 * a, low + 8 * a + 8) for a in range(tiles)]
                tail = pack([top[p] for p in parts], [sums[p] for p in parts])
                results.append((numerator[low : low + numerators], tail))
            for b, (found_block, tail) in enumerate(results):
                to = block.at[c * per_chunk + b // halves, (first + i) * halves + b % halves]
                to[:numerators] = found_block
                to[numerators:] = tail
            scores = later
        send(pair).start()

    for pair in range(pairs):
        send(pair).wait()


def attend(info, near, caches, heads, chunk):
    layers, members, numerators, _ = near.shape
    halves = members // KVH
    near = near.reshape(layers, KVH, halves * numerators, HEAD)
    arrays = [x for cache in caches for x in cache]
    out = jax.ShapeDtypeStruct((layers, members, numerators + TAIL, HEAD), jnp.bfloat16)
    tiled = (heads, halves, numerators // 8, 8)
    anywhere = pl.BlockSpec(memory_space=pl.ANY)
    pairs = KVH // heads
    return pl.pallas_call(
        functools.partial(attend_kernel, sides=len(caches), heads=heads, chunk=chunk),
        in_specs=[
            pl.BlockSpec(memory_space=pltpu.SMEM),
            pl.BlockSpec(memory_space=pltpu.VMEM),
        ]
        + [anywhere] * len(arrays),
        out_specs=anywhere,
        out_shape=out,
        scratch_shapes=[
            pltpu.VMEM((pairs,) + x.shape[:-1] + (heads * HEAD,), x.dtype) for x in arrays
        ]
        + [
            pltpu.VMEM(out.shape, out.dtype),
            pltpu.VMEM((layers,) + tiled + (HEAD,), jnp.float32),
            pltpu.VMEM((layers + 1,) + tiled + (HEAD,), jnp.float32),
            pltpu.VMEM((layers + 1,) + tiled + (2 * HEAD,), jnp.float32),
            pltpu.SemaphoreType.DMA((len(arrays), pairs)),
            pltpu.SemaphoreType.DMA((pairs,)),
        ],
        compiler_params=pltpu.CompilerParams(vmem_limit_bytes=48 << 20),
        name="attend",
    )(info, near, *arrays)


def new_kernel(q_ref, new_ref, score_ref, value_ref):
    rows, steps, width = q_ref.shape
    member = lax.axis_index("z") * lax.axis_size("x") + lax.axis_index("x")
    kv_head = member * (width // HEAD) // (H // KVH)
    at_head = pl.ds(pl.multiple_of(kv_head * HEAD, HEAD), HEAD)
    step = lax.rem(iota((8, HEAD), 0), steps)
    queries = query_rows(q_ref)
    for r in range(rows):
        for u in range(steps):
            key, value = (
                jnp.broadcast_to(new_ref[r, u, n : n + 1, at_head].astype(jnp.float32), (8, HEAD))
                for n in range(2)
            )
            score = jnp.sum(queries[r * 8 : r * 8 + 8] * key, axis=1, keepdims=True) * SCALE
            score_ref[u, r] = jnp.where(step >= u, jnp.broadcast_to(score, (8, HEAD)), LOWEST)
            value_ref[u, r] = value


def new_tokens(queries, new_kv):
    rows, steps, _ = queries.shape
    out = jax.ShapeDtypeStruct((steps, rows, 8, HEAD), jnp.float32)
    return pl.pallas_call(
        new_kernel,
        out_shape=[out, out],
        compiler_params=PARAMS,
        name="new_tokens",
    )(queries, new_kv)


def merge_kernel(parts_ref, score_ref, value_ref, out_ref):
    rows, steps, width = out_ref.shape
    sources, size, _ = parts_ref.shape
    numerators = size - TAIL
    one = jnp.ones((8, HEAD), jnp.float32)
    blocks = [parts_ref[s] for s in range(sources)]
    tails = [x[numerators:].astype(jnp.float32) for x in blocks]
    opened = unpack(jnp.concatenate(tails, axis=0).astype(jnp.bfloat16), rows)
    opened = [columns(x) for x in opened]
    results = []
    for r in range(rows):
        pieces = [slice(s * 8, s * 8 + 8) for s in range(sources)]
        tops = [opened[0][r][p] for p in pieces]
        totals = [opened[1][r][p] for p in pieces]
        sums = [x[r * 8 : r * 8 + 8].astype(jnp.float32) for x in blocks]
        for u in range(steps):
            tops.append(score_ref[u, r])
            totals.append(one)
            sums.append(value_ref[u, r])
        _, total, summed = combine(tops, totals, sums)
        results.append(summed / total)
    for r, result in enumerate(results):
        for h in range(width // HEAD):
            out_ref[r, :, h * HEAD : (h + 1) * HEAD] = result[h * steps : (h + 1) * steps].astype(
                jnp.bfloat16
            )


def merge(parts, scores, values, shape):
    return pl.pallas_call(
        merge_kernel,
        out_shape=jax.ShapeDtypeStruct(shape, jnp.bfloat16),
        compiler_params=PARAMS,
        name="merge",
    )(parts, scores, values)


CHIPS = ("y", "z", "x")


def exchange(x, axes):
    return lax.all_to_all(x, axes, split_axis=0, concat_axis=0, tiled=True)


def per_device(
    queries,
    new_kv,
    prefix_keys,
    prefix_values,
    suffix_keys,
    suffix_values,
    suffix_lengths,
    row_slot,
):
    layers = lax.axis_size("y")
    cores = lax.axis_size("core")
    members = lax.axis_size("z") * lax.axis_size("x")
    chips = layers * members
    swap = [(i, (i + 1) % cores) for i in range(cores)]

    own = (prefix_keys, prefix_values, suffix_keys, suffix_values)
    blocks, row_slot, suffix_lengths, *own = lax.optimization_barrier(
        (spread(queries, chips), row_slot, suffix_lengths, *own)
    )
    far = tuple(lax.ppermute(x, "core", swap) for x in own)
    far_lengths = lax.ppermute(suffix_lengths, "core", swap)
    own = tuple(pltpu.with_memory_space_constraint(x, pltpu.HBM) for x in own)

    near = exchange(blocks, CHIPS)
    info = locate(row_slot, (suffix_lengths, far_lengths), suffix_keys.shape[1])
    near, info = lax.optimization_barrier((near, info))
    near = near.reshape((layers, members) + near.shape[1:])
    parts = attend(info, near, (own, far), 2, 128)
    parts, queries, new_kv = lax.optimization_barrier((parts, queries, new_kv))
    received = exchange(parts.reshape((chips,) + parts.shape[2:]), CHIPS)
    scores, values = new_tokens(queries, new_kv)
    return merge(received, scores, values, queries.shape)


def solution(mesh):
    fine = jax.sharding.Mesh(mesh.devices.reshape(4, 2, 4, 4), ("y", "core", "z", "x"))
    grp, seq = ("y", "core"), ("z", "x")
    placed = (
        P(grp, None, seq),
        P(grp, None, None, None),
        P(grp + seq, None),
        P(grp + seq, None),
        P(grp, seq, None),
        P(grp, seq, None),
        P(grp),
        P(),
    )
    return jax.shard_map(
        per_device, mesh=fine, in_specs=placed, out_specs=P(grp, None, seq), check_vma=False
    )
```

```python
import functools
import math

import jax
import jax.numpy as jnp
from jax import lax
from jax.experimental import pallas as pl
from jax.experimental.pallas import tpu as pltpu
from jax.sharding import PartitionSpec as P

H = 64
KVH = 8
HEAD = 128
LOWEST = -(2.0**100)
SCALE = HEAD ** (-0.5) * math.log2(math.e)
TAIL = 8
PARAMS = pltpu.CompilerParams(vmem_limit_bytes=32 << 20)

NT = (((1,), (1,)), ((), ()))
NN = (((1,), (0,)), ((), ()))


def dot(a, b, dims):
    return lax.dot_general(a, b, dims, preferred_element_type=jnp.float32)


def iota(shape, axis):
    return lax.broadcasted_iota(jnp.int32, shape, axis)


def as_bf16(x):
    return x.astype(jnp.bfloat16).astype(jnp.float32)


def columns(x):
    return [x[:, a * HEAD : (a + 1) * HEAD] for a in range(x.shape[1] // HEAD)]


def pack(tops, totals):
    lane = iota((TAIL, HEAD), 1)
    piece = lax.rem(lane, 32) // 8
    packed = None
    for a, (top, total) in enumerate(zip(tops, totals)):
        high = as_bf16(total)
        mixed = jnp.where(piece == 1, high, total - high)
        mixed = jnp.where(piece == 0, top, mixed)
        packed = mixed if a == 0 else jnp.where(lane // 32 == a, mixed, packed)
    return packed.astype(jnp.bfloat16)


def unpack(tails, tiles):
    shape = (HEAD, tiles * HEAD)
    start = iota(shape, 0) - 32 * (iota(shape, 1) // HEAD)
    first = (start == 0).astype(jnp.float32).astype(jnp.bfloat16)
    second = ((start == 8) | (start == 16)).astype(jnp.float32).astype(jnp.bfloat16)
    return dot(tails, first, NN), dot(tails, second, NN)


def combine(tops, totals, numerators):
    upper = functools.reduce(jnp.maximum, tops)
    factors = [jnp.exp2(top - upper) for top in tops]
    total = sum(x * f for x, f in zip(totals, factors))
    return upper, total, sum(x * f for x, f in zip(numerators, factors))


def query_rows(q_ref):
    heads = range(q_ref.shape[2] // HEAD)
    held = [q_ref[r].astype(jnp.float32) for r in range(q_ref.shape[0])]
    return jnp.concatenate([x[:, h * HEAD : (h + 1) * HEAD] for x in held for h in heads], axis=0)


def spread_kernel(q_ref, out_ref):
    block = query_rows(q_ref).astype(jnp.bfloat16)
    for d in range(out_ref.shape[0]):
        out_ref[d] = block


def spread(queries, copies):
    return pl.pallas_call(
        spread_kernel,
        out_shape=jax.ShapeDtypeStruct((copies, queries.size // HEAD, HEAD), jnp.bfloat16),
        compiler_params=PARAMS,
        name="spread",
    )(pltpu.with_memory_space_constraint(queries, pltpu.HBM))


def locate_kernel(slot_ref, *refs, span):
    lengths, info = refs[:-1], refs[-1]
    slots = lengths[0].shape[0]
    cores, layers = lax.axis_size("core"), lax.axis_size("y")
    core = lax.axis_index("core")
    start = (lax.axis_index("z") * lax.axis_size("x") + lax.axis_index("x")) * span
    total = slots * len(lengths)
    for side, length_ref in enumerate(lengths):
        owner = lax.rem(core + side, cores)
        first = (lax.axis_index("y") * cores + owner) * slots
        for j in range(slots):
            row = jnp.int32(0)
            for r in range(slot_ref.shape[0]):
                row = jnp.where(slot_ref[r] == first + j, jnp.int32(r), row)
            group = lax.div(row, slots)
            served = lax.rem(group, cores) == core
            at = side * slots + j
            info[at] = jnp.where(served, lax.div(group, cores), layers)
            info[total + at] = lax.rem(row, slots)
            info[2 * total + at] = jnp.clip(length_ref[j] - start, 0, span)


def locate(row_slot, lengths, span):
    smem = pl.BlockSpec(memory_space=pltpu.SMEM)
    total = sum(x.shape[0] for x in lengths)
    return pl.pallas_call(
        functools.partial(locate_kernel, span=span),
        in_specs=[smem] * (1 + len(lengths)),
        out_specs=smem,
        out_shape=jax.ShapeDtypeStruct((3 * total,), jnp.int32),
        compiler_params=PARAMS,
        name="locate",
    )(row_slot, *lengths)


def attend_kernel(info, near_ref, *refs, sides, heads, chunk):
    count = 4 * sides
    sources, out_ref, held = refs[:count], refs[count], refs[count + 1 : 2 * count + 1]
    block, q_ref, own_top, own_acc, sems, out_sems = refs[2 * count + 1 :]
    layers, _, rows, _ = near_ref.shape
    _, _, halves, tiles = q_ref.shape[:4]
    numerators = tiles * 8
    per_chunk = chunk // rows
    wide = heads * HEAD
    length = sources[0].shape[0]
    slots, span, _ = sources[2].shape
    ones = jnp.ones((length, HEAD), jnp.bfloat16)
    pairs = KVH // heads

    def copy(n, pair):
        start = pair * wide if isinstance(pair, int) else pl.multiple_of(pair * wide, wide)
        at = pl.ds(start, wide)
        part = sources[n].at[:, at] if n % 4 < 2 else sources[n].at[:, :, at]
        return pltpu.make_async_copy(part, held[n].at[pair], sems.at[n, pair])

    def send(pair):
        at = pl.ds(pair * heads * halves, heads * halves)
        return pltpu.make_async_copy(block.at[:, at], out_ref.at[:, at], out_sems.at[pair])

    for pair in range(pairs):
        for n in range(count):
            copy(n, pair).start()

    own_top[...] = jnp.full(own_top.shape, LOWEST, jnp.float32)
    own_acc[...] = jnp.zeros(own_acc.shape, jnp.float32)
    position = iota((heads * halves * 8, span), 1)

    def cut(i):
        return slice(i * HEAD, (i + 1) * HEAD)

    @pl.loop(0, pairs)
    def _(pair):
        for n in range(count):
            copy(n, pair).wait()
        first = pair * heads

        def scored(i, c):
            at = slice(c * per_chunk, (c + 1) * per_chunk)
            q = near_ref[at, first + i].reshape(chunk, HEAD)
            return [dot(q, held[4 * side][pair, :, cut(i)], NT) for side in range(sides)]

        items = [(i, c) for i in range(heads) for c in range(layers // per_chunk)]
        scores = scored(*items[0])

        for i in range(heads):
            x = near_ref[:, first + i].astype(jnp.float32)
            q_ref[:, i] = x.reshape((layers,) + q_ref.shape[2:])
        found = []
        total = sides * slots
        size = halves * 8
        none = jnp.zeros((size, HEAD), jnp.float32)
        for j in range(total):
            layer, row, live = info[j], info[total + j], info[2 * total + j]
            sk_ref, sv_ref = held[4 * (j // slots) + 2 : 4 * (j // slots) + 4]
            stacked = []
            for i in range(heads):
                q = q_ref[jnp.minimum(layer, layers - 1), i, :, row].reshape(size, HEAD)
                stacked.append(jnp.concatenate([q if n == i else none for n in range(heads)], axis=1))
            q = jnp.concatenate(stacked, axis=0).astype(jnp.bfloat16)
            own = dot(q, sk_ref[pair, j % slots], NT) * SCALE
            own = jnp.where(position < live, own, LOWEST)
            peak = jnp.max(own, axis=1, keepdims=True)
            peak = jnp.broadcast_to(as_bf16(peak), (heads * size, HEAD))
            shift = jnp.concatenate([peak] * (span // HEAD), axis=1)
            weights = jnp.exp2(own - shift).astype(jnp.bfloat16)
            found.append((layer, row, peak, weights, dot(weights, sv_ref[pair, j % slots], NN)))
        sums = dot(jnp.concatenate([x[3] for x in found], axis=0), ones[:span], NN)
        for j, (layer, row, peak, _, summed) in enumerate(found):
            for i in range(heads):
                at = slice(i * size, (i + 1) * size)
                total_at = slice((j * heads + i) * size, (j * heads + i + 1) * size)
                state = jnp.concatenate([summed[at, cut(i)], sums[total_at]], axis=1)
                own_top[layer, i, :, row] = peak[at].reshape(halves, 8, HEAD)
                own_acc[layer, i, :, row] = state.reshape(halves, 8, 2 * HEAD)

        for number, (i, c) in enumerate(items):
            later = scored(*items[number + 1]) if number + 1 < len(items) else None
            peak = functools.reduce(jnp.maximum, [jnp.max(x, axis=1, keepdims=True) for x in scores])
            peak = jnp.broadcast_to(as_bf16(peak * SCALE), (chunk, HEAD))
            shift = jnp.concatenate([peak] * (length // HEAD), axis=1)
            summed = None
            for side, x in enumerate(scores):
                weights = jnp.exp2(x * SCALE - shift).astype(jnp.bfloat16)
                values = held[4 * side + 1][pair, :, cut(i)]
                part = dot(weights, jnp.concatenate([values, ones], axis=1), NN)
                summed = part if summed is None else summed + part
            at = slice(c * per_chunk, (c + 1) * per_chunk)
            own = own_top[at, i].reshape(chunk, HEAD)
            carried = own_acc[at, i].reshape(chunk, 2 * HEAD)
            top = jnp.maximum(peak, own)
            keep, add = jnp.exp2(peak - top), jnp.exp2(own - top)
            sums = summed[:, HEAD:] * keep + carried[:, HEAD:] * add
            numerator = (summed[:, :HEAD] * keep + carried[:, :HEAD] * add).astype(jnp.bfloat16)
            results = []
            for b in range(chunk // numerators):
                low = b * numerators
                parts = [slice(low + 8 * a, low + 8 * a + 8) for a in range(tiles)]
                tail = pack([top[p] for p in parts], [sums[p] for p in parts])
                results.append((numerator[low : low + numerators], tail))
            for b, (found_block, tail) in enumerate(results):
                to = block.at[c * per_chunk + b // halves, (first + i) * halves + b % halves]
                to[:numerators] = found_block
                to[numerators:] = tail
            scores = later
        send(pair).start()

    for pair in range(pairs):
        send(pair).wait()


def attend(info, near, caches, heads, chunk):
    layers, members, numerators, _ = near.shape
    halves = members // KVH
    near = near.reshape(layers, KVH, halves * numerators, HEAD)
    arrays = [x for cache in caches for x in cache]
    out = jax.ShapeDtypeStruct((layers, members, numerators + TAIL, HEAD), jnp.bfloat16)
    tiled = (heads, halves, numerators // 8, 8)
    anywhere = pl.BlockSpec(memory_space=pl.ANY)
    pairs = KVH // heads
    return pl.pallas_call(
        functools.partial(attend_kernel, sides=len(caches), heads=heads, chunk=chunk),
        in_specs=[
            pl.BlockSpec(memory_space=pltpu.SMEM),
            pl.BlockSpec(memory_space=pltpu.VMEM),
        ]
        + [anywhere] * len(arrays),
        out_specs=anywhere,
        out_shape=out,
        scratch_shapes=[
            pltpu.VMEM((pairs,) + x.shape[:-1] + (heads * HEAD,), x.dtype) for x in arrays
        ]
        + [
            pltpu.VMEM(out.shape, out.dtype),
            pltpu.VMEM((layers,) + tiled + (HEAD,), jnp.float32),
            pltpu.VMEM((layers + 1,) + tiled + (HEAD,), jnp.float32),
            pltpu.VMEM((layers + 1,) + tiled + (2 * HEAD,), jnp.float32),
            pltpu.SemaphoreType.DMA((len(arrays), pairs)),
            pltpu.SemaphoreType.DMA((pairs,)),
        ],
        compiler_params=pltpu.CompilerParams(vmem_limit_bytes=48 << 20),
        name="attend",
    )(info, near, *arrays)


def new_kernel(q_ref, new_ref, score_ref, value_ref):
    rows, steps, width = q_ref.shape
    member = lax.axis_index("z") * lax.axis_size("x") + lax.axis_index("x")
    kv_head = member * (width // HEAD) // (H // KVH)
    at_head = pl.ds(pl.multiple_of(kv_head * HEAD, HEAD), HEAD)
    step = lax.rem(iota((8, HEAD), 0), steps)
    queries = query_rows(q_ref)
    for r in range(rows):
        for u in range(steps):
            key, value = (
                jnp.broadcast_to(new_ref[r, u, n : n + 1, at_head].astype(jnp.float32), (8, HEAD))
                for n in range(2)
            )
            score = jnp.sum(queries[r * 8 : r * 8 + 8] * key, axis=1, keepdims=True) * SCALE
            score_ref[u, r] = jnp.where(step >= u, jnp.broadcast_to(score, (8, HEAD)), LOWEST)
            value_ref[u, r] = value


def new_tokens(queries, new_kv):
    rows, steps, _ = queries.shape
    out = jax.ShapeDtypeStruct((steps, rows, 8, HEAD), jnp.float32)
    return pl.pallas_call(
        new_kernel,
        out_shape=[out, out],
        compiler_params=PARAMS,
        name="new_tokens",
    )(queries, new_kv)


def merge_kernel(parts_ref, score_ref, value_ref, out_ref):
    rows, steps, width = out_ref.shape
    sources, size, _ = parts_ref.shape
    numerators = size - TAIL
    one = jnp.ones((8, HEAD), jnp.float32)
    blocks = [parts_ref[s] for s in range(sources)]
    tails = [x[numerators:].astype(jnp.float32) for x in blocks]
    opened = unpack(jnp.concatenate(tails, axis=0).astype(jnp.bfloat16), rows)
    opened = [columns(x) for x in opened]
    results = []
    for r in range(rows):
        pieces = [slice(s * 8, s * 8 + 8) for s in range(sources)]
        tops = [opened[0][r][p] for p in pieces]
        totals = [opened[1][r][p] for p in pieces]
        sums = [x[r * 8 : r * 8 + 8].astype(jnp.float32) for x in blocks]
        for u in range(steps):
            tops.append(score_ref[u, r])
            totals.append(one)
            sums.append(value_ref[u, r])
        _, total, summed = combine(tops, totals, sums)
        results.append(summed / total)
    for r, result in enumerate(results):
        for h in range(width // HEAD):
            out_ref[r, :, h * HEAD : (h + 1) * HEAD] = result[h * steps : (h + 1) * steps].astype(
                jnp.bfloat16
            )


def merge(parts, scores, values, shape):
    return pl.pallas_call(
        merge_kernel,
        out_shape=jax.ShapeDtypeStruct(shape, jnp.bfloat16),
        compiler_params=PARAMS,
        name="merge",
    )(parts, scores, values)


CHIPS = ("y", "z", "x")


def exchange(x, axes):
    return lax.all_to_all(x, axes, split_axis=0, concat_axis=0, tiled=True)


def per_device(
    queries,
    new_kv,
    prefix_keys,
    prefix_values,
    suffix_keys,
    suffix_values,
    suffix_lengths,
    row_slot,
):
    layers = lax.axis_size("y")
    cores = lax.axis_size("core")
    members = lax.axis_size("z") * lax.axis_size("x")
    chips = layers * members
    swap = [(i, (i + 1) % cores) for i in range(cores)]

    own = (prefix_keys, prefix_values, suffix_keys, suffix_values)
    far = tuple(lax.ppermute(x, "core", swap) for x in own)
    own = tuple(pltpu.with_memory_space_constraint(x, pltpu.HBM) for x in own)
    far_lengths = lax.ppermute(suffix_lengths, "core", swap)

    blocks, row_slot = lax.optimization_barrier((spread(queries, chips), row_slot))
    near = exchange(blocks, CHIPS)
    info = locate(row_slot, (suffix_lengths, far_lengths), suffix_keys.shape[1])
    near, info = lax.optimization_barrier((near, info))
    near = near.reshape((layers, members) + near.shape[1:])
    parts = attend(info, near, (own, far), 2, 128)
    parts, queries, new_kv = lax.optimization_barrier((parts, queries, new_kv))
    received = exchange(parts.reshape((chips,) + parts.shape[2:]), CHIPS)
    scores, values = new_tokens(queries, new_kv)
    return merge(received, scores, values, queries.shape)


def solution(mesh):
    fine = jax.sharding.Mesh(mesh.devices.reshape(4, 2, 4, 4), ("y", "core", "z", "x"))
    grp, seq = ("y", "core"), ("z", "x")
    placed = (
        P(grp, None, seq),
        P(grp, None, None, None),
        P(grp + seq, None),
        P(grp + seq, None),
        P(grp, seq, None),
        P(grp, seq, None),
        P(grp),
        P(),
    )
    return jax.shard_map(
        per_device, mesh=fine, in_specs=placed, out_specs=P(grp, None, seq), check_vma=False
    )
```

```python
import functools
import math

import jax
import jax.numpy as jnp
from jax import lax
from jax.experimental import pallas as pl
from jax.experimental.pallas import tpu as pltpu
from jax.sharding import PartitionSpec as P

H = 64
KVH = 8
HEAD = 128
LOWEST = -(2.0**100)
SCALE = HEAD ** (-0.5) * math.log2(math.e)
TAIL = 8
PARAMS = pltpu.CompilerParams(vmem_limit_bytes=32 << 20)

NT = (((1,), (1,)), ((), ()))
NN = (((1,), (0,)), ((), ()))


def dot(a, b, dims):
    return lax.dot_general(a, b, dims, preferred_element_type=jnp.float32)


def iota(shape, axis):
    return lax.broadcasted_iota(jnp.int32, shape, axis)


def as_bf16(x):
    return x.astype(jnp.bfloat16).astype(jnp.float32)


def columns(x):
    return [x[:, a * HEAD : (a + 1) * HEAD] for a in range(x.shape[1] // HEAD)]


def pack(tops, totals):
    lane = iota((TAIL, HEAD), 1)
    piece = lax.rem(lane, 32) // 8
    packed = None
    for a, (top, total) in enumerate(zip(tops, totals)):
        high = as_bf16(total)
        mixed = jnp.where(piece == 1, high, total - high)
        mixed = jnp.where(piece == 0, top, mixed)
        packed = mixed if a == 0 else jnp.where(lane // 32 == a, mixed, packed)
    return packed.astype(jnp.bfloat16)


def unpack(tails, tiles):
    shape = (HEAD, tiles * HEAD)
    start = iota(shape, 0) - 32 * (iota(shape, 1) // HEAD)
    first = (start == 0).astype(jnp.float32).astype(jnp.bfloat16)
    second = ((start == 8) | (start == 16)).astype(jnp.float32).astype(jnp.bfloat16)
    return dot(tails, first, NN), dot(tails, second, NN)


def combine(tops, totals, numerators):
    upper = functools.reduce(jnp.maximum, tops)
    factors = [jnp.exp2(top - upper) for top in tops]
    total = sum(x * f for x, f in zip(totals, factors))
    return upper, total, sum(x * f for x, f in zip(numerators, factors))


def query_rows(q_ref):
    heads = range(q_ref.shape[2] // HEAD)
    held = [q_ref[r].astype(jnp.float32) for r in range(q_ref.shape[0])]
    return jnp.concatenate([x[:, h * HEAD : (h + 1) * HEAD] for x in held for h in heads], axis=0)


def spread_kernel(q_ref, out_ref):
    block = query_rows(q_ref).astype(jnp.bfloat16)
    for d in range(out_ref.shape[0]):
        out_ref[d] = block


def spread(queries, copies):
    return pl.pallas_call(
        spread_kernel,
        out_shape=jax.ShapeDtypeStruct((copies, queries.size // HEAD, HEAD), jnp.bfloat16),
        compiler_params=PARAMS,
        name="spread",
    )(pltpu.with_memory_space_constraint(queries, pltpu.HBM))


def locate_kernel(slot_ref, *refs, span):
    lengths, info = refs[:-1], refs[-1]
    slots = lengths[0].shape[0]
    cores, layers = lax.axis_size("core"), lax.axis_size("y")
    core = lax.axis_index("core")
    start = (lax.axis_index("z") * lax.axis_size("x") + lax.axis_index("x")) * span
    total = slots * len(lengths)
    for side, length_ref in enumerate(lengths):
        owner = lax.rem(core + side, cores)
        first = (lax.axis_index("y") * cores + owner) * slots
        for j in range(slots):
            row = jnp.int32(0)
            for r in range(slot_ref.shape[0]):
                row = jnp.where(slot_ref[r] == first + j, jnp.int32(r), row)
            group = lax.div(row, slots)
            served = lax.rem(group, cores) == core
            at = side * slots + j
            info[at] = jnp.where(served, lax.div(group, cores), layers)
            info[total + at] = lax.rem(row, slots)
            info[2 * total + at] = jnp.clip(length_ref[j] - start, 0, span)


def locate(row_slot, lengths, span):
    smem = pl.BlockSpec(memory_space=pltpu.SMEM)
    total = sum(x.shape[0] for x in lengths)
    return pl.pallas_call(
        functools.partial(locate_kernel, span=span),
        in_specs=[smem] * (1 + len(lengths)),
        out_specs=smem,
        out_shape=jax.ShapeDtypeStruct((3 * total,), jnp.int32),
        compiler_params=PARAMS,
        name="locate",
    )(row_slot, *lengths)


def attend_kernel(info, near_ref, *refs, sides, heads, chunk):
    count = 4 * sides
    sources, out_ref, held = refs[:count], refs[count], refs[count + 1 : 2 * count + 1]
    block, q_ref, own_top, own_acc, sems, out_sems = refs[2 * count + 1 :]
    layers, _, rows, _ = near_ref.shape
    _, _, halves, tiles = q_ref.shape[:4]
    numerators = tiles * 8
    per_chunk = chunk // rows
    wide = heads * HEAD
    length = sources[0].shape[0]
    slots, span, _ = sources[2].shape
    ones = jnp.ones((length, HEAD), jnp.bfloat16)
    pairs = KVH // heads

    def copy(n, pair):
        start = pair * wide if isinstance(pair, int) else pl.multiple_of(pair * wide, wide)
        at = pl.ds(start, wide)
        part = sources[n].at[:, at] if n % 4 < 2 else sources[n].at[:, :, at]
        return pltpu.make_async_copy(part, held[n].at[pair], sems.at[n, pair])

    def send(pair):
        at = pl.ds(pair * heads * halves, heads * halves)
        return pltpu.make_async_copy(block.at[:, at], out_ref.at[:, at], out_sems.at[pair])

    for pair in range(pairs):
        for n in range(count):
            copy(n, pair).start()

    own_top[...] = jnp.full(own_top.shape, LOWEST, jnp.float32)
    own_acc[...] = jnp.zeros(own_acc.shape, jnp.float32)
    position = iota((heads * halves * 8, span), 1)

    def cut(i):
        return slice(i * HEAD, (i + 1) * HEAD)

    @pl.loop(0, pairs)
    def _(pair):
        for n in range(count):
            copy(n, pair).wait()
        first = pair * heads

        def scored(i, c):
            at = slice(c * per_chunk, (c + 1) * per_chunk)
            q = near_ref[at, first + i].reshape(chunk, HEAD)
            return [dot(q, held[4 * side][pair, :, cut(i)], NT) for side in range(sides)]

        items = [(i, c) for i in range(heads) for c in range(layers // per_chunk)]
        scores = scored(*items[0])

        for i in range(heads):
            x = near_ref[:, first + i].astype(jnp.float32)
            q_ref[:, i] = x.reshape((layers,) + q_ref.shape[2:])
        found = []
        total = sides * slots
        size = halves * 8
        none = jnp.zeros((size, HEAD), jnp.float32)
        for j in range(total):
            layer, row, live = info[j], info[total + j], info[2 * total + j]
            sk_ref, sv_ref = held[4 * (j // slots) + 2 : 4 * (j // slots) + 4]
            stacked = []
            for i in range(heads):
                q = q_ref[jnp.minimum(layer, layers - 1), i, :, row].reshape(size, HEAD)
                stacked.append(jnp.concatenate([q if n == i else none for n in range(heads)], axis=1))
            q = jnp.concatenate(stacked, axis=0).astype(jnp.bfloat16)
            own = dot(q, sk_ref[pair, j % slots], NT) * SCALE
            own = jnp.where(position < live, own, LOWEST)
            peak = jnp.max(own, axis=1, keepdims=True)
            peak = jnp.broadcast_to(as_bf16(peak), (heads * size, HEAD))
            shift = jnp.concatenate([peak] * (span // HEAD), axis=1)
            weights = jnp.exp2(own - shift).astype(jnp.bfloat16)
            for i in range(heads):
                at = slice(i * size, (i + 1) * size)
                values = sv_ref[pair, j % slots, :, cut(i)]
                values = jnp.concatenate([values, ones[:span]], axis=1)
                found.append((layer, i, row, peak[at], dot(weights[at], values, NN)))
        for layer, i, row, peak, summed in found:
            own_top[layer, i, :, row] = peak.reshape(halves, 8, HEAD)
            own_acc[layer, i, :, row] = summed.reshape(halves, 8, 2 * HEAD)

        for number, (i, c) in enumerate(items):
            later = scored(*items[number + 1]) if number + 1 < len(items) else None
            peak = functools.reduce(jnp.maximum, [jnp.max(x, axis=1, keepdims=True) for x in scores])
            peak = jnp.broadcast_to(as_bf16(peak * SCALE), (chunk, HEAD))
            shift = jnp.concatenate([peak] * (length // HEAD), axis=1)
            summed = None
            for side, x in enumerate(scores):
                weights = jnp.exp2(x * SCALE - shift).astype(jnp.bfloat16)
                values = held[4 * side + 1][pair, :, cut(i)]
                part = dot(weights, jnp.concatenate([values, ones], axis=1), NN)
                summed = part if summed is None else summed + part
            at = slice(c * per_chunk, (c + 1) * per_chunk)
            own = own_top[at, i].reshape(chunk, HEAD)
            carried = own_acc[at, i].reshape(chunk, 2 * HEAD)
            top = jnp.maximum(peak, own)
            keep, add = jnp.exp2(peak - top), jnp.exp2(own - top)
            sums = summed[:, HEAD:] * keep + carried[:, HEAD:] * add
            numerator = (summed[:, :HEAD] * keep + carried[:, :HEAD] * add).astype(jnp.bfloat16)
            results = []
            for b in range(chunk // numerators):
                low = b * numerators
                parts = [slice(low + 8 * a, low + 8 * a + 8) for a in range(tiles)]
                tail = pack([top[p] for p in parts], [sums[p] for p in parts])
                results.append((numerator[low : low + numerators], tail))
            for b, (found_block, tail) in enumerate(results):
                to = block.at[c * per_chunk + b // halves, (first + i) * halves + b % halves]
                to[:numerators] = found_block
                to[numerators:] = tail
            scores = later
        send(pair).start()

    for pair in range(pairs):
        send(pair).wait()


def attend(info, near, caches, heads, chunk):
    layers, members, numerators, _ = near.shape
    halves = members // KVH
    near = near.reshape(layers, KVH, halves * numerators, HEAD)
    arrays = [x for cache in caches for x in cache]
    out = jax.ShapeDtypeStruct((layers, members, numerators + TAIL, HEAD), jnp.bfloat16)
    tiled = (heads, halves, numerators // 8, 8)
    anywhere = pl.BlockSpec(memory_space=pl.ANY)
    pairs = KVH // heads
    return pl.pallas_call(
        functools.partial(attend_kernel, sides=len(caches), heads=heads, chunk=chunk),
        in_specs=[
            pl.BlockSpec(memory_space=pltpu.SMEM),
            pl.BlockSpec(memory_space=pltpu.VMEM),
        ]
        + [anywhere] * len(arrays),
        out_specs=anywhere,
        out_shape=out,
        scratch_shapes=[
            pltpu.VMEM((pairs,) + x.shape[:-1] + (heads * HEAD,), x.dtype) for x in arrays
        ]
        + [
            pltpu.VMEM(out.shape, out.dtype),
            pltpu.VMEM((layers,) + tiled + (HEAD,), jnp.float32),
            pltpu.VMEM((layers + 1,) + tiled + (HEAD,), jnp.float32),
            pltpu.VMEM((layers + 1,) + tiled + (2 * HEAD,), jnp.float32),
            pltpu.SemaphoreType.DMA((len(arrays), pairs)),
            pltpu.SemaphoreType.DMA((pairs,)),
        ],
        compiler_params=pltpu.CompilerParams(vmem_limit_bytes=48 << 20),
        name="attend",
    )(info, near, *arrays)


def new_kernel(q_ref, new_ref, score_ref, value_ref):
    rows, steps, width = q_ref.shape
    member = lax.axis_index("z") * lax.axis_size("x") + lax.axis_index("x")
    kv_head = member * (width // HEAD) // (H // KVH)
    at_head = pl.ds(pl.multiple_of(kv_head * HEAD, HEAD), HEAD)
    step = lax.rem(iota((8, HEAD), 0), steps)
    queries = query_rows(q_ref)
    for r in range(rows):
        for u in range(steps):
            key, value = (
                jnp.broadcast_to(new_ref[r, u, n : n + 1, at_head].astype(jnp.float32), (8, HEAD))
                for n in range(2)
            )
            score = jnp.sum(queries[r * 8 : r * 8 + 8] * key, axis=1, keepdims=True) * SCALE
            score_ref[u, r] = jnp.where(step >= u, jnp.broadcast_to(score, (8, HEAD)), LOWEST)
            value_ref[u, r] = value


def new_tokens(queries, new_kv):
    rows, steps, _ = queries.shape
    out = jax.ShapeDtypeStruct((steps, rows, 8, HEAD), jnp.float32)
    return pl.pallas_call(
        new_kernel,
        out_shape=[out, out],
        compiler_params=PARAMS,
        name="new_tokens",
    )(queries, new_kv)


def merge_kernel(parts_ref, score_ref, value_ref, out_ref):
    rows, steps, width = out_ref.shape
    sources, size, _ = parts_ref.shape
    numerators = size - TAIL
    one = jnp.ones((8, HEAD), jnp.float32)
    blocks = [parts_ref[s] for s in range(sources)]
    tails = [x[numerators:].astype(jnp.float32) for x in blocks]
    opened = unpack(jnp.concatenate(tails, axis=0).astype(jnp.bfloat16), rows)
    opened = [columns(x) for x in opened]
    results = []
    for r in range(rows):
        pieces = [slice(s * 8, s * 8 + 8) for s in range(sources)]
        tops = [opened[0][r][p] for p in pieces]
        totals = [opened[1][r][p] for p in pieces]
        sums = [x[r * 8 : r * 8 + 8].astype(jnp.float32) for x in blocks]
        for u in range(steps):
            tops.append(score_ref[u, r])
            totals.append(one)
            sums.append(value_ref[u, r])
        _, total, summed = combine(tops, totals, sums)
        results.append(summed / total)
    for r, result in enumerate(results):
        for h in range(width // HEAD):
            out_ref[r, :, h * HEAD : (h + 1) * HEAD] = result[h * steps : (h + 1) * steps].astype(
                jnp.bfloat16
            )


def merge(parts, scores, values, shape):
    return pl.pallas_call(
        merge_kernel,
        out_shape=jax.ShapeDtypeStruct(shape, jnp.bfloat16),
        compiler_params=PARAMS,
        name="merge",
    )(parts, scores, values)


CHIPS = ("y", "z", "x")


def exchange(x, axes):
    return lax.all_to_all(x, axes, split_axis=0, concat_axis=0, tiled=True)


def per_device(
    queries,
    new_kv,
    prefix_keys,
    prefix_values,
    suffix_keys,
    suffix_values,
    suffix_lengths,
    row_slot,
):
    layers = lax.axis_size("y")
    cores = lax.axis_size("core")
    members = lax.axis_size("z") * lax.axis_size("x")
    chips = layers * members
    swap = [(i, (i + 1) % cores) for i in range(cores)]

    far_lengths = lax.ppermute(suffix_lengths, "core", swap)
    far_lengths, suffix_keys, suffix_values = lax.optimization_barrier(
        (far_lengths, suffix_keys, suffix_values)
    )
    own = (prefix_keys, prefix_values, suffix_keys, suffix_values)
    far = tuple(lax.ppermute(x, "core", swap) for x in own)
    own = tuple(pltpu.with_memory_space_constraint(x, pltpu.HBM) for x in own)

    blocks, row_slot = lax.optimization_barrier((spread(queries, chips), row_slot))
    near = exchange(blocks, CHIPS)
    info = locate(row_slot, (suffix_lengths, far_lengths), suffix_keys.shape[1])
    near, info = lax.optimization_barrier((near, info))
    near = near.reshape((layers, members) + near.shape[1:])
    parts = attend(info, near, (own, far), 2, 128)
    parts, queries, new_kv = lax.optimization_barrier((parts, queries, new_kv))
    received = exchange(parts.reshape((chips,) + parts.shape[2:]), CHIPS)
    scores, values = new_tokens(queries, new_kv)
    return merge(received, scores, values, queries.shape)


def solution(mesh):
    fine = jax.sharding.Mesh(mesh.devices.reshape(4, 2, 4, 4), ("y", "core", "z", "x"))
    grp, seq = ("y", "core"), ("z", "x")
    placed = (
        P(grp, None, seq),
        P(grp, None, None, None),
        P(grp + seq, None),
        P(grp + seq, None),
        P(grp, seq, None),
        P(grp, seq, None),
        P(grp),
        P(),
    )
    return jax.shard_map(
        per_device, mesh=fine, in_specs=placed, out_specs=P(grp, None, seq), check_vma=False
    )
```

```python
import functools
import math

import jax
import jax.numpy as jnp
from jax import lax
from jax.experimental import pallas as pl
from jax.experimental.pallas import tpu as pltpu
from jax.sharding import PartitionSpec as P

H = 64
KVH = 8
HEAD = 128
LOWEST = -(2.0**100)
SCALE = HEAD ** (-0.5) * math.log2(math.e)
TAIL = 8
PARAMS = pltpu.CompilerParams(vmem_limit_bytes=32 << 20)

NT = (((1,), (1,)), ((), ()))
NN = (((1,), (0,)), ((), ()))


def dot(a, b, dims):
    return lax.dot_general(a, b, dims, preferred_element_type=jnp.float32)


def iota(shape, axis):
    return lax.broadcasted_iota(jnp.int32, shape, axis)


def as_bf16(x):
    return x.astype(jnp.bfloat16).astype(jnp.float32)


def columns(x):
    return [x[:, a * HEAD : (a + 1) * HEAD] for a in range(x.shape[1] // HEAD)]


def pack(tops, totals):
    lane = iota((TAIL, HEAD), 1)
    piece = lax.rem(lane, 32) // 8
    packed = None
    for a, (top, total) in enumerate(zip(tops, totals)):
        high = as_bf16(total)
        mixed = jnp.where(piece == 1, high, total - high)
        mixed = jnp.where(piece == 0, top, mixed)
        packed = mixed if a == 0 else jnp.where(lane // 32 == a, mixed, packed)
    return packed.astype(jnp.bfloat16)


def unpack(tails, tiles):
    shape = (HEAD, tiles * HEAD)
    start = iota(shape, 0) - 32 * (iota(shape, 1) // HEAD)
    first = (start == 0).astype(jnp.float32).astype(jnp.bfloat16)
    second = ((start == 8) | (start == 16)).astype(jnp.float32).astype(jnp.bfloat16)
    return dot(tails, first, NN), dot(tails, second, NN)


def combine(tops, totals, numerators):
    upper = functools.reduce(jnp.maximum, tops)
    factors = [jnp.exp2(top - upper) for top in tops]
    total = sum(x * f for x, f in zip(totals, factors))
    return upper, total, sum(x * f for x, f in zip(numerators, factors))


def query_rows(q_ref):
    heads = range(q_ref.shape[2] // HEAD)
    held = [q_ref[r].astype(jnp.float32) for r in range(q_ref.shape[0])]
    return jnp.concatenate([x[:, h * HEAD : (h + 1) * HEAD] for x in held for h in heads], axis=0)


def spread_kernel(q_ref, out_ref):
    block = query_rows(q_ref).astype(jnp.bfloat16)
    for d in range(out_ref.shape[0]):
        out_ref[d] = block


def spread(queries, copies):
    return pl.pallas_call(
        spread_kernel,
        out_shape=jax.ShapeDtypeStruct((copies, queries.size // HEAD, HEAD), jnp.bfloat16),
        compiler_params=PARAMS,
        name="spread",
    )(pltpu.with_memory_space_constraint(queries, pltpu.HBM))


def locate_kernel(slot_ref, *refs, span):
    lengths, info = refs[:-1], refs[-1]
    slots = lengths[0].shape[0]
    cores, layers = lax.axis_size("core"), lax.axis_size("y")
    core = lax.axis_index("core")
    start = (lax.axis_index("z") * lax.axis_size("x") + lax.axis_index("x")) * span
    total = slots * len(lengths)
    for side, length_ref in enumerate(lengths):
        owner = lax.rem(core + side, cores)
        first = (lax.axis_index("y") * cores + owner) * slots
        for j in range(slots):
            row = jnp.int32(0)
            for r in range(slot_ref.shape[0]):
                row = jnp.where(slot_ref[r] == first + j, jnp.int32(r), row)
            group = lax.div(row, slots)
            served = lax.rem(group, cores) == core
            at = side * slots + j
            info[at] = jnp.where(served, lax.div(group, cores), layers)
            info[total + at] = lax.rem(row, slots)
            info[2 * total + at] = jnp.clip(length_ref[j] - start, 0, span)


def locate(row_slot, lengths, span):
    smem = pl.BlockSpec(memory_space=pltpu.SMEM)
    total = sum(x.shape[0] for x in lengths)
    return pl.pallas_call(
        functools.partial(locate_kernel, span=span),
        in_specs=[smem] * (1 + len(lengths)),
        out_specs=smem,
        out_shape=jax.ShapeDtypeStruct((3 * total,), jnp.int32),
        compiler_params=PARAMS,
        name="locate",
    )(row_slot, *lengths)


def attend_kernel(info, near_ref, *refs, sides, heads, chunk):
    count = 4 * sides
    sources, out_ref, held = refs[:count], refs[count], refs[count + 1 : 2 * count + 1]
    block, q_ref, own_top, own_acc, sems, out_sems = refs[2 * count + 1 :]
    layers, _, rows, _ = near_ref.shape
    _, _, halves, tiles = q_ref.shape[:4]
    numerators = tiles * 8
    per_chunk = chunk // rows
    wide = heads * HEAD
    length = sources[0].shape[0]
    slots, span, _ = sources[2].shape
    ones = jnp.ones((length, HEAD), jnp.bfloat16)
    pairs = KVH // heads

    def copy(n, pair):
        start = pair * wide if isinstance(pair, int) else pl.multiple_of(pair * wide, wide)
        at = pl.ds(start, wide)
        part = sources[n].at[:, at] if n % 4 < 2 else sources[n].at[:, :, at]
        return pltpu.make_async_copy(part, held[n].at[pair], sems.at[n, pair])

    def send(pair):
        at = pl.ds(pair * heads * halves, heads * halves)
        return pltpu.make_async_copy(block.at[:, at], out_ref.at[:, at], out_sems.at[pair])

    for pair in range(pairs):
        for n in range(count):
            copy(n, pair).start()

    own_top[...] = jnp.full(own_top.shape, LOWEST, jnp.float32)
    own_acc[...] = jnp.zeros(own_acc.shape, jnp.float32)
    position = iota((halves * 8, span), 1)

    def cut(i):
        return slice(i * HEAD, (i + 1) * HEAD)

    def padded(x):
        return jnp.concatenate([x, jnp.zeros_like(x)], axis=1)

    @pl.loop(0, pairs)
    def _(pair):
        for n in range(count):
            copy(n, pair).wait()
        first = pair * heads

        def scored(i, c):
            at = slice(c * per_chunk, (c + 1) * per_chunk)
            q = padded(near_ref[at, first + i].reshape(chunk, HEAD))
            return [dot(q, padded(held[4 * side][pair, :, cut(i)]), NT) for side in range(sides)]

        items = [(i, c) for i in range(heads) for c in range(layers // per_chunk)]
        scores = scored(*items[0])

        for i in range(heads):
            x = near_ref[:, first + i].astype(jnp.float32)
            q_ref[:, i] = x.reshape((layers,) + q_ref.shape[2:])
        found = []
        total = sides * slots
        for j in range(total):
            layer, row, live = info[j], info[total + j], info[2 * total + j]
            sk_ref, sv_ref = held[4 * (j // slots) + 2 : 4 * (j // slots) + 4]
            for i in range(heads):
                q = q_ref[jnp.minimum(layer, layers - 1), i, :, row]
                q = q.reshape(halves * 8, HEAD).astype(jnp.bfloat16)
                own = dot(padded(q), padded(sk_ref[pair, j % slots, :, cut(i)]), NT) * SCALE
                own = jnp.where(position < live, own, LOWEST)
                peak = jnp.max(own, axis=1, keepdims=True)
                peak = jnp.broadcast_to(as_bf16(peak), (halves * 8, HEAD))
                shift = jnp.concatenate([peak] * (span // HEAD), axis=1)
                weights = jnp.exp2(own - shift).astype(jnp.bfloat16)
                values = sv_ref[pair, j % slots, :, cut(i)]
                values = jnp.concatenate([values, ones[:span]], axis=1)
                found.append((layer, i, row, peak, dot(weights, values, NN)))
        for layer, i, row, peak, summed in found:
            own_top[layer, i, :, row] = peak.reshape(halves, 8, HEAD)
            own_acc[layer, i, :, row] = summed.reshape(halves, 8, 2 * HEAD)

        for number, (i, c) in enumerate(items):
            later = scored(*items[number + 1]) if number + 1 < len(items) else None
            peak = functools.reduce(jnp.maximum, [jnp.max(x, axis=1, keepdims=True) for x in scores])
            peak = jnp.broadcast_to(as_bf16(peak * SCALE), (chunk, HEAD))
            shift = jnp.concatenate([peak] * (length // HEAD), axis=1)
            summed = None
            for side, x in enumerate(scores):
                weights = jnp.exp2(x * SCALE - shift).astype(jnp.bfloat16)
                values = held[4 * side + 1][pair, :, cut(i)]
                part = dot(weights, jnp.concatenate([values, ones], axis=1), NN)
                summed = part if summed is None else summed + part
            at = slice(c * per_chunk, (c + 1) * per_chunk)
            own = own_top[at, i].reshape(chunk, HEAD)
            carried = own_acc[at, i].reshape(chunk, 2 * HEAD)
            top = jnp.maximum(peak, own)
            keep, add = jnp.exp2(peak - top), jnp.exp2(own - top)
            sums = summed[:, HEAD:] * keep + carried[:, HEAD:] * add
            numerator = (summed[:, :HEAD] * keep + carried[:, :HEAD] * add).astype(jnp.bfloat16)
            results = []
            for b in range(chunk // numerators):
                low = b * numerators
                parts = [slice(low + 8 * a, low + 8 * a + 8) for a in range(tiles)]
                tail = pack([top[p] for p in parts], [sums[p] for p in parts])
                results.append((numerator[low : low + numerators], tail))
            for b, (found_block, tail) in enumerate(results):
                to = block.at[c * per_chunk + b // halves, (first + i) * halves + b % halves]
                to[:numerators] = found_block
                to[numerators:] = tail
            scores = later
        send(pair).start()

    for pair in range(pairs):
        send(pair).wait()


def attend(info, near, caches, heads, chunk):
    layers, members, numerators, _ = near.shape
    halves = members // KVH
    near = near.reshape(layers, KVH, halves * numerators, HEAD)
    arrays = [x for cache in caches for x in cache]
    out = jax.ShapeDtypeStruct((layers, members, numerators + TAIL, HEAD), jnp.bfloat16)
    tiled = (heads, halves, numerators // 8, 8)
    anywhere = pl.BlockSpec(memory_space=pl.ANY)
    pairs = KVH // heads
    return pl.pallas_call(
        functools.partial(attend_kernel, sides=len(caches), heads=heads, chunk=chunk),
        in_specs=[
            pl.BlockSpec(memory_space=pltpu.SMEM),
            pl.BlockSpec(memory_space=pltpu.VMEM),
        ]
        + [anywhere] * len(arrays),
        out_specs=anywhere,
        out_shape=out,
        scratch_shapes=[
            pltpu.VMEM((pairs,) + x.shape[:-1] + (heads * HEAD,), x.dtype) for x in arrays
        ]
        + [
            pltpu.VMEM(out.shape, out.dtype),
            pltpu.VMEM((layers,) + tiled + (HEAD,), jnp.float32),
            pltpu.VMEM((layers + 1,) + tiled + (HEAD,), jnp.float32),
            pltpu.VMEM((layers + 1,) + tiled + (2 * HEAD,), jnp.float32),
            pltpu.SemaphoreType.DMA((len(arrays), pairs)),
            pltpu.SemaphoreType.DMA((pairs,)),
        ],
        compiler_params=pltpu.CompilerParams(vmem_limit_bytes=48 << 20),
        name="attend",
    )(info, near, *arrays)


def new_kernel(q_ref, new_ref, score_ref, value_ref):
    rows, steps, width = q_ref.shape
    member = lax.axis_index("z") * lax.axis_size("x") + lax.axis_index("x")
    kv_head = member * (width // HEAD) // (H // KVH)
    at_head = pl.ds(pl.multiple_of(kv_head * HEAD, HEAD), HEAD)
    step = lax.rem(iota((8, HEAD), 0), steps)
    queries = query_rows(q_ref)
    for r in range(rows):
        for u in range(steps):
            key, value = (
                jnp.broadcast_to(new_ref[r, u, n : n + 1, at_head].astype(jnp.float32), (8, HEAD))
                for n in range(2)
            )
            score = jnp.sum(queries[r * 8 : r * 8 + 8] * key, axis=1, keepdims=True) * SCALE
            score_ref[u, r] = jnp.where(step >= u, jnp.broadcast_to(score, (8, HEAD)), LOWEST)
            value_ref[u, r] = value


def new_tokens(queries, new_kv):
    rows, steps, _ = queries.shape
    out = jax.ShapeDtypeStruct((steps, rows, 8, HEAD), jnp.float32)
    return pl.pallas_call(
        new_kernel,
        out_shape=[out, out],
        compiler_params=PARAMS,
        name="new_tokens",
    )(queries, new_kv)


def merge_kernel(parts_ref, score_ref, value_ref, out_ref):
    rows, steps, width = out_ref.shape
    sources, size, _ = parts_ref.shape
    numerators = size - TAIL
    one = jnp.ones((8, HEAD), jnp.float32)
    blocks = [parts_ref[s] for s in range(sources)]
    tails = [x[numerators:].astype(jnp.float32) for x in blocks]
    opened = unpack(jnp.concatenate(tails, axis=0).astype(jnp.bfloat16), rows)
    opened = [columns(x) for x in opened]
    results = []
    for r in range(rows):
        pieces = [slice(s * 8, s * 8 + 8) for s in range(sources)]
        tops = [opened[0][r][p] for p in pieces]
        totals = [opened[1][r][p] for p in pieces]
        sums = [x[r * 8 : r * 8 + 8].astype(jnp.float32) for x in blocks]
        for u in range(steps):
            tops.append(score_ref[u, r])
            totals.append(one)
            sums.append(value_ref[u, r])
        _, total, summed = combine(tops, totals, sums)
        results.append(summed / total)
    for r, result in enumerate(results):
        for h in range(width // HEAD):
            out_ref[r, :, h * HEAD : (h + 1) * HEAD] = result[h * steps : (h + 1) * steps].astype(
                jnp.bfloat16
            )


def merge(parts, scores, values, shape):
    return pl.pallas_call(
        merge_kernel,
        out_shape=jax.ShapeDtypeStruct(shape, jnp.bfloat16),
        compiler_params=PARAMS,
        name="merge",
    )(parts, scores, values)


CHIPS = ("y", "z", "x")


def exchange(x, axes):
    return lax.all_to_all(x, axes, split_axis=0, concat_axis=0, tiled=True)


def per_device(
    queries,
    new_kv,
    prefix_keys,
    prefix_values,
    suffix_keys,
    suffix_values,
    suffix_lengths,
    row_slot,
):
    layers = lax.axis_size("y")
    cores = lax.axis_size("core")
    members = lax.axis_size("z") * lax.axis_size("x")
    chips = layers * members
    swap = [(i, (i + 1) % cores) for i in range(cores)]

    own = (prefix_keys, prefix_values, suffix_keys, suffix_values)
    far = tuple(lax.ppermute(x, "core", swap) for x in own)
    own = tuple(pltpu.with_memory_space_constraint(x, pltpu.HBM) for x in own)
    far_lengths = lax.ppermute(suffix_lengths, "core", swap)

    blocks, row_slot = lax.optimization_barrier((spread(queries, chips), row_slot))
    near = exchange(blocks, CHIPS)
    info = locate(row_slot, (suffix_lengths, far_lengths), suffix_keys.shape[1])
    near, info = lax.optimization_barrier((near, info))
    near = near.reshape((layers, members) + near.shape[1:])
    parts = attend(info, near, (own, far), 2, 128)
    parts, queries, new_kv = lax.optimization_barrier((parts, queries, new_kv))
    received = exchange(parts.reshape((chips,) + parts.shape[2:]), CHIPS)
    scores, values = new_tokens(queries, new_kv)
    return merge(received, scores, values, queries.shape)


def solution(mesh):
    fine = jax.sharding.Mesh(mesh.devices.reshape(4, 2, 4, 4), ("y", "core", "z", "x"))
    grp, seq = ("y", "core"), ("z", "x")
    placed = (
        P(grp, None, seq),
        P(grp, None, None, None),
        P(grp + seq, None),
        P(grp + seq, None),
        P(grp, seq, None),
        P(grp, seq, None),
        P(grp),
        P(),
    )
    return jax.shard_map(
        per_device, mesh=fine, in_specs=placed, out_specs=P(grp, None, seq), check_vma=False
    )
```

```python
import functools
import math

import jax
import jax.numpy as jnp
from jax import lax
from jax.experimental import pallas as pl
from jax.experimental.pallas import tpu as pltpu
from jax.sharding import PartitionSpec as P

H = 64
KVH = 8
HEAD = 128
LOWEST = -(2.0**100)
SCALE = HEAD ** (-0.5) * math.log2(math.e)
TAIL = 8
PARAMS = pltpu.CompilerParams(vmem_limit_bytes=32 << 20)

NT = (((1,), (1,)), ((), ()))
NN = (((1,), (0,)), ((), ()))


def dot(a, b, dims):
    return lax.dot_general(a, b, dims, preferred_element_type=jnp.float32)


def iota(shape, axis):
    return lax.broadcasted_iota(jnp.int32, shape, axis)


def as_bf16(x):
    return x.astype(jnp.bfloat16).astype(jnp.float32)


def columns(x):
    return [x[:, a * HEAD : (a + 1) * HEAD] for a in range(x.shape[1] // HEAD)]


def pack(tops, totals):
    lane = iota((TAIL, HEAD), 1)
    piece = lax.rem(lane, 32) // 8
    packed = None
    for a, (top, total) in enumerate(zip(tops, totals)):
        high = as_bf16(total)
        mixed = jnp.where(piece == 1, high, total - high)
        mixed = jnp.where(piece == 0, top, mixed)
        packed = mixed if a == 0 else jnp.where(lane // 32 == a, mixed, packed)
    return packed.astype(jnp.bfloat16)


def unpack(tails, tiles):
    shape = (HEAD, tiles * HEAD)
    start = iota(shape, 0) - 32 * (iota(shape, 1) // HEAD)
    first = (start == 0).astype(jnp.float32).astype(jnp.bfloat16)
    second = ((start == 8) | (start == 16)).astype(jnp.float32).astype(jnp.bfloat16)
    return dot(tails, first, NN), dot(tails, second, NN)


def combine(tops, totals, numerators):
    upper = functools.reduce(jnp.maximum, tops)
    factors = [jnp.exp2(top - upper) for top in tops]
    total = sum(x * f for x, f in zip(totals, factors))
    return upper, total, sum(x * f for x, f in zip(numerators, factors))


def query_rows(q_ref):
    heads = range(q_ref.shape[2] // HEAD)
    held = [q_ref[r].astype(jnp.float32) for r in range(q_ref.shape[0])]
    return jnp.concatenate([x[:, h * HEAD : (h + 1) * HEAD] for x in held for h in heads], axis=0)


def spread_kernel(q_ref, out_ref):
    block = query_rows(q_ref).astype(jnp.bfloat16)
    for d in range(out_ref.shape[0]):
        out_ref[d] = block


def spread(queries, copies):
    return pl.pallas_call(
        spread_kernel,
        out_shape=jax.ShapeDtypeStruct((copies, queries.size // HEAD, HEAD), jnp.bfloat16),
        compiler_params=PARAMS,
        name="spread",
    )(pltpu.with_memory_space_constraint(queries, pltpu.HBM))


def locate_kernel(slot_ref, *refs, span):
    lengths, info = refs[:-1], refs[-1]
    slots = lengths[0].shape[0]
    cores, layers = lax.axis_size("core"), lax.axis_size("y")
    core = lax.axis_index("core")
    start = (lax.axis_index("z") * lax.axis_size("x") + lax.axis_index("x")) * span
    total = slots * len(lengths)
    for side, length_ref in enumerate(lengths):
        owner = lax.rem(core + side, cores)
        first = (lax.axis_index("y") * cores + owner) * slots
        for j in range(slots):
            row = jnp.int32(0)
            for r in range(slot_ref.shape[0]):
                row = jnp.where(slot_ref[r] == first + j, jnp.int32(r), row)
            group = lax.div(row, slots)
            served = lax.rem(group, cores) == core
            at = side * slots + j
            info[at] = jnp.where(served, lax.div(group, cores), layers)
            info[total + at] = lax.rem(row, slots)
            info[2 * total + at] = jnp.clip(length_ref[j] - start, 0, span)


def locate(row_slot, lengths, span):
    smem = pl.BlockSpec(memory_space=pltpu.SMEM)
    total = sum(x.shape[0] for x in lengths)
    return pl.pallas_call(
        functools.partial(locate_kernel, span=span),
        in_specs=[smem] * (1 + len(lengths)),
        out_specs=smem,
        out_shape=jax.ShapeDtypeStruct((3 * total,), jnp.int32),
        compiler_params=PARAMS,
        name="locate",
    )(row_slot, *lengths)


def attend_kernel(info, near_ref, *refs, sides, heads, chunk):
    count = 4 * sides
    sources, out_ref, held = refs[:count], refs[count], refs[count + 1 : 2 * count + 1]
    block, q_ref, own_top, own_acc, sems, out_sems = refs[2 * count + 1 :]
    layers, _, rows, _ = near_ref.shape
    _, _, halves, tiles = q_ref.shape[:4]
    numerators = tiles * 8
    per_chunk = chunk // rows
    wide = heads * HEAD
    length = sources[0].shape[0]
    slots, span, _ = sources[2].shape
    ones = jnp.ones((length, HEAD), jnp.bfloat16)
    pairs = KVH // heads

    def copy(n, pair):
        start = pair * wide if isinstance(pair, int) else pl.multiple_of(pair * wide, wide)
        at = pl.ds(start, wide)
        part = sources[n].at[:, at] if n % 4 < 2 else sources[n].at[:, :, at]
        return pltpu.make_async_copy(part, held[n].at[pair], sems.at[n, pair])

    def send(pair):
        at = pl.ds(pair * heads * halves, heads * halves)
        return pltpu.make_async_copy(block.at[:, at], out_ref.at[:, at], out_sems.at[pair])

    for pair in range(pairs):
        for n in range(count):
            copy(n, pair).start()

    own_top[...] = jnp.full(own_top.shape, LOWEST, jnp.float32)
    own_acc[...] = jnp.zeros(own_acc.shape, jnp.float32)
    position = iota((halves * 8, span), 1)

    def cut(i):
        return slice(i * HEAD, (i + 1) * HEAD)

    @pl.loop(0, pairs)
    def _(pair):
        for n in range(count):
            copy(n, pair).wait()
        first = pair * heads

        def scored(i, c):
            at = slice(c * per_chunk, (c + 1) * per_chunk)
            q = near_ref[at, first + i].reshape(chunk, HEAD)
            return [dot(q, held[4 * side][pair, :, cut(i)], NT) for side in range(sides)]

        items = [(i, c) for i in range(heads) for c in range(layers // per_chunk)]
        scores = scored(*items[0])

        for i in range(heads):
            x = near_ref[:, first + i].astype(jnp.float32)
            q_ref[:, i] = x.reshape((layers,) + q_ref.shape[2:])
        found = []
        total = sides * slots
        for j in range(total):
            layer, row, live = info[j], info[total + j], info[2 * total + j]
            sk_ref, sv_ref = held[4 * (j // slots) + 2 : 4 * (j // slots) + 4]
            for i in range(heads):
                q = q_ref[jnp.minimum(layer, layers - 1), i, :, row]
                q = q.reshape(halves * 8, HEAD).astype(jnp.bfloat16)
                own = dot(q, sk_ref[pair, j % slots, :, cut(i)], NT) * SCALE
                own = jnp.where(position < live, own, LOWEST)
                peak = functools.reduce(jnp.maximum, columns(own))
                peak = jnp.max(peak, axis=1, keepdims=True)
                peak = jnp.broadcast_to(as_bf16(peak), (halves * 8, HEAD))
                shift = jnp.concatenate([peak] * (span // HEAD), axis=1)
                weights = jnp.exp2(own - shift).astype(jnp.bfloat16)
                values = sv_ref[pair, j % slots, :, cut(i)]
                values = jnp.concatenate([values, ones[:span]], axis=1)
                found.append((layer, i, row, peak, dot(weights, values, NN)))
        for layer, i, row, peak, summed in found:
            own_top[layer, i, :, row] = peak.reshape(halves, 8, HEAD)
            own_acc[layer, i, :, row] = summed.reshape(halves, 8, 2 * HEAD)

        for number, (i, c) in enumerate(items):
            later = scored(*items[number + 1]) if number + 1 < len(items) else None
            peak = functools.reduce(jnp.maximum, [y for x in scores for y in columns(x)])
            peak = jnp.max(peak, axis=1, keepdims=True)
            peak = jnp.broadcast_to(as_bf16(peak * SCALE), (chunk, HEAD))
            shift = jnp.concatenate([peak] * (length // HEAD), axis=1)
            summed = None
            for side, x in enumerate(scores):
                weights = jnp.exp2(x * SCALE - shift).astype(jnp.bfloat16)
                values = held[4 * side + 1][pair, :, cut(i)]
                part = dot(weights, jnp.concatenate([values, ones], axis=1), NN)
                summed = part if summed is None else summed + part
            at = slice(c * per_chunk, (c + 1) * per_chunk)
            own = own_top[at, i].reshape(chunk, HEAD)
            carried = own_acc[at, i].reshape(chunk, 2 * HEAD)
            top = jnp.maximum(peak, own)
            keep, add = jnp.exp2(peak - top), jnp.exp2(own - top)
            sums = summed[:, HEAD:] * keep + carried[:, HEAD:] * add
            numerator = (summed[:, :HEAD] * keep + carried[:, :HEAD] * add).astype(jnp.bfloat16)
            results = []
            for b in range(chunk // numerators):
                low = b * numerators
                parts = [slice(low + 8 * a, low + 8 * a + 8) for a in range(tiles)]
                tail = pack([top[p] for p in parts], [sums[p] for p in parts])
                results.append((numerator[low : low + numerators], tail))
            for b, (found_block, tail) in enumerate(results):
                to = block.at[c * per_chunk + b // halves, (first + i) * halves + b % halves]
                to[:numerators] = found_block
                to[numerators:] = tail
            scores = later
        send(pair).start()

    for pair in range(pairs):
        send(pair).wait()


def attend(info, near, caches, heads, chunk):
    layers, members, numerators, _ = near.shape
    halves = members // KVH
    near = near.reshape(layers, KVH, halves * numerators, HEAD)
    arrays = [x for cache in caches for x in cache]
    out = jax.ShapeDtypeStruct((layers, members, numerators + TAIL, HEAD), jnp.bfloat16)
    tiled = (heads, halves, numerators // 8, 8)
    anywhere = pl.BlockSpec(memory_space=pl.ANY)
    pairs = KVH // heads
    return pl.pallas_call(
        functools.partial(attend_kernel, sides=len(caches), heads=heads, chunk=chunk),
        in_specs=[
            pl.BlockSpec(memory_space=pltpu.SMEM),
            pl.BlockSpec(memory_space=pltpu.VMEM),
        ]
        + [anywhere] * len(arrays),
        out_specs=anywhere,
        out_shape=out,
        scratch_shapes=[
            pltpu.VMEM((pairs,) + x.shape[:-1] + (heads * HEAD,), x.dtype) for x in arrays
        ]
        + [
            pltpu.VMEM(out.shape, out.dtype),
            pltpu.VMEM((layers,) + tiled + (HEAD,), jnp.float32),
            pltpu.VMEM((layers + 1,) + tiled + (HEAD,), jnp.float32),
            pltpu.VMEM((layers + 1,) + tiled + (2 * HEAD,), jnp.float32),
            pltpu.SemaphoreType.DMA((len(arrays), pairs)),
            pltpu.SemaphoreType.DMA((pairs,)),
        ],
        compiler_params=pltpu.CompilerParams(vmem_limit_bytes=48 << 20),
        name="attend",
    )(info, near, *arrays)


def new_kernel(q_ref, new_ref, score_ref, value_ref):
    rows, steps, width = q_ref.shape
    member = lax.axis_index("z") * lax.axis_size("x") + lax.axis_index("x")
    kv_head = member * (width // HEAD) // (H // KVH)
    at_head = pl.ds(pl.multiple_of(kv_head * HEAD, HEAD), HEAD)
    step = lax.rem(iota((8, HEAD), 0), steps)
    queries = query_rows(q_ref)
    for r in range(rows):
        for u in range(steps):
            key, value = (
                jnp.broadcast_to(new_ref[r, u, n : n + 1, at_head].astype(jnp.float32), (8, HEAD))
                for n in range(2)
            )
            score = jnp.sum(queries[r * 8 : r * 8 + 8] * key, axis=1, keepdims=True) * SCALE
            score_ref[u, r] = jnp.where(step >= u, jnp.broadcast_to(score, (8, HEAD)), LOWEST)
            value_ref[u, r] = value


def new_tokens(queries, new_kv):
    rows, steps, _ = queries.shape
    out = jax.ShapeDtypeStruct((steps, rows, 8, HEAD), jnp.float32)
    return pl.pallas_call(
        new_kernel,
        out_shape=[out, out],
        compiler_params=PARAMS,
        name="new_tokens",
    )(queries, new_kv)


def merge_kernel(parts_ref, score_ref, value_ref, out_ref):
    rows, steps, width = out_ref.shape
    sources, size, _ = parts_ref.shape
    numerators = size - TAIL
    one = jnp.ones((8, HEAD), jnp.float32)
    blocks = [parts_ref[s] for s in range(sources)]
    tails = [x[numerators:].astype(jnp.float32) for x in blocks]
    opened = unpack(jnp.concatenate(tails, axis=0).astype(jnp.bfloat16), rows)
    opened = [columns(x) for x in opened]
    results = []
    for r in range(rows):
        pieces = [slice(s * 8, s * 8 + 8) for s in range(sources)]
        tops = [opened[0][r][p] for p in pieces]
        totals = [opened[1][r][p] for p in pieces]
        sums = [x[r * 8 : r * 8 + 8].astype(jnp.float32) for x in blocks]
        for u in range(steps):
            tops.append(score_ref[u, r])
            totals.append(one)
            sums.append(value_ref[u, r])
        _, total, summed = combine(tops, totals, sums)
        results.append(summed / total)
    for r, result in enumerate(results):
        for h in range(width // HEAD):
            out_ref[r, :, h * HEAD : (h + 1) * HEAD] = result[h * steps : (h + 1) * steps].astype(
                jnp.bfloat16
            )


def merge(parts, scores, values, shape):
    return pl.pallas_call(
        merge_kernel,
        out_shape=jax.ShapeDtypeStruct(shape, jnp.bfloat16),
        compiler_params=PARAMS,
        name="merge",
    )(parts, scores, values)


CHIPS = ("y", "z", "x")


def exchange(x, axes):
    return lax.all_to_all(x, axes, split_axis=0, concat_axis=0, tiled=True)


def per_device(
    queries,
    new_kv,
    prefix_keys,
    prefix_values,
    suffix_keys,
    suffix_values,
    suffix_lengths,
    row_slot,
):
    layers = lax.axis_size("y")
    cores = lax.axis_size("core")
    members = lax.axis_size("z") * lax.axis_size("x")
    chips = layers * members
    swap = [(i, (i + 1) % cores) for i in range(cores)]

    own = (prefix_keys, prefix_values, suffix_keys, suffix_values)
    far = tuple(lax.ppermute(x, "core", swap) for x in own)
    own = tuple(pltpu.with_memory_space_constraint(x, pltpu.HBM) for x in own)
    far_lengths = lax.ppermute(suffix_lengths, "core", swap)

    blocks, row_slot = lax.optimization_barrier((spread(queries, chips), row_slot))
    near = exchange(blocks, CHIPS)
    info = locate(row_slot, (suffix_lengths, far_lengths), suffix_keys.shape[1])
    near, info = lax.optimization_barrier((near, info))
    near = near.reshape((layers, members) + near.shape[1:])
    parts = attend(info, near, (own, far), 2, 128)
    parts, queries, new_kv = lax.optimization_barrier((parts, queries, new_kv))
    received = exchange(parts.reshape((chips,) + parts.shape[2:]), CHIPS)
    scores, values = new_tokens(queries, new_kv)
    return merge(received, scores, values, queries.shape)


def solution(mesh):
    fine = jax.sharding.Mesh(mesh.devices.reshape(4, 2, 4, 4), ("y", "core", "z", "x"))
    grp, seq = ("y", "core"), ("z", "x")
    placed = (
        P(grp, None, seq),
        P(grp, None, None, None),
        P(grp + seq, None),
        P(grp + seq, None),
        P(grp, seq, None),
        P(grp, seq, None),
        P(grp),
        P(),
    )
    return jax.shard_map(
        per_device, mesh=fine, in_specs=placed, out_specs=P(grp, None, seq), check_vma=False
    )
```

```python
import functools
import math

import jax
import jax.numpy as jnp
from jax import lax
from jax.experimental import pallas as pl
from jax.experimental.pallas import tpu as pltpu
from jax.sharding import PartitionSpec as P

H = 64
KVH = 8
HEAD = 128
LOWEST = -(2.0**100)
SCALE = HEAD ** (-0.5) * math.log2(math.e)
TAIL = 8
PARAMS = pltpu.CompilerParams(vmem_limit_bytes=32 << 20)

NT = (((1,), (1,)), ((), ()))
NN = (((1,), (0,)), ((), ()))


def dot(a, b, dims):
    return lax.dot_general(a, b, dims, preferred_element_type=jnp.float32)


def iota(shape, axis):
    return lax.broadcasted_iota(jnp.int32, shape, axis)


def as_bf16(x):
    return x.astype(jnp.bfloat16).astype(jnp.float32)


def columns(x):
    return [x[:, a * HEAD : (a + 1) * HEAD] for a in range(x.shape[1] // HEAD)]


def pack(tops, totals):
    lane = iota((TAIL, HEAD), 1)
    piece = lax.rem(lane, 32) // 8
    packed = None
    for a, (top, total) in enumerate(zip(tops, totals)):
        high = as_bf16(total)
        mixed = jnp.where(piece == 1, high, total - high)
        mixed = jnp.where(piece == 0, top, mixed)
        packed = mixed if a == 0 else jnp.where(lane // 32 == a, mixed, packed)
    return packed.astype(jnp.bfloat16)


def unpack(tails, tiles):
    shape = (HEAD, tiles * HEAD)
    start = iota(shape, 0) - 32 * (iota(shape, 1) // HEAD)
    first = (start == 0).astype(jnp.float32).astype(jnp.bfloat16)
    second = ((start == 8) | (start == 16)).astype(jnp.float32).astype(jnp.bfloat16)
    return dot(tails, first, NN), dot(tails, second, NN)


def combine(tops, totals, numerators):
    upper = functools.reduce(jnp.maximum, tops)
    factors = [jnp.exp2(top - upper) for top in tops]
    total = sum(x * f for x, f in zip(totals, factors))
    return upper, total, sum(x * f for x, f in zip(numerators, factors))


def query_rows(q_ref):
    heads = range(q_ref.shape[2] // HEAD)
    held = [q_ref[r].astype(jnp.float32) for r in range(q_ref.shape[0])]
    return jnp.concatenate([x[:, h * HEAD : (h + 1) * HEAD] for x in held for h in heads], axis=0)


def spread_kernel(q_ref, out_ref):
    block = query_rows(q_ref).astype(jnp.bfloat16)
    for d in range(out_ref.shape[0]):
        out_ref[d] = block


def spread(queries, copies):
    return pl.pallas_call(
        spread_kernel,
        out_shape=jax.ShapeDtypeStruct((copies, queries.size // HEAD, HEAD), jnp.bfloat16),
        compiler_params=PARAMS,
        name="spread",
    )(pltpu.with_memory_space_constraint(queries, pltpu.HBM))


def locate_kernel(slot_ref, *refs, span):
    lengths, info = refs[:-1], refs[-1]
    slots = lengths[0].shape[0]
    cores, layers = lax.axis_size("core"), lax.axis_size("y")
    core = lax.axis_index("core")
    start = (lax.axis_index("z") * lax.axis_size("x") + lax.axis_index("x")) * span
    total = slots * len(lengths)
    for side, length_ref in enumerate(lengths):
        owner = lax.rem(core + side, cores)
        first = (lax.axis_index("y") * cores + owner) * slots
        for j in range(slots):
            row = jnp.int32(0)
            for r in range(slot_ref.shape[0]):
                row = jnp.where(slot_ref[r] == first + j, jnp.int32(r), row)
            group = lax.div(row, slots)
            served = lax.rem(group, cores) == core
            at = side * slots + j
            info[at] = jnp.where(served, lax.div(group, cores), layers)
            info[total + at] = lax.rem(row, slots)
            info[2 * total + at] = jnp.clip(length_ref[j] - start, 0, span)


def locate(row_slot, lengths, span):
    smem = pl.BlockSpec(memory_space=pltpu.SMEM)
    total = sum(x.shape[0] for x in lengths)
    return pl.pallas_call(
        functools.partial(locate_kernel, span=span),
        in_specs=[smem] * (1 + len(lengths)),
        out_specs=smem,
        out_shape=jax.ShapeDtypeStruct((3 * total,), jnp.int32),
        compiler_params=PARAMS,
        name="locate",
    )(row_slot, *lengths)


def attend_kernel(info, near_ref, *refs, sides, heads, chunk):
    count = 4 * sides
    sources, out_ref, held = refs[:count], refs[count], refs[count + 1 : 2 * count + 1]
    block, q_ref, own_top, own_acc, sems, out_sems = refs[2 * count + 1 :]
    layers, _, rows, _ = near_ref.shape
    _, _, halves, tiles = q_ref.shape[:4]
    numerators = tiles * 8
    per_chunk = chunk // rows
    wide = heads * HEAD
    length = sources[0].shape[0]
    slots, span, _ = sources[2].shape
    ones = jnp.ones((length, HEAD), jnp.bfloat16)
    pairs = KVH // heads

    def copy(n, pair):
        start = pair * wide if isinstance(pair, int) else pl.multiple_of(pair * wide, wide)
        at = pl.ds(start, wide)
        part = sources[n].at[:, at] if n % 4 < 2 else sources[n].at[:, :, at]
        return pltpu.make_async_copy(part, held[n].at[pair], sems.at[n, pair])

    def send(pair):
        at = pl.ds(pair * heads * halves, heads * halves)
        return pltpu.make_async_copy(block.at[:, at], out_ref.at[:, at], out_sems.at[pair])

    for pair in range(pairs):
        for n in range(count):
            copy(n, pair).start()

    own_top[...] = jnp.full(own_top.shape, LOWEST, jnp.float32)
    own_acc[...] = jnp.zeros(own_acc.shape, jnp.float32)
    position = iota((halves * 8, span), 1)

    def cut(i):
        return slice(i * HEAD, (i + 1) * HEAD)

    @pl.loop(0, pairs)
    def _(pair):
        for n in range(count):
            copy(n, pair).wait()
        first = pair * heads

        def scored(i, c):
            at = slice(c * per_chunk, (c + 1) * per_chunk)
            q = near_ref[at, first + i].reshape(chunk, HEAD)
            keys = [held[4 * side][pair, :, cut(i)] for side in range(sides)]
            return dot(q, jnp.concatenate(keys, axis=0), NT)

        items = [(i, c) for i in range(heads) for c in range(layers // per_chunk)]
        scores = scored(*items[0])

        for i in range(heads):
            x = near_ref[:, first + i].astype(jnp.float32)
            q_ref[:, i] = x.reshape((layers,) + q_ref.shape[2:])
        found = []
        total = sides * slots
        for j in range(total):
            layer, row, live = info[j], info[total + j], info[2 * total + j]
            sk_ref, sv_ref = held[4 * (j // slots) + 2 : 4 * (j // slots) + 4]
            for i in range(heads):
                q = q_ref[jnp.minimum(layer, layers - 1), i, :, row]
                q = q.reshape(halves * 8, HEAD).astype(jnp.bfloat16)
                own = dot(q, sk_ref[pair, j % slots, :, cut(i)], NT) * SCALE
                own = jnp.where(position < live, own, LOWEST)
                peak = jnp.max(own, axis=1, keepdims=True)
                peak = jnp.broadcast_to(as_bf16(peak), (halves * 8, HEAD))
                shift = jnp.concatenate([peak] * (span // HEAD), axis=1)
                weights = jnp.exp2(own - shift).astype(jnp.bfloat16)
                values = sv_ref[pair, j % slots, :, cut(i)]
                values = jnp.concatenate([values, ones[:span]], axis=1)
                found.append((layer, i, row, peak, dot(weights, values, NN)))
        for layer, i, row, peak, summed in found:
            own_top[layer, i, :, row] = peak.reshape(halves, 8, HEAD)
            own_acc[layer, i, :, row] = summed.reshape(halves, 8, 2 * HEAD)

        for number, (i, c) in enumerate(items):
            later = scored(*items[number + 1]) if number + 1 < len(items) else None
            peak = jnp.max(scores, axis=1, keepdims=True)
            peak = jnp.broadcast_to(as_bf16(peak * SCALE), (chunk, HEAD))
            shift = jnp.concatenate([peak] * (sides * length // HEAD), axis=1)
            weights = jnp.exp2(scores * SCALE - shift).astype(jnp.bfloat16)
            values = [
                jnp.concatenate([held[4 * side + 1][pair, :, cut(i)], ones], axis=1)
                for side in range(sides)
            ]
            summed = dot(weights, jnp.concatenate(values, axis=0), NN)
            at = slice(c * per_chunk, (c + 1) * per_chunk)
            own = own_top[at, i].reshape(chunk, HEAD)
            carried = own_acc[at, i].reshape(chunk, 2 * HEAD)
            top = jnp.maximum(peak, own)
            keep, add = jnp.exp2(peak - top), jnp.exp2(own - top)
            sums = summed[:, HEAD:] * keep + carried[:, HEAD:] * add
            numerator = (summed[:, :HEAD] * keep + carried[:, :HEAD] * add).astype(jnp.bfloat16)
            results = []
            for b in range(chunk // numerators):
                low = b * numerators
                parts = [slice(low + 8 * a, low + 8 * a + 8) for a in range(tiles)]
                tail = pack([top[p] for p in parts], [sums[p] for p in parts])
                results.append((numerator[low : low + numerators], tail))
            for b, (found_block, tail) in enumerate(results):
                to = block.at[c * per_chunk + b // halves, (first + i) * halves + b % halves]
                to[:numerators] = found_block
                to[numerators:] = tail
            scores = later
        send(pair).start()

    for pair in range(pairs):
        send(pair).wait()


def attend(info, near, caches, heads, chunk):
    layers, members, numerators, _ = near.shape
    halves = members // KVH
    near = near.reshape(layers, KVH, halves * numerators, HEAD)
    arrays = [x for cache in caches for x in cache]
    out = jax.ShapeDtypeStruct((layers, members, numerators + TAIL, HEAD), jnp.bfloat16)
    tiled = (heads, halves, numerators // 8, 8)
    anywhere = pl.BlockSpec(memory_space=pl.ANY)
    pairs = KVH // heads
    return pl.pallas_call(
        functools.partial(attend_kernel, sides=len(caches), heads=heads, chunk=chunk),
        in_specs=[
            pl.BlockSpec(memory_space=pltpu.SMEM),
            pl.BlockSpec(memory_space=pltpu.VMEM),
        ]
        + [anywhere] * len(arrays),
        out_specs=anywhere,
        out_shape=out,
        scratch_shapes=[
            pltpu.VMEM((pairs,) + x.shape[:-1] + (heads * HEAD,), x.dtype) for x in arrays
        ]
        + [
            pltpu.VMEM(out.shape, out.dtype),
            pltpu.VMEM((layers,) + tiled + (HEAD,), jnp.float32),
            pltpu.VMEM((layers + 1,) + tiled + (HEAD,), jnp.float32),
            pltpu.VMEM((layers + 1,) + tiled + (2 * HEAD,), jnp.float32),
            pltpu.SemaphoreType.DMA((len(arrays), pairs)),
            pltpu.SemaphoreType.DMA((pairs,)),
        ],
        compiler_params=pltpu.CompilerParams(vmem_limit_bytes=48 << 20),
        name="attend",
    )(info, near, *arrays)


def new_kernel(q_ref, new_ref, score_ref, value_ref):
    rows, steps, width = q_ref.shape
    member = lax.axis_index("z") * lax.axis_size("x") + lax.axis_index("x")
    kv_head = member * (width // HEAD) // (H // KVH)
    at_head = pl.ds(pl.multiple_of(kv_head * HEAD, HEAD), HEAD)
    step = lax.rem(iota((8, HEAD), 0), steps)
    queries = query_rows(q_ref)
    for r in range(rows):
        for u in range(steps):
            key, value = (
                jnp.broadcast_to(new_ref[r, u, n : n + 1, at_head].astype(jnp.float32), (8, HEAD))
                for n in range(2)
            )
            score = jnp.sum(queries[r * 8 : r * 8 + 8] * key, axis=1, keepdims=True) * SCALE
            score_ref[u, r] = jnp.where(step >= u, jnp.broadcast_to(score, (8, HEAD)), LOWEST)
            value_ref[u, r] = value


def new_tokens(queries, new_kv):
    rows, steps, _ = queries.shape
    out = jax.ShapeDtypeStruct((steps, rows, 8, HEAD), jnp.float32)
    return pl.pallas_call(
        new_kernel,
        out_shape=[out, out],
        compiler_params=PARAMS,
        name="new_tokens",
    )(queries, new_kv)


def merge_kernel(parts_ref, score_ref, value_ref, out_ref):
    rows, steps, width = out_ref.shape
    sources, size, _ = parts_ref.shape
    numerators = size - TAIL
    one = jnp.ones((8, HEAD), jnp.float32)
    blocks = [parts_ref[s] for s in range(sources)]
    tails = [x[numerators:].astype(jnp.float32) for x in blocks]
    opened = unpack(jnp.concatenate(tails, axis=0).astype(jnp.bfloat16), rows)
    opened = [columns(x) for x in opened]
    results = []
    for r in range(rows):
        pieces = [slice(s * 8, s * 8 + 8) for s in range(sources)]
        tops = [opened[0][r][p] for p in pieces]
        totals = [opened[1][r][p] for p in pieces]
        sums = [x[r * 8 : r * 8 + 8].astype(jnp.float32) for x in blocks]
        for u in range(steps):
            tops.append(score_ref[u, r])
            totals.append(one)
            sums.append(value_ref[u, r])
        _, total, summed = combine(tops, totals, sums)
        results.append(summed / total)
    for r, result in enumerate(results):
        for h in range(width // HEAD):
            out_ref[r, :, h * HEAD : (h + 1) * HEAD] = result[h * steps : (h + 1) * steps].astype(
                jnp.bfloat16
            )


def merge(parts, scores, values, shape):
    return pl.pallas_call(
        merge_kernel,
        out_shape=jax.ShapeDtypeStruct(shape, jnp.bfloat16),
        compiler_params=PARAMS,
        name="merge",
    )(parts, scores, values)


CHIPS = ("y", "z", "x")


def exchange(x, axes):
    return lax.all_to_all(x, axes, split_axis=0, concat_axis=0, tiled=True)


def per_device(
    queries,
    new_kv,
    prefix_keys,
    prefix_values,
    suffix_keys,
    suffix_values,
    suffix_lengths,
    row_slot,
):
    layers = lax.axis_size("y")
    cores = lax.axis_size("core")
    members = lax.axis_size("z") * lax.axis_size("x")
    chips = layers * members
    swap = [(i, (i + 1) % cores) for i in range(cores)]

    own = (prefix_keys, prefix_values, suffix_keys, suffix_values)
    far = tuple(lax.ppermute(x, "core", swap) for x in own)
    own = tuple(pltpu.with_memory_space_constraint(x, pltpu.HBM) for x in own)
    far_lengths = lax.ppermute(suffix_lengths, "core", swap)

    blocks, row_slot = lax.optimization_barrier((spread(queries, chips), row_slot))
    near = exchange(blocks, CHIPS)
    info = locate(row_slot, (suffix_lengths, far_lengths), suffix_keys.shape[1])
    near, info = lax.optimization_barrier((near, info))
    near = near.reshape((layers, members) + near.shape[1:])
    parts = attend(info, near, (own, far), 2, 128)
    parts, queries, new_kv = lax.optimization_barrier((parts, queries, new_kv))
    received = exchange(parts.reshape((chips,) + parts.shape[2:]), CHIPS)
    scores, values = new_tokens(queries, new_kv)
    return merge(received, scores, values, queries.shape)


def solution(mesh):
    fine = jax.sharding.Mesh(mesh.devices.reshape(4, 2, 4, 4), ("y", "core", "z", "x"))
    grp, seq = ("y", "core"), ("z", "x")
    placed = (
        P(grp, None, seq),
        P(grp, None, None, None),
        P(grp + seq, None),
        P(grp + seq, None),
        P(grp, seq, None),
        P(grp, seq, None),
        P(grp),
        P(),
    )
    return jax.shard_map(
        per_device, mesh=fine, in_specs=placed, out_specs=P(grp, None, seq), check_vma=False
    )
```

```python
import functools
import math

import jax
import jax.numpy as jnp
from jax import lax
from jax.experimental import pallas as pl
from jax.experimental.pallas import tpu as pltpu
from jax.sharding import PartitionSpec as P

H = 64
KVH = 8
HEAD = 128
LOWEST = -(2.0**100)
SCALE = HEAD ** (-0.5) * math.log2(math.e)
TAIL = 8
PARAMS = pltpu.CompilerParams(vmem_limit_bytes=32 << 20)

NT = (((1,), (1,)), ((), ()))
NN = (((1,), (0,)), ((), ()))


def dot(a, b, dims):
    return lax.dot_general(a, b, dims, preferred_element_type=jnp.float32)


def iota(shape, axis):
    return lax.broadcasted_iota(jnp.int32, shape, axis)


def as_bf16(x):
    return x.astype(jnp.bfloat16).astype(jnp.float32)


def columns(x):
    return [x[:, a * HEAD : (a + 1) * HEAD] for a in range(x.shape[1] // HEAD)]


def pack(tops, totals):
    lane = iota((TAIL, HEAD), 1)
    piece = lax.rem(lane, 32) // 8
    packed = None
    for a, (top, total) in enumerate(zip(tops, totals)):
        high = as_bf16(total)
        mixed = jnp.where(piece == 1, high, total - high)
        mixed = jnp.where(piece == 0, top, mixed)
        packed = mixed if a == 0 else jnp.where(lane // 32 == a, mixed, packed)
    return packed.astype(jnp.bfloat16)


def unpack(tails, tiles):
    shape = (HEAD, tiles * HEAD)
    start = iota(shape, 0) - 32 * (iota(shape, 1) // HEAD)
    first = (start == 0).astype(jnp.float32).astype(jnp.bfloat16)
    second = ((start == 8) | (start == 16)).astype(jnp.float32).astype(jnp.bfloat16)
    return dot(tails, first, NN), dot(tails, second, NN)


def combine(tops, totals, numerators):
    upper = functools.reduce(jnp.maximum, tops)
    factors = [jnp.exp2(top - upper) for top in tops]
    total = sum(x * f for x, f in zip(totals, factors))
    return upper, total, sum(x * f for x, f in zip(numerators, factors))


def query_rows(q_ref):
    heads = range(q_ref.shape[2] // HEAD)
    held = [q_ref[r].astype(jnp.float32) for r in range(q_ref.shape[0])]
    return jnp.concatenate([x[:, h * HEAD : (h + 1) * HEAD] for x in held for h in heads], axis=0)


def spread_kernel(q_ref, out_ref):
    block = query_rows(q_ref).astype(jnp.bfloat16)
    for d in range(out_ref.shape[0]):
        out_ref[d] = block


def spread(queries, copies):
    return pl.pallas_call(
        spread_kernel,
        out_shape=jax.ShapeDtypeStruct((copies, queries.size // HEAD, HEAD), jnp.bfloat16),
        compiler_params=PARAMS,
        name="spread",
    )(pltpu.with_memory_space_constraint(queries, pltpu.HBM))


def locate_kernel(slot_ref, *refs, span):
    lengths, info = refs[:-1], refs[-1]
    slots = lengths[0].shape[0]
    cores, layers = lax.axis_size("core"), lax.axis_size("y")
    core = lax.axis_index("core")
    start = (lax.axis_index("z") * lax.axis_size("x") + lax.axis_index("x")) * span
    total = slots * len(lengths)
    for side, length_ref in enumerate(lengths):
        owner = lax.rem(core + side, cores)
        first = (lax.axis_index("y") * cores + owner) * slots
        for j in range(slots):
            row = jnp.int32(0)
            for r in range(slot_ref.shape[0]):
                row = jnp.where(slot_ref[r] == first + j, jnp.int32(r), row)
            group = lax.div(row, slots)
            served = lax.rem(group, cores) == core
            at = side * slots + j
            info[at] = jnp.where(served, lax.div(group, cores), layers)
            info[total + at] = lax.rem(row, slots)
            info[2 * total + at] = jnp.clip(length_ref[j] - start, 0, span)


def locate(row_slot, lengths, span):
    smem = pl.BlockSpec(memory_space=pltpu.SMEM)
    total = sum(x.shape[0] for x in lengths)
    return pl.pallas_call(
        functools.partial(locate_kernel, span=span),
        in_specs=[smem] * (1 + len(lengths)),
        out_specs=smem,
        out_shape=jax.ShapeDtypeStruct((3 * total,), jnp.int32),
        compiler_params=PARAMS,
        name="locate",
    )(row_slot, *lengths)


def attend_kernel(info, near_ref, *refs, sides, heads, chunk):
    count = 4 * sides
    sources, out_ref, held = refs[:count], refs[count], refs[count + 1 : 2 * count + 1]
    block, q_ref, own_top, own_acc, sems, out_sems = refs[2 * count + 1 :]
    layers, _, rows, _ = near_ref.shape
    _, _, halves, tiles = q_ref.shape[:4]
    numerators = tiles * 8
    per_chunk = chunk // rows
    wide = heads * HEAD
    length = sources[0].shape[0]
    slots, span, _ = sources[2].shape
    ones = jnp.ones((length, HEAD), jnp.bfloat16)
    pairs = KVH // heads

    def copy(n, pair):
        start = pair * wide if isinstance(pair, int) else pl.multiple_of(pair * wide, wide)
        at = pl.ds(start, wide)
        part = sources[n].at[:, at] if n % 4 < 2 else sources[n].at[:, :, at]
        return pltpu.make_async_copy(part, held[n].at[pair], sems.at[n, pair])

    def send(pair):
        at = pl.ds(pair * heads * halves, heads * halves)
        return pltpu.make_async_copy(block.at[:, at], out_ref.at[:, at], out_sems.at[pair])

    for pair in range(pairs):
        for n in range(count):
            copy(n, pair).start()

    own_top[...] = jnp.full(own_top.shape, LOWEST, jnp.float32)
    own_acc[...] = jnp.zeros(own_acc.shape, jnp.float32)
    position = iota((halves * 8, span), 1)

    def cut(i):
        return slice(i * HEAD, (i + 1) * HEAD)

    @pl.loop(0, pairs)
    def _(pair):
        for n in range(count):
            copy(n, pair).wait()
        first = pair * heads

        def scored(i, c):
            at = slice(c * per_chunk, (c + 1) * per_chunk)
            q = near_ref[at, first + i].reshape(chunk, HEAD)
            keys = [held[4 * side][pair, :, cut(i)] for side in range(sides)]
            return dot(q, jnp.concatenate(keys, axis=0), NT)

        items = [(i, c) for i in range(heads) for c in range(layers // per_chunk)]
        scores = scored(*items[0])

        for i in range(heads):
            x = near_ref[:, first + i].astype(jnp.float32)
            q_ref[:, i] = x.reshape((layers,) + q_ref.shape[2:])
        found = []
        total = sides * slots
        for j in range(total):
            layer, row, live = info[j], info[total + j], info[2 * total + j]
            sk_ref, sv_ref = held[4 * (j // slots) + 2 : 4 * (j // slots) + 4]
            for i in range(heads):
                q = q_ref[jnp.minimum(layer, layers - 1), i, :, row]
                q = q.reshape(halves * 8, HEAD).astype(jnp.bfloat16)
                own = dot(q, sk_ref[pair, j % slots, :, cut(i)], NT) * SCALE
                own = jnp.where(position < live, own, LOWEST)
                peak = jnp.max(own, axis=1, keepdims=True)
                peak = jnp.broadcast_to(as_bf16(peak), (halves * 8, HEAD))
                shift = jnp.concatenate([peak] * (span // HEAD), axis=1)
                weights = jnp.exp2(own - shift).astype(jnp.bfloat16)
                values = sv_ref[pair, j % slots, :, cut(i)]
                values = jnp.concatenate([values, ones[:span]], axis=1)
                found.append((layer, i, row, peak, dot(weights, values, NN)))
        for layer, i, row, peak, summed in found:
            own_top[layer, i, :, row] = peak.reshape(halves, 8, HEAD)
            own_acc[layer, i, :, row] = summed.reshape(halves, 8, 2 * HEAD)

        for number, (i, c) in enumerate(items):
            later = scored(*items[number + 1]) if number + 1 < len(items) else None
            peak = jnp.max(scores, axis=1, keepdims=True)
            peak = jnp.broadcast_to(as_bf16(peak * SCALE), (chunk, HEAD))
            shift = jnp.concatenate([peak] * (sides * length // HEAD), axis=1)
            weights = jnp.exp2(scores * SCALE - shift).astype(jnp.bfloat16)
            values = [
                jnp.concatenate([held[4 * side + 1][pair, :, cut(i)], ones], axis=1)
                for side in range(sides)
            ]
            summed = dot(weights, jnp.concatenate(values, axis=0), NN)
            at = slice(c * per_chunk, (c + 1) * per_chunk)
            own = own_top[at, i].reshape(chunk, HEAD)
            carried = own_acc[at, i].reshape(chunk, 2 * HEAD)
            top = jnp.maximum(peak, own)
            keep, add = jnp.exp2(peak - top), jnp.exp2(own - top)
            sums = summed[:, HEAD:] * keep + carried[:, HEAD:] * add
            numerator = (summed[:, :HEAD] * keep + carried[:, :HEAD] * add).astype(jnp.bfloat16)
            results = []
            for b in range(chunk // numerators):
                low = b * numerators
                parts = [slice(low + 8 * a, low + 8 * a + 8) for a in range(tiles)]
                tail = pack([top[p] for p in parts], [sums[p] for p in parts])
                results.append((numerator[low : low + numerators], tail))
            for b, (found_block, tail) in enumerate(results):
                to = block.at[c * per_chunk + b // halves, (first + i) * halves + b % halves]
                to[:numerators] = found_block
                to[numerators:] = tail
            scores = later
        send(pair).start()

    for pair in range(pairs):
        send(pair).wait()


def attend(info, near, caches, heads, chunk):
    layers, members, numerators, _ = near.shape
    halves = members // KVH
    near = near.reshape(layers, KVH, halves * numerators, HEAD)
    arrays = [x for cache in caches for x in cache]
    out = jax.ShapeDtypeStruct((layers, members, numerators + TAIL, HEAD), jnp.bfloat16)
    tiled = (heads, halves, numerators // 8, 8)
    anywhere = pl.BlockSpec(memory_space=pl.ANY)
    pairs = KVH // heads
    return pl.pallas_call(
        functools.partial(attend_kernel, sides=len(caches), heads=heads, chunk=chunk),
        in_specs=[
            pl.BlockSpec(memory_space=pltpu.SMEM),
            pl.BlockSpec(memory_space=pltpu.VMEM),
        ]
        + [anywhere] * len(arrays),
        out_specs=anywhere,
        out_shape=out,
        scratch_shapes=[
            pltpu.VMEM((pairs,) + x.shape[:-1] + (heads * HEAD,), x.dtype) for x in arrays
        ]
        + [
            pltpu.VMEM(out.shape, out.dtype),
            pltpu.VMEM((layers,) + tiled + (HEAD,), jnp.float32),
            pltpu.VMEM((layers + 1,) + tiled + (HEAD,), jnp.float32),
            pltpu.VMEM((layers + 1,) + tiled + (2 * HEAD,), jnp.float32),
            pltpu.SemaphoreType.DMA((len(arrays), pairs)),
            pltpu.SemaphoreType.DMA((pairs,)),
        ],
        compiler_params=pltpu.CompilerParams(vmem_limit_bytes=48 << 20),
        name="attend",
    )(info, near, *arrays)


def new_kernel(q_ref, new_ref, score_ref, value_ref):
    rows, steps, width = q_ref.shape
    member = lax.axis_index("z") * lax.axis_size("x") + lax.axis_index("x")
    kv_head = member * (width // HEAD) // (H // KVH)
    at_head = pl.ds(pl.multiple_of(kv_head * HEAD, HEAD), HEAD)
    step = lax.rem(iota((8, HEAD), 0), steps)
    queries = query_rows(q_ref)
    for r in range(rows):
        for u in range(steps):
            key, value = (
                jnp.broadcast_to(new_ref[r, u, n : n + 1, at_head].astype(jnp.float32), (8, HEAD))
                for n in range(2)
            )
            score = jnp.sum(queries[r * 8 : r * 8 + 8] * key, axis=1, keepdims=True) * SCALE
            score_ref[u, r] = jnp.where(step >= u, jnp.broadcast_to(score, (8, HEAD)), LOWEST)
            value_ref[u, r] = value


def new_tokens(queries, new_kv):
    rows, steps, _ = queries.shape
    out = jax.ShapeDtypeStruct((steps, rows, 8, HEAD), jnp.float32)
    return pl.pallas_call(
        new_kernel,
        out_shape=[out, out],
        compiler_params=PARAMS,
        name="new_tokens",
    )(queries, new_kv)


def merge_kernel(parts_ref, score_ref, value_ref, out_ref):
    rows, steps, width = out_ref.shape
    sources, size, _ = parts_ref.shape
    numerators = size - TAIL
    one = jnp.ones((8, HEAD), jnp.float32)
    blocks = [parts_ref[s] for s in range(sources)]
    tails = [x[numerators:].astype(jnp.float32) for x in blocks]
    opened = unpack(jnp.concatenate(tails, axis=0).astype(jnp.bfloat16), rows)
    opened = [columns(x) for x in opened]
    results = []
    for r in range(rows):
        pieces = [slice(s * 8, s * 8 + 8) for s in range(sources)]
        tops = [opened[0][r][p] for p in pieces]
        totals = [opened[1][r][p] for p in pieces]
        sums = [x[r * 8 : r * 8 + 8].astype(jnp.float32) for x in blocks]
        for u in range(steps):
            tops.append(score_ref[u, r])
            totals.append(one)
            sums.append(value_ref[u, r])
        _, total, summed = combine(tops, totals, sums)
        results.append(summed / total)
    for r, result in enumerate(results):
        for h in range(width // HEAD):
            out_ref[r, :, h * HEAD : (h + 1) * HEAD] = result[h * steps : (h + 1) * steps].astype(
                jnp.bfloat16
            )


def merge(parts, scores, values, shape):
    return pl.pallas_call(
        merge_kernel,
        out_shape=jax.ShapeDtypeStruct(shape, jnp.bfloat16),
        compiler_params=PARAMS,
        name="merge",
    )(parts, scores, values)


CHIPS = ("y", "z", "x")


def exchange(x, axes):
    return lax.all_to_all(x, axes, split_axis=0, concat_axis=0, tiled=True)


def per_device(
    queries,
    new_kv,
    prefix_keys,
    prefix_values,
    suffix_keys,
    suffix_values,
    suffix_lengths,
    row_slot,
):
    layers = lax.axis_size("y")
    cores = lax.axis_size("core")
    members = lax.axis_size("z") * lax.axis_size("x")
    chips = layers * members
    swap = [(i, (i + 1) % cores) for i in range(cores)]

    own = (prefix_keys, prefix_values, suffix_keys, suffix_values)
    far = tuple(lax.ppermute(x, "core", swap) for x in own)
    own = tuple(pltpu.with_memory_space_constraint(x, pltpu.HBM) for x in own)
    far_lengths = lax.ppermute(suffix_lengths, "core", swap)

    blocks, row_slot = lax.optimization_barrier((spread(queries, chips), row_slot))
    near = exchange(blocks, CHIPS)
    info = locate(row_slot, (suffix_lengths, far_lengths), suffix_keys.shape[1])
    near, info = lax.optimization_barrier((near, info))
    near = near.reshape((layers, members) + near.shape[1:])
    parts = attend(info, near, (own, far), 2, 256)
    parts, queries, new_kv = lax.optimization_barrier((parts, queries, new_kv))
    received = exchange(parts.reshape((chips,) + parts.shape[2:]), CHIPS)
    scores, values = new_tokens(queries, new_kv)
    return merge(received, scores, values, queries.shape)


def solution(mesh):
    fine = jax.sharding.Mesh(mesh.devices.reshape(4, 2, 4, 4), ("y", "core", "z", "x"))
    grp, seq = ("y", "core"), ("z", "x")
    placed = (
        P(grp, None, seq),
        P(grp, None, None, None),
        P(grp + seq, None),
        P(grp + seq, None),
        P(grp, seq, None),
        P(grp, seq, None),
        P(grp),
        P(),
    )
    return jax.shard_map(
        per_device, mesh=fine, in_specs=placed, out_specs=P(grp, None, seq), check_vma=False
    )
```
